32 devices in a mesh: section: 2 (over core), expert: 8 (over z, y), tensor: 2 (over x).
Axes of the slice: x: 2, y: 2, z: 4, core: 2. Of those that a mesh axis runs over, the one named last changes fastest.
Arguments:
- ends_in: bfloat16 [2, 2, 512, 2048], P('section', None, 'expert'), may hold values from -6 to 6
- attn_gain: bfloat16 [2, 2048], P('section', 'expert'), may hold values from 0.5 to 1.5
- w_query: bfloat16 [2, 2048, 4096], P('section', 'expert', 'tensor'), may hold values from -0.125 to 0.125
- key_matrix: bfloat16 [2, 2048, 512], P('section', 'expert', 'tensor'), may hold values from -0.125 to 0.125
- value_matrix: bfloat16 [2, 2048, 512], P('section', 'expert', 'tensor'), may hold values from -0.125 to 0.125
- query_gain: bfloat16 [2, 128], P('section', 'expert'), may hold values from 0.5 to 1.5
- key_gain: bfloat16 [2, 128], P('section', 'expert'), may hold values from 0.5 to 1.5
- w_out: bfloat16 [2, 4096, 2048], P('section', 'tensor', 'expert'), may hold values from -0.375 to 0.375
- ffn_gain: bfloat16 [2, 2048], P('section', 'expert'), may hold values from 0.5 to 1.5
- router: bfloat16 [2, 2048, 16], P('section', 'expert'), may hold values from -0.0625 to 0.0625
- w_gate: bfloat16 [2, 16, 2048, 768], P('section', 'expert', None, 'tensor'), may hold values from -0.125 to 0.125
- w_up: bfloat16 [2, 16, 2048, 768], P('section', 'expert', None, 'tensor'), may hold values from -0.125 to 0.125
- w_down: bfloat16 [2, 16, 768, 2048], P('section', 'expert', 'tensor'), may hold values from -0.625 to 0.625
- routes: int32 [2, 2, 512, 8], P('section', None, 'expert'), may hold values from 0 to 15, all different within a row; in each aligned block of 64 rows (0 to 63, 64 to 127, ..., all dimensions but the last counted through in order) at most 64 rows name the same one
- lengths: int32 [2, 8, 3], P(None, 'expert'), may hold values from 1 to 48, 64 in all within a row
Outputs:
- ends_out: bfloat16 [2, 2, 512, 2048], P('section', None, 'expert')
- grad_attn_gain: float32 [2, 2048], P('section', 'expert')
- grad_w_query: float32 [2, 2048, 4096], P('section', 'expert', 'tensor')
- grad_w_key: float32 [2, 2048, 512], P('section', 'expert', 'tensor')
- grad_w_value: float32 [2, 2048, 512], P('section', 'expert', 'tensor')
- grad_query_gain: float32 [2, 128], P('section', 'expert')
- grad_key_gain: float32 [2, 128], P('section', 'expert')
- grad_w_out: float32 [2, 4096, 2048], P('section', 'tensor', 'expert')
- grad_ffn_gain: float32 [2, 2048], P('section', 'expert')
- grad_router: float32 [2, 2048, 16], P('section', 'expert')
- grad_w_gate: float32 [2, 16, 2048, 768], P('section', 'expert', None, 'tensor')
- grad_w_up: float32 [2, 16, 2048, 768], P('section', 'expert', None, 'tensor')
- grad_w_down: float32 [2, 16, 768, 2048], P('section', 'expert', 'tensor')
The draws below stay inside these ranges and needn't reach their ends.
Inputs may be any that keep to these rules, and one draw needn't show every extreme that they name: `routes`: in each layer and micro-batch, the 64 rows of one block name 8 different experts each, no expert more than 64 times in the block, and in some blocks an expert exactly 64 times. Each row holds 3 lengths that sum to 64.
All inputs are finite; a program needn't handle non-finite values.
Results may differ from the reference program's by a relative error of at most 0.025.
Values may be sent and summed in bfloat16 or wider, within the bound.
No kernel may reach another device: no remote copies, remote signals or barrier semaphores. Data moves between devices by JAX's collectives and lax.ppermute only.
A program may use at most 256 MiB of HBM per device.

```python
import math
import jax
import jax.numpy as jnp
import numpy as np
from jax import lax

D = 2048
QUERY_HEADS = 32
KEY_VALUE_HEADS = 4
HEAD_DIMENSION = 128
FF = 768
TOP = 8
TOK_MB = 64
MICRO = 2
SEQS = 3
LAYERS = 2
EXPERTS = 16
GROUPS = 8
TOKENS = 512
SEQ_MOST = 48
CAP = 64
QD = 4096
KD = 512


def block_scale(key, shape, split, smallest, top_value):
    factor_of = 1.0
    for dim, shards_of in split:
        steps = jax.random.uniform(jax.random.fold_in(jax.random.fold_in(key, 6), dim), (shards_of,), jnp.float32, smallest / len(split), top_value / len(split))
        factor_of = factor_of * jnp.repeat(jnp.exp(steps), shape[dim] // shards_of).reshape((-1,) + (1,) * (len(shape) - 1 - dim))
    return factor_of


def length_profile(count, total, reach, lean):
    weights = [(1 << 20) // math.isqrt(grade ** lean) + 1 for grade in range(2, count + 1)]
    rest, given = total - reach - (count - 1), [1] * (count - 1)
    while rest > 0:
        candidates = [i for i in range(count - 1) if given[i] < reach]
        whole, left = sum([weights[i] for i in candidates]), rest
        for i in candidates:
            extra = min(reach - given[i], max(1, left * weights[i] // whole), rest)
            given[i] = given[i] + extra
            rest = rest - extra
    return np.array([reach] + given)


def uneven_parts(rng, count, total, limit, slope):
    if count == 2:
        one = jax.random.randint(rng, (), max(1, total - limit), min(limit, total - 1) + 1)
        return jnp.stack([one, total - one])
    tallies = jnp.asarray(length_profile(count, total, limit, slope), jnp.int32)
    twos = (count - 1) // 2
    donor, receiver = tallies[1:1 + 2 * twos:2], tallies[2:2 + 2 * twos:2]
    slack = jnp.minimum(donor - 1, limit - receiver)
    moved = jax.random.randint(jax.random.fold_in(rng, 1), (twos,), 0, 1 << 20) % (slack + 1)
    tallies = tallies.at[1:1 + 2 * twos:2].set(donor - moved).at[2:2 + 2 * twos:2].set(receiver + moved)
    return tallies[jax.random.permutation(jax.random.fold_in(rng, 2), count)]


def shared_out(own_key, own, number, rows, amount, top, limit, lean):
    sequence = jax.random.permutation(own_key, amount)
    heavy_load, ordinary = load_shares(amount, rows * top, limit, lean, True), load_shares(amount, rows * top, limit, lean, False)
    places = jnp.arange(amount)

    def named(sizes, offset_by):
        used = int((sizes > 0).sum())
        fixed = max(1, used // 4)
        shifted = fixed + (places - fixed + offset_by * (used - fixed)) % max(1, amount - fixed)
        return jnp.zeros((amount,), jnp.int32).at[sequence[jnp.where(places < fixed, places, shifted)]].set(jnp.asarray(sizes, jnp.int32))

    sizes = jnp.where(number % 4 == 0, named(heavy_load, number // 4), named(ordinary, number - number // 4 - 1))
    mixed = jax.random.permutation(jax.random.fold_in(own, 3), amount)
    source_of, taker = mixed[0:amount // 2 * 2:2], mixed[1:amount // 2 * 2:2]
    room = jnp.minimum(sizes[source_of] - 1, limit - sizes[taker]) // 2
    room = jnp.where((source_of == sequence[0]) | (taker == sequence[0]) | (sizes[taker] == 0), 0, jnp.maximum(room, 0))
    shifted = jax.random.randint(jax.random.fold_in(own, 4), (amount // 2,), 0, 1 << 20) % (room + 1)
    sizes = sizes.at[source_of].add(-shifted).at[taker].add(shifted)
    members = jnp.searchsorted(jnp.cumsum(sizes), jnp.arange(rows * top), side="right").astype(jnp.int32)
    table = members.reshape(top, rows).T
    table = table[jax.random.permutation(jax.random.fold_in(own, 1), rows)]
    offset_by = jax.random.randint(jax.random.fold_in(own, 2), (rows, 1), 0, top)
    return jnp.take_along_axis(table, (jnp.arange(top)[None, :] + offset_by) % top, axis=1)


def load_shares(number_of, total, reach, skew, full):
    weights = [(1 << 20) // math.isqrt(rank ** skew) + 1 for rank in range(1, number_of + 1)]
    largest = reach if full else min(reach, max(-(-total // number_of), total * weights[0] // sum(weights)))
    least = 1 if total - largest >= number_of - 1 else 0
    given, rest = [largest] + [least] * (number_of - 1), total - largest - least * (number_of - 1)
    while rest > 0:
        movable = [i for i in range(1, number_of) if given[i] < largest] or [i for i in range(1, number_of) if given[i] < reach]
        whole, budget = sum([weights[i] for i in movable]), rest
        for i in movable:
            addition = min(reach - given[i], max(1, budget * weights[i] // whole), rest)
            given[i] = given[i] + addition
            rest = rest - addition
    return np.array(given)


def noise(stream_key, dims, scale, limit, cuts=(), kind=jnp.bfloat16):
    values = scale * jax.random.normal(stream_key, dims, jnp.float32)
    if cuts:
        values = values * block_scale(stream_key, dims, cuts, -0.22, 0.18)
    return jnp.clip(values, -limit, limit).astype(kind)


def setup_inputs(seed: int = 0) -> dict:
    seeds = jax.random.split(jax.random.key(seed), 16)
    ends_in = noise(seeds[0], (2, MICRO, TOKENS, D), 1.0, 6.0, ((0, 2), (2, 8)))
    attn_gain = jnp.clip(1.0 + 0.1 * jax.random.normal(seeds[1], (LAYERS, D), jnp.float32), 0.5, 1.5).astype(jnp.bfloat16)
    w_query = noise(seeds[2], (LAYERS, D, QD), D ** -0.5, 0.125, ((0, 2), (1, 8), (2, 2)))
    key_matrix = noise(seeds[3], (LAYERS, D, KD), D ** -0.5, 0.125, ((0, 2), (1, 8), (2, 2)))
    value_matrix = noise(seeds[4], (LAYERS, D, KD), D ** -0.5, 0.125, ((0, 2), (1, 8), (2, 2)))
    query_gain = jnp.clip(1.0 + 0.1 * jax.random.normal(seeds[5], (LAYERS, HEAD_DIMENSION), jnp.float32), 0.5, 1.5).astype(jnp.bfloat16)
    key_gain = jnp.clip(1.0 + 0.1 * jax.random.normal(seeds[6], (LAYERS, HEAD_DIMENSION), jnp.float32), 0.5, 1.5).astype(jnp.bfloat16)
    w_out = noise(seeds[7], (LAYERS, QD, D), (QD // 16) ** -0.5, 0.375, ((0, 2), (1, 2), (2, 8)))
    ffn_gain = jnp.clip(1.0 + 0.1 * jax.random.normal(seeds[8], (LAYERS, D), jnp.float32), 0.5, 1.5).astype(jnp.bfloat16)
    router = noise(seeds[9], (LAYERS, D, EXPERTS), (4 * D) ** -0.5, 0.0625, ((0, 2), (1, 8)))
    w_gate = noise(seeds[10], (LAYERS, EXPERTS, D, FF), D ** -0.5, 0.125, ((0, 2), (1, 8), (3, 2)))
    w_up = noise(seeds[11], (LAYERS, EXPERTS, D, FF), D ** -0.5, 0.125, ((0, 2), (1, 8), (3, 2)))
    w_down = noise(seeds[12], (LAYERS, EXPERTS, FF, D), (FF // 8) ** -0.5, 0.625, ((0, 2), (1, 8), (2, 2)))
    routes_keys = jax.random.split(jax.random.fold_in(seeds[13], 1), LAYERS * MICRO * TOKENS // TOK_MB)
    routes_turns = jax.random.permutation(jax.random.fold_in(seeds[13], 3), LAYERS * MICRO * TOKENS // TOK_MB)
    routes = jax.vmap(lambda own, number: shared_out(jax.random.fold_in(seeds[13], 2), own, number, TOK_MB, EXPERTS, TOP, CAP, 1))(routes_keys, routes_turns).reshape((LAYERS, MICRO, TOKENS, TOP))
    lengths = jax.vmap(lambda own: uneven_parts(own, SEQS, TOK_MB, SEQ_MOST, 2))(jax.random.split(seeds[14], MICRO * GROUPS)).reshape((MICRO, GROUPS, SEQS)).astype(jnp.int32)
    return {"ends_in": ends_in, "attn_gain": attn_gain, "w_query": w_query, "key_matrix": key_matrix, "value_matrix": value_matrix, "query_gain": query_gain, "key_gain": key_gain, "w_out": w_out, "ffn_gain": ffn_gain, "router": router, "w_gate": w_gate, "w_up": w_up, "w_down": w_down, "routes": routes, "lengths": lengths}


@jax.custom_vjp
def low(v):
    return lax.optimization_barrier(v.astype(jnp.bfloat16)).astype(jnp.float32)

@jax.custom_vjp
def low_back(v):
    return v

def low_keep(v):
    return (low(v), None)

def low_pass(kept, grad):
    return (grad,)

def back_keep(v):
    return (v, None)

def back_low(kept, grad):
    return (low(grad),)
low.defvjp(low_keep, low_pass)
low_back.defvjp(back_keep, back_low)
epsilon = 1e-06
rope_base = 1000000.0
masked_score = -1e+30
highest_precision = lax.Precision.HIGHEST

def round_pair_values(tensor_in):
    return low(low_back(tensor_in))

def rms_norm(tensor_in, gain_vec):
    return tensor_in * lax.rsqrt(lax.optimization_barrier(jnp.mean(tensor_in * tensor_in, axis=-1, keepdims=True)) + epsilon) * gain_vec

def rotary(tensor_in, cosine_table, sine_table):
    half_size = tensor_in.shape[-1] // 2
    first_half = tensor_in[..., :half_size]
    second_half = tensor_in[..., half_size:]
    return jnp.concatenate([first_half * cosine_table - second_half * sine_table, second_half * cosine_table + first_half * sine_table], axis=-1)

def prepare(raw_proj, gain_vec, cosine_table, sine_table, factor):
    return rotary(rms_norm(raw_proj, gain_vec), cosine_table, sine_table) * factor

def layout(lengths_row, count_of_rows):
    seq_ends = jnp.cumsum(lengths_row, dtype=jnp.int32)
    row_index = jnp.arange(count_of_rows, dtype=jnp.int32)
    segment_ids = lax.optimization_barrier(jnp.sum((row_index[:, None] >= seq_ends[None, :]).astype(jnp.int32), axis=1, dtype=jnp.int32))
    seq_starts = seq_ends - lengths_row
    membership = segment_ids[:, None] == jnp.arange(seq_ends.shape[0], dtype=jnp.int32)[None, :]
    row_start = lax.optimization_barrier(jnp.sum(jnp.where(membership, seq_starts[None, :], 0), axis=1, dtype=jnp.int32))
    return (segment_ids, row_index - row_start)

def tables(position, head_size):
    half_size = head_size // 2
    inverse = rope_base ** (-(jnp.arange(half_size, dtype=jnp.float32) * 2.0) / head_size)
    angles = position.astype(jnp.float32)[:, None] * inverse[None, :]
    return (jnp.cos(angles)[:, None, :], jnp.sin(angles)[:, None, :])

def slot_ranks(flat_routes, experts):
    one_hot = (flat_routes[:, None] == jnp.arange(experts, dtype=jnp.int32)[None, :]).astype(jnp.int32)
    before = jnp.cumsum(one_hot, axis=0, dtype=jnp.int32) - 1
    return lax.optimization_barrier(jnp.sum(before * one_hot, axis=1, dtype=jnp.int32))

def attend_heads(pieces):
    query_rows, key_rotated, value_rows, segment_ids = pieces
    count_of_rows = query_rows.shape[0]
    heads_kv = key_rotated.shape[1]
    grouped = query_rows.reshape(count_of_rows, heads_kv, query_rows.shape[1] // heads_kv, query_rows.shape[2])
    scores = low_back(jnp.einsum('rkgd,skd->kgrs', grouped, key_rotated, precision=highest_precision))
    row_index = jnp.arange(count_of_rows, dtype=jnp.int32)
    allowed = (segment_ids[:, None] == segment_ids[None, :]) & (row_index[None, :] <= row_index[:, None])
    scores = jnp.where(allowed, scores, masked_score)
    probabilities = low(jax.nn.softmax(scores, axis=-1))
    mixed_rows = jnp.einsum('kgrs,skd->rkgd', probabilities, value_rows, precision=highest_precision)
    return mixed_rows.reshape(count_of_rows, -1)

def layer(resid_in, params, routes_mb, lengths_mb):
    attn_gain, w_query, key_matrix, value_matrix, query_gain, key_gain, w_out, ffn_gain, router, w_gate, w_up, w_down = params
    token_rows = resid_in.shape[0]
    block_list = lengths_mb.shape[0]
    count_of_rows = token_rows // block_list
    normed_rows = low(rms_norm(resid_in, attn_gain))
    q_raw = low_back(jnp.dot(normed_rows, w_query, precision=highest_precision)).reshape(token_rows, QUERY_HEADS, HEAD_DIMENSION)
    key_unrotated = low_back(jnp.dot(normed_rows, key_matrix, precision=highest_precision)).reshape(token_rows, KEY_VALUE_HEADS, HEAD_DIMENSION)
    value_rows = round_pair_values(jnp.dot(normed_rows, value_matrix, precision=highest_precision)).reshape(token_rows, KEY_VALUE_HEADS, HEAD_DIMENSION)
    segment_ids, position = jax.vmap(layout, in_axes=(0, None))(lengths_mb, count_of_rows)
    cosine_table, sine_table = tables(position.reshape(token_rows), HEAD_DIMENSION)
    query_rows = low(prepare(q_raw, query_gain, cosine_table, sine_table, HEAD_DIMENSION ** (-0.5)))
    key_rotated = low(prepare(key_unrotated, key_gain, cosine_table, sine_table, 1.0))
    mixed_rows = lax.map(jax.checkpoint(attend_heads), (query_rows.reshape(block_list, count_of_rows, QUERY_HEADS, HEAD_DIMENSION), key_rotated.reshape(block_list, count_of_rows, KEY_VALUE_HEADS, HEAD_DIMENSION), value_rows.reshape(block_list, count_of_rows, KEY_VALUE_HEADS, HEAD_DIMENSION), segment_ids))
    mixed_rows = round_pair_values(mixed_rows.reshape(token_rows, QUERY_HEADS * HEAD_DIMENSION))
    resid_mid = resid_in + low_back(jnp.dot(mixed_rows, w_out, precision=highest_precision))
    normed_ffn = low(rms_norm(resid_mid, ffn_gain))
    logits = low_back(jnp.dot(normed_ffn, router, precision=highest_precision))
    chosen = jnp.take_along_axis(logits, routes_mb, axis=1)
    gates = jax.nn.softmax(chosen, axis=-1)
    route_blocks = routes_mb.reshape(block_list, count_of_rows * TOP)
    rank_in = jax.vmap(slot_ranks, in_axes=(0, None))(route_blocks, EXPERTS)
    block_ids = jnp.arange(block_list, dtype=jnp.int32)[:, None]
    slot_index = ((route_blocks * block_list + block_ids) * CAP + rank_in).reshape(token_rows * TOP)
    pairs = jnp.repeat(normed_ffn, TOP, axis=0)
    buffer = jnp.zeros((EXPERTS * block_list * CAP, D), jnp.float32).at[slot_index].set(pairs)
    rows_in = low_back(buffer.reshape(EXPERTS, block_list * CAP, D))
    gate_act = low_back(jnp.einsum('end,edf->enf', rows_in, w_gate, precision=highest_precision))
    up_act = low_back(jnp.einsum('end,edf->enf', rows_in, w_up, precision=highest_precision))
    hidden = low(jax.nn.silu(gate_act) * up_act)
    result = round_pair_values(jnp.einsum('enf,efd->end', hidden, w_down, precision=highest_precision))
    picked = result.reshape(EXPERTS * block_list * CAP, D)[slot_index].reshape(token_rows, TOP, D)
    ffn_total = lax.optimization_barrier(jnp.sum(gates[:, :, None] * picked, axis=1))
    return resid_mid + ffn_total

def reference(ends_in, attn_gain, w_query, key_matrix, value_matrix, query_gain, key_gain, w_out, ffn_gain, router, w_gate, w_up, w_down, routes, lengths):
    inputs = ends_in[0].astype(jnp.float32)
    cotangent = ends_in[1].astype(jnp.float32)
    params = tuple((param.astype(jnp.float32) for param in (attn_gain, w_query, key_matrix, value_matrix, query_gain, key_gain, w_out, ffn_gain, router, w_gate, w_up, w_down)))

    def forward(inputs, params):
        results = []
        for micro_idx in range(MICRO):
            first_out = layer(inputs[micro_idx], tuple((param[0] for param in params)), routes[0, micro_idx], lengths[micro_idx])
            middle = round_pair_values(first_out)
            results.append(layer(middle, tuple((param[1] for param in params)), routes[1, micro_idx], lengths[micro_idx]))
        return jnp.stack(results)
    result, pullback = jax.vjp(forward, inputs, params)
    grad_in, grad_params = pullback(cotangent)
    ends_out = jnp.stack([grad_in, result]).astype(jnp.bfloat16)
    return (ends_out, grad_params[0], grad_params[1], grad_params[2], grad_params[3], grad_params[4], grad_params[5], grad_params[6], grad_params[7], grad_params[8], grad_params[9], grad_params[10], grad_params[11])
```

```python
import jax
import jax.numpy as jnp
from jax import lax
from jax.sharding import PartitionSpec as P

epsilon = 1e-06
rope_base = 1000000.0
masked_score = -1e30
bf16 = jnp.bfloat16
f32 = jnp.float32


def dot(left, right):
    return jnp.dot(left, right, preferred_element_type=f32)


def dot_rows(left, right):
    return lax.dot_general(left, right, (((0,), (0,)), ((), ())), preferred_element_type=f32)


def dot_cols(left, right):
    return lax.dot_general(left, right, (((1,), (1,)), ((), ())), preferred_element_type=f32)


def cat(*pieces, axis=0):
    return jnp.concatenate(pieces, axis=axis)


def swap_core(value):
    return lax.ppermute(value, "section", [(0, 1), (1, 0)])


def swap_x(value):
    return lax.ppermute(value, "tensor", [(0, 1), (1, 0)])


def swap_e(value, bits):
    count = lax.axis_size("expert")
    return lax.ppermute(value, "expert", [(i, i ^ bits) for i in range(count)])


def small_grid():
    return lax.axis_size("expert") == 8


def gather_rows(shard):
    if not small_grid():
        return lax.all_gather(shard, ("expert", "tensor"), axis=0, tiled=True)
    own = cat(shard, swap_e(shard, 2), swap_e(shard, 4), swap_e(shard, 6))
    half = own.shape[0] // 2
    from_x = swap_x(own)
    from_y = swap_e(own, 1)
    far_top = swap_e(from_x[:half], 1)
    far_bottom = swap_x(from_y[half:])
    return cat(own, from_x, from_y, far_top, far_bottom)


def scatter_rows(partial):
    if not small_grid():
        return lax.psum_scatter(partial, ("expert", "tensor"), scatter_dimension=0, tiled=True)
    quarter = partial.shape[0] // 4
    half = quarter // 2
    own, to_x, to_y, far = [partial[i * quarter : (i + 1) * quarter] for i in range(4)]
    top = swap_e(far[:half].astype(bf16), 1)
    bottom = swap_x(far[half:].astype(bf16))
    to_x = cat(to_x[:half] + top, to_x[half:]).astype(bf16)
    to_y = cat(to_y[:half], to_y[half:] + bottom).astype(bf16)
    total = own + swap_x(to_x) + swap_e(to_y, 1)
    step = quarter // 4
    for position, bits in ((1, 2), (2, 4), (3, 6)):
        block = total[position * step : (position + 1) * step].astype(bf16)
        if position == 1:
            result = total[:step] + swap_e(block, bits)
        else:
            result = result + swap_e(block, bits)
    return result


def gather_expert(shard):
    return lax.all_gather(shard, "expert", axis=0, tiled=True)


def normalize(value):
    return value * lax.rsqrt(jnp.mean(value * value, axis=-1, keepdims=True) + epsilon)


def rms_norm(value, gain):
    return normalize(value) * gain


def rotary(value, cosine, sine):
    half = value.shape[-1] // 2
    first = value[..., :half]
    second = value[..., half:]
    return cat(first * cosine - second * sine, second * cosine + first * sine, axis=-1)


def prepare(raw, gain, cosine, sine, factor):
    return rotary(rms_norm(raw, gain), cosine, sine) * factor


def layout(lengths_row, row_index):
    ends = jnp.cumsum(lengths_row, dtype=jnp.int32)
    starts = ends - lengths_row
    segment = jnp.sum((row_index[:, None] >= ends[None, :]).astype(jnp.int32), axis=1)
    member = segment[:, None] == jnp.arange(ends.shape[0], dtype=jnp.int32)[None, :]
    return segment, row_index - jnp.sum(jnp.where(member, starts[None, :], 0), axis=1)


def positions(lengths_row, row_index, head):
    segment, position = layout(lengths_row, row_index)
    half = head // 2
    inverse = rope_base ** (-(jnp.arange(half, dtype=f32) * 2.0) / head)
    angles = position.astype(f32)[:, None] * inverse[None, :]
    allowed = (segment[:, None] == segment[None, :]) & (row_index[None, :] <= row_index[:, None])
    return jnp.cos(angles), jnp.sin(angles), allowed


def attend(normed, w_qkv, query_gain, key_gain, tables):
    cosine, sine, allowed = tables
    head = query_gain.shape[0]
    rows = normed.shape[0] // 2
    group = w_qkv.shape[1] // head - 2
    raw = dot(normed, w_qkv).reshape(2, rows, group + 2, head)
    q_raw, k_raw, values = raw[:, :, :group], raw[:, :, group], raw[:, :, group + 1].astype(bf16)
    queries = prepare(
        q_raw, query_gain, cosine[:, :, None], sine[:, :, None], head ** (-0.5)
    ).astype(bf16)
    keys = prepare(k_raw, key_gain, cosine, sine, 1.0).astype(bf16)
    scores = jnp.einsum("mrgd,msd->mgrs", queries, keys, preferred_element_type=f32)
    scores = jnp.where(allowed[:, None], scores, masked_score)
    weights = jnp.exp(scores - jnp.max(scores, axis=-1, keepdims=True))
    probs = weights / jnp.sum(weights, axis=-1, keepdims=True)
    mixed = jnp.einsum("mgrs,msd->mrgd", probs.astype(bf16), values, preferred_element_type=f32)
    mixed = mixed.astype(bf16).reshape(2 * rows, group * head)
    return mixed, (q_raw, k_raw, values, queries, keys, probs)


def attend_back(d_mixed, state, query_gain, key_gain, tables):
    cosine, sine, allowed = tables
    q_raw, k_raw, values, queries, keys, probs = state
    mb, rows, group, head = q_raw.shape
    d_mixed = d_mixed.astype(bf16).reshape(mb, rows, group, head)
    d_probs = jnp.einsum("mrgd,msd->mgrs", d_mixed, values, preferred_element_type=f32)
    d_scores = probs * (d_probs - jnp.sum(probs * d_probs, axis=-1, keepdims=True))
    d_scores = d_scores.astype(bf16)
    d_values = jnp.einsum(
        "mgrs,mrgd->msd", probs.astype(bf16), d_mixed, preferred_element_type=f32
    ).astype(bf16)
    d_queries = jnp.einsum("mgrs,msd->mrgd", d_scores, keys, preferred_element_type=f32)
    d_keys = jnp.einsum("mgrs,mrgd->msd", d_scores, queries, preferred_element_type=f32)
    _, pull = jax.vjp(
        lambda raw, gain: prepare(
            raw, gain, cosine[:, :, None], sine[:, :, None], head ** (-0.5)
        ),
        q_raw,
        query_gain,
    )
    d_q, g_query_gain = pull(d_queries)
    _, pull = jax.vjp(
        lambda raw, gain: prepare(raw, gain, cosine, sine, 1.0), k_raw, key_gain
    )
    d_k, g_key_gain = pull(d_keys)
    d_qkv = cat(
        d_q.astype(bf16).reshape(mb * rows, group * head),
        d_k.astype(bf16).reshape(mb * rows, head),
        d_values.reshape(mb * rows, head),
        axis=1,
    )
    return d_qkv, g_query_gain, g_key_gain


def both_rows(shard):
    block = cat(shard, swap_x(shard))
    return cat(block, swap_core(block))


def own_rows(partial):
    rows = partial.shape[0] // 2
    block = partial[:rows] + swap_core(partial[rows:].astype(bf16))
    half = rows // 2
    return block[:half] + swap_x(block[half:].astype(bf16))


def router_gates(normed, router, mask):
    logits = jnp.where(mask, dot(normed, router), masked_score)
    weights = jnp.exp(logits - jnp.max(logits, axis=-1, keepdims=True))
    return weights / jnp.sum(weights, axis=-1, keepdims=True)


def forward_layer(x, weights, mask, tables, local_experts):
    attn_gain, w_qkv, query_gain, key_gain, w_out, ffn_gain, router, w_gate, w_up, w_down = weights
    width = x.shape[1]
    experts = router.shape[1]
    normed = both_rows(rms_norm(x, attn_gain).astype(bf16))
    mixed, attn_state = attend(normed, w_qkv, query_gain, key_gain, tables)
    mid = x + own_rows(dot_cols(mixed, w_out))
    normed_ffn = rms_norm(mid, ffn_gain).astype(bf16)
    gates = router_gates(normed_ffn, router, mask)
    high = gates.astype(bf16)
    low = (gates - high.astype(f32)).astype(bf16)
    extra = jnp.zeros((x.shape[0], 128 - 2 * experts), bf16)
    gathered = gather_rows(cat(normed_ffn, high, low, extra, axis=1))
    rows_in = gathered[:, :width]
    all_gates = gathered[:, width : width + experts].astype(f32) + gathered[
        :, width + experts : width + 2 * experts
    ].astype(f32)
    local = jnp.stack(
        [jnp.sum(jnp.where(one[None, :], all_gates, 0.0), axis=1) for one in local_experts], axis=1
    )
    hidden_units = w_gate.shape[1] // len(local_experts)
    wide = jnp.repeat(local, hidden_units, axis=1)
    gate_act = dot(rows_in, w_gate)
    up_act = dot(rows_in, w_up)
    hidden = (jax.nn.silu(gate_act) * up_act).astype(bf16)
    scaled = (hidden.astype(f32) * wide).astype(bf16)
    out = mid + scatter_rows(dot(scaled, w_down))
    state = (x, normed, mixed, attn_state, mid, normed_ffn, gates, wide)
    state = state + (rows_in, gate_act, up_act, hidden, scaled)
    return out, state


def backward_layer(grad, state, weights, mask, tables, local_experts):
    attn_gain, w_qkv, query_gain, key_gain, w_out, ffn_gain, router, w_gate, w_up, w_down = weights
    x, normed, mixed, attn_state, mid, normed_ffn, gates, wide = state[:8]
    rows_in, gate_act, up_act, hidden, scaled = state[8:]
    width = x.shape[1]
    experts = router.shape[1]
    grad_rows = gather_rows(grad)
    plain = dot_cols(grad_rows, w_down)
    hidden_units = w_gate.shape[1] // len(local_experts)
    products = (hidden.astype(f32) * plain).reshape(plain.shape[0], -1, hidden_units)
    gate_grads = jnp.sum(products, axis=2)
    placed = sum(
        gate_grads[:, i : i + 1] * one.astype(f32)[None, :] for i, one in enumerate(local_experts)
    )
    d_hidden = plain * wide
    sigmoid = jax.nn.sigmoid(gate_act)
    d_up = (d_hidden * gate_act * sigmoid).astype(bf16)
    d_gate = (d_hidden * up_act * sigmoid * (1.0 + gate_act * (1.0 - sigmoid))).astype(bf16)
    d_rows = dot_cols(d_gate, w_gate) + dot_cols(d_up, w_up)
    extra = jnp.zeros((d_rows.shape[0], 128 - experts), f32)
    back = scatter_rows(cat(d_rows, placed, extra, axis=1))
    gate_grad = back[:, width : width + experts]
    d_logits = gates * (gate_grad - jnp.sum(gates * gate_grad, axis=-1, keepdims=True))
    d_logits = d_logits.astype(bf16)
    d_normed_ffn = back[:, :width] + dot_cols(d_logits, router)
    _, pull = jax.vjp(rms_norm, mid, ffn_gain)
    d_mid, g_ffn_gain = pull(d_normed_ffn)
    d_mid = d_mid + grad.astype(f32)
    d_attn = both_rows(d_mid.astype(bf16))
    d_mixed = dot(d_attn, w_out)
    d_qkv, g_query_gain, g_key_gain = attend_back(
        d_mixed, attn_state, query_gain, key_gain, tables
    )
    d_normed = own_rows(dot_cols(d_qkv, w_qkv))
    _, pull = jax.vjp(rms_norm, x, attn_gain)
    d_x, g_attn_gain = pull(d_normed)
    g_router = dot_rows(d_logits, normed_ffn)
    small = (g_router, g_attn_gain, g_ffn_gain, g_query_gain, g_key_gain)
    heavy = (grad_rows, d_gate, d_up, d_attn, d_qkv)
    return d_mid + d_x, small, heavy


def sum_small(own, other):
    value = own + swap_core(other)
    if not small_grid():
        value = lax.psum(value, "tensor")
        return lax.psum_scatter(value, "expert", scatter_dimension=0, tiled=True)[0]
    value = value + swap_x(value)
    index = lax.axis_index("expert")
    for bit in (4, 2, 1):
        pair = value.reshape(2, value.shape[0] // 2, *value.shape[1:])
        upper = (index & bit) != 0
        keep = jnp.where(upper, pair[1], pair[0])
        give = jnp.where(upper, pair[0], pair[1])
        value = keep + swap_e(give, bit)
    return value[0]


def body(
    ends_in,
    attn_gain,
    w_query,
    key_matrix,
    value_matrix,
    query_gain,
    key_gain,
    w_out,
    ffn_gain,
    router,
    w_gate,
    w_up,
    w_down,
    routes,
    lengths,
):
    core = lax.axis_index("section")
    first = core == 0
    side = lax.axis_index("tensor")
    index = lax.axis_index("expert")
    split = lax.axis_size("expert")
    rows, width = ends_in.shape[2:]
    half = rows // 2
    experts = router.shape[2]
    head = query_gain.shape[1] * split

    def pick(zero, one):
        return jnp.where(first, zero, one)

    def mine(pair):
        return pick(pair[0], pair[1])

    def theirs(pair):
        return pick(pair[1], pair[0])

    def by_layer(own):
        got = swap_core(own)
        return pick(own, got), pick(got, own)

    def half_rows(block):
        return pick_side(block[:half], block[half:])

    def pick_side(zero, one):
        return jnp.where(side == 0, zero, one)

    columns = w_query.shape[2] // 2
    part = w_query.shape[1]
    transposed = w_out[0].T
    groups = [
        (
            cat(
                w_query[0][:, g * columns : (g + 1) * columns],
                key_matrix[0][:, g * head : (g + 1) * head],
                value_matrix[0][:, g * head : (g + 1) * head],
                axis=1,
            ),
            transposed[:, g * columns : (g + 1) * columns],
        )
        for g in range(2)
    ]
    kept = [mine(pair) for pair in zip(*groups)]
    got = [swap_core(theirs(pair)) for pair in zip(*groups)]
    slices = [[pick(k, g) for k, g in zip(kept, got)], [pick(g, k) for k, g in zip(kept, got)]]
    tiny = cat(
        attn_gain[0],
        ffn_gain[0],
        query_gain[0],
        key_gain[0],
        router[0].T.reshape(-1),
    )
    tiny_layers = jnp.stack(by_layer(tiny))
    tiny_all = lax.all_gather(tiny_layers[None], "expert", axis=0, tiled=True)
    full = [gather_expert(slices[0][0]), gather_expert(slices[0][1])]
    full = full + [gather_expert(slices[1][0]), gather_expert(slices[1][1])]
    gates_both = by_layer(w_gate[0].transpose(1, 0, 2).reshape(width, -1))
    ups_both = by_layer(w_up[0].transpose(1, 0, 2).reshape(width, -1))
    downs_both = by_layer(w_down[0].reshape(-1, width))
    layers = []
    for number in range(2):
        one = tiny_all[:, number]
        sizes = (part, part, head // split, head // split)
        vectors, start = [], 0
        for size in sizes:
            vectors.append(one[:, start : start + size].reshape(-1).astype(f32))
            start += size
        router_all = one[:, start:].reshape(split, experts, part).transpose(0, 2, 1)
        layers.append(
            (
                vectors[0],
                full[2 * number],
                vectors[2],
                vectors[3],
                full[2 * number + 1],
                vectors[1],
                router_all.reshape(width, experts),
                gates_both[number],
                ups_both[number],
                downs_both[number],
            )
        )

    crossed = swap_core(pick(ends_in[0, 1], ends_in[0, 0]))
    x_in = half_rows(pick(ends_in[0, 0], crossed)).astype(f32)
    grad_last = half_rows(pick(crossed, ends_in[0, 1]))
    routes_crossed = swap_core(pick(routes[0, 1], routes[0, 0]))
    routes_own = [pick(routes[0, 0], routes_crossed), pick(routes_crossed, routes[0, 1])]
    expert_ids = jnp.arange(experts, dtype=jnp.int32)
    masks = [
        jnp.any(half_rows(r)[:, :, None] == expert_ids[None, None, :], axis=1) for r in routes_own
    ]
    per_device = w_gate.shape[1]
    local_experts = [expert_ids == index * per_device + i for i in range(per_device)]
    row_index = (jnp.arange(rows, dtype=jnp.int32) + side * half) % rows
    length_pair = [pick(lengths[0, 0], lengths[1, 0]), pick(lengths[1, 0], lengths[0, 0])]
    tables = [positions(one, row_index, head) for one in length_pair]
    tables = tuple(jnp.stack(one) for one in zip(*tables))

    out0, state0 = forward_layer(x_in, layers[0], masks[0], tables, local_experts)
    x_mid = out0.astype(bf16).astype(f32)
    out1, state1 = forward_layer(x_mid, layers[1], masks[1], tables, local_experts)
    out1 = out1.astype(bf16)
    d_one, small1, heavy1 = backward_layer(
        grad_last, state1, layers[1], masks[1], tables, local_experts
    )
    d_one = d_one.astype(bf16)
    d_zero, small0, heavy0 = backward_layer(
        d_one, state0, layers[0], masks[0], tables, local_experts
    )
    d_zero = d_zero.astype(bf16)

    def both_batches(zero, one):
        own = pick(zero, one)
        return own, swap_core(pick(one, zero))

    rows_pair = both_batches(state0[8], state1[8])
    scaled_pair = both_batches(state0[12], state1[12])
    grad_pair = both_batches(heavy0[0], heavy1[0])
    gate_pair = both_batches(heavy0[1], heavy1[1])
    up_pair = both_batches(heavy0[2], heavy1[2])

    def both_dots(left, right):
        return dot_rows(left[0], right[0]) + dot_rows(left[1], right[1])

    units = w_gate.shape[3]
    g_gate = both_dots(rows_pair, gate_pair).reshape(width, per_device, units).transpose(1, 0, 2)
    g_up = both_dots(rows_pair, up_pair).reshape(width, per_device, units).transpose(1, 0, 2)
    g_down = both_dots(scaled_pair, grad_pair).reshape(per_device, units, width)

    def spread(value):
        return lax.all_to_all(value, "expert", split_axis=1, concat_axis=0, tiled=True)

    def swap_batches(value):
        return cat(value[rows:], value[:rows])

    normed_cols = spread(pick(state0[1], state1[1]))
    d_attn_cols = spread(pick(heavy0[3], heavy1[3]))
    mixed_own = pick(state0[2], state1[2])
    mixed_got = swap_batches(swap_core(pick(state1[2], state0[2])))
    mixed_all = gather_expert(
        cat(pick(mixed_own, mixed_got), pick(mixed_got, mixed_own), axis=1)
    )
    g_out = dot_rows(mixed_all, d_attn_cols)
    qkv_own = pick(heavy0[4], heavy1[4])
    qkv_got = swap_batches(swap_core(pick(heavy1[4], heavy0[4])))
    qkv_all = gather_expert(cat(pick(qkv_own, qkv_got), pick(qkv_got, qkv_own), axis=1))
    g_qkv = dot_rows(normed_cols, qkv_all)
    wide = g_qkv.shape[1] // 2
    g_query = cat(g_qkv[:, :columns], g_qkv[:, wide : wide + columns], axis=1)
    g_key = cat(
        g_qkv[:, columns : columns + head],
        g_qkv[:, wide + columns : wide + columns + head],
        axis=1,
    )
    g_value = cat(g_qkv[:, columns + head : wide], g_qkv[:, wide + columns + head :], axis=1)

    def by_owner(small):
        g_router, g_attn_gain, g_ffn_gain, g_query_gain, g_key_gain = small
        owned = [
            g_router.reshape(experts, split, part).transpose(1, 0, 2),
            g_attn_gain.reshape(split, 1, part),
            g_ffn_gain.reshape(split, 1, part),
        ]
        heads = cat(g_query_gain.reshape(split, 1, -1), g_key_gain.reshape(split, 1, -1), axis=2)
        owned.append(jnp.pad(heads, ((0, 0), (0, 0), (0, part - heads.shape[2]))))
        return cat(*owned, axis=1)

    small = (by_owner(small0), by_owner(small1))
    summed = sum_small(mine(small), theirs(small))
    g_router = summed[:experts].T
    g_attn_gain = summed[experts]
    g_ffn_gain = summed[experts + 1]
    g_query_gain = summed[experts + 2, : head // split]
    g_key_gain = summed[experts + 2, head // split : 2 * (head // split)]

    end_own = pick(d_zero, out1)
    end_got = swap_core(pick(out1, d_zero))
    ends = jnp.stack([pick(end_own, end_got), pick(end_got, end_own)])
    ends_far = swap_x(ends)
    ends_out = cat(pick_side(ends, ends_far), pick_side(ends_far, ends), axis=1)

    outs = (
        ends_out,
        g_attn_gain,
        g_query,
        g_key,
        g_value,
        g_query_gain,
        g_key_gain,
        g_out,
        g_ffn_gain,
        g_router,
        g_gate,
        g_up,
        g_down,
    )
    return tuple(one[None] for one in outs)


def solution(mesh):
    return jax.shard_map(
        body,
        mesh=mesh,
        in_specs=(
            P("section", None, "expert", None),
            P("section", "expert"),
            P("section", "expert", "tensor"),
            P("section", "expert", "tensor"),
            P("section", "expert", "tensor"),
            P("section", "expert"),
            P("section", "expert"),
            P("section", "tensor", "expert"),
            P("section", "expert"),
            P("section", "expert", None),
            P("section", "expert", None, "tensor"),
            P("section", "expert", None, "tensor"),
            P("section", "expert", "tensor", None),
            P("section", None, "expert", None),
            P(None, "expert", None),
        ),
        out_specs=(
            P("section", None, "expert", None),
            P("section", "expert"),
            P("section", "expert", "tensor"),
            P("section", "expert", "tensor"),
            P("section", "expert", "tensor"),
            P("section", "expert"),
            P("section", "expert"),
            P("section", "tensor", "expert"),
            P("section", "expert"),
            P("section", "expert", None),
            P("section", "expert", None, "tensor"),
            P("section", "expert", None, "tensor"),
            P("section", "expert", "tensor", None),
        ),
        check_vma=False,
    )
```

```python
import functools

import jax
import jax.numpy as jnp
import numpy as np
from jax import lax
from jax.experimental import pallas as pl
from jax.experimental.pallas import tpu as pltpu
from jax.sharding import PartitionSpec as P

epsilon = 1e-06
rope_base = 1000000.0
masked_score = -1e30
bf16 = jnp.bfloat16
f32 = jnp.float32
lanes = 128
tile_rows = 512


def dot(left, right):
    return jnp.dot(left, right, preferred_element_type=f32)


def dot_rows(left, right):
    return lax.dot_general(left, right, (((0,), (0,)), ((), ())), preferred_element_type=f32)


def dot_cols(left, right):
    return lax.dot_general(left, right, (((1,), (1,)), ((), ())), preferred_element_type=f32)


def cat(*pieces, axis=0):
    return jnp.concatenate(pieces, axis=axis)


def swap_core(value):
    return lax.ppermute(value, "section", [(0, 1), (1, 0)])


def swap_x(value):
    return lax.ppermute(value, "tensor", [(0, 1), (1, 0)])


def swap_e(value, bits):
    count = lax.axis_size("expert")
    return lax.ppermute(value, "expert", [(i, i ^ bits) for i in range(count)])


def small_grid():
    return lax.axis_size("expert") == 8


def after(value, *others):
    return lax.optimization_barrier((value, *others))[0] if others else value


anywhere = pl.BlockSpec(memory_space=pl.ANY)


def full(one):
    return pl.BlockSpec(one.shape, lambda *_: (0,) * len(one.shape))


def array(shape, kind):
    return jax.ShapeDtypeStruct(shape, kind)


def kernel_params(megabytes):
    return pltpu.CompilerParams(vmem_limit_bytes=megabytes * 2**20)


def cost(flops, moved):
    return pl.CostEstimate(flops=flops, bytes_accessed=moved, transcendentals=0)


def simple(kernel, shapes, *operands):
    return pl.pallas_call(
        kernel,
        in_specs=[full(one) for one in operands],
        out_specs=tuple(full(one) for one in shapes),
        out_shape=tuple(shapes),
        compiler_params=kernel_params(16),
        cost_estimate=cost(1000, 1000),
    )(*operands)


def stack_kernel(*refs):
    start = 0
    for ref in refs[:-1]:
        refs[-1][start : start + ref.shape[0]] = ref[...]
        start += ref.shape[0]


def stack(*pieces):
    rows = sum(one.shape[0] for one in pieces)
    return simple(stack_kernel, [array((rows, pieces[0].shape[1]), pieces[0].dtype)], *pieces)[0]


def near_kernel(to_x, top, to_y, bottom, out_x, out_y):
    half = top.shape[0]
    out_x[:half] = (to_x[:half].astype(f32) + top[...].astype(f32)).astype(bf16)
    out_x[half:] = to_x[half:]
    out_y[:half] = to_y[:half]
    out_y[half:] = (to_y[half:].astype(f32) + bottom[...].astype(f32)).astype(bf16)


def total_kernel(own, from_x, from_y, kept, *blocks):
    total = own[...].astype(f32) + from_x[...].astype(f32) + from_y[...].astype(f32)
    step = kept.shape[0]
    kept[...] = total[:step]
    for number, block in enumerate(blocks):
        block[...] = total[(number + 1) * step : (number + 2) * step].astype(bf16)


class Gather:
    def __init__(self, shard):
        self.shard = shard
        self.small = small_grid()

    def along_z(self, *gate):
        if self.small:
            shard = after(self.shard, *gate)
            self.line = (shard, swap_e(shard, 2), swap_e(shard, 4), swap_e(shard, 6))
            return self.line[1:]
        return ()

    def near(self, *gate):
        if self.small:
            own = after(stack(*self.line), *gate)
            self.near_pieces = (own, swap_x(own), swap_e(own, 1))
            return self.near_pieces[1:]
        return ()

    def far(self, *gate):
        if self.small:
            own, from_x, from_y = self.near_pieces
            half = own.shape[0] // 2
            self.far_pieces = (
                swap_e(after(from_x[:half], *gate), 1),
                swap_x(after(from_y[half:], *gate)),
            )
            return self.far_pieces
        shard = after(self.shard, *gate)
        self.whole = lax.all_gather(shard, ("expert", "tensor"), axis=0, tiled=True)
        return (self.whole,)

    def tiles(self, *gate):
        if self.small:
            top, bottom = self.far_pieces
            return [[*self.near_pieces, top, after(bottom, *gate)]]
        whole = after(self.whole, *gate)
        return [[whole]] * (whole.shape[0] // tile_rows)


class Scatter:
    def __init__(self, tiles):
        self.tiles = tiles
        self.small = small_grid()

    def far(self, *gate):
        if self.small:
            far_top, far_bottom = self.tiles[0][3:]
            self.top = swap_e(after(far_top, *gate), 1)
            self.bottom = swap_x(after(far_bottom, *gate))
            return (self.top, self.bottom)
        return ()

    def near(self, *gate, beside=()):
        if self.small:
            own, to_x, to_y = self.tiles[0][:3]
            shape = array(to_x.shape, bf16)
            to_x, to_y = simple(near_kernel, [shape] * 2, to_x, self.top, to_y, self.bottom)
            from_x, from_y = swap_x(after(to_x, *gate)), swap_e(after(to_y, *gate), 1)
            from_x = after(from_x, *beside)
            rows, columns = own.shape
            shapes = [array((rows // 4, columns), kind) for kind in (f32, bf16, bf16, bf16)]
            self.blocks = simple(total_kernel, shapes, own, from_x, from_y)
            return self.blocks[:1]
        return ()

    def along_z(self, *gate):
        if self.small:
            kept, *blocks = self.blocks
            moved = [swap_e(after(one, *gate), bits) for one, bits in zip(blocks, (2, 4, 6))]
            return [kept, *moved]
        whole = cat(*[one for pieces in self.tiles for one in pieces])
        whole = after(whole, *gate).astype(f32)
        return [lax.psum_scatter(whole, ("expert", "tensor"), scatter_dimension=0, tiled=True)]


cycle = (0, 2, 4, 6, 7, 5, 3, 1)


def owner_at(distance):
    index = lax.axis_index("expert")
    place = jnp.where(index % 2 == 0, index // 2, 7 - index // 2)
    spot = (place + distance) & 7
    return jnp.where(spot < 4, 2 * spot, 15 - 2 * spot)


class Ring:
    def __init__(self, shard):
        self.shard = shard
        self.rows = shard.shape[0]
        self.plus = self.minus = shard
        self.pieces = [shard]
        self.plan = [(0, 0)]
        self.latest = (shard,)
        self.small = small_grid()

    def advance(self, *gate):
        if not self.small:
            if len(self.latest) == 1 and self.latest[0] is self.shard:
                whole = lax.all_gather(after(self.shard, *gate), "expert", axis=0, tiled=True)
                self.pieces, self.plan, self.latest = [whole], [(None, 0)], (whole,)
            return self.latest
        number = len(self.pieces) // 2 + 1
        up = [(a, b) for a, b in zip(cycle, cycle[1:] + cycle[:1])]
        down = [(b, a) for a, b in up]
        plus, minus, middle = self.plus, self.minus, 0
        if number == 4:
            middle = self.rows // 32 * 16
            plus, minus = plus[:middle], minus[middle:]
        self.plus = lax.ppermute(after(plus, *gate), "expert", up)
        self.minus = lax.ppermute(after(minus, *gate), "expert", down)
        self.pieces += [self.plus, self.minus]
        self.plan += [(-number, 0), (number, middle)]
        self.latest = (self.plus, self.minus)
        return self.latest

    def collect(self, part):
        if not self.small:
            return part(self.pieces[0])
        columns = part(self.shard).shape[1]
        whole = jnp.zeros((8 * self.rows, columns), self.shard.dtype)
        for (distance, start), piece in zip(self.plan, self.pieces):
            place = (owner_at(distance) * self.rows + start, 0)
            whole = lax.dynamic_update_slice(whole, part(piece), place)
        return whole


def copy_pieces(pieces, plan, rows, columns, target, sems, first=0):
    copies = []
    for number, ((distance, start), piece) in enumerate(zip(plan, pieces)):
        place = start
        if distance is not None:
            place = pl.multiple_of(owner_at(distance) * rows + start, 16)
        copies.append(
            pltpu.make_async_copy(
                piece.at[:, columns],
                target.at[pl.ds(place, piece.shape[0]), columns],
                sems.at[first + number],
            )
        )
    return copies


def start_all(copies):
    for one in copies:
        one.start()


def wait_all(copies):
    for one in copies:
        one.wait()


def inverse_rms(value):
    return lax.rsqrt(jnp.mean(value * value, axis=-1, keepdims=True) + epsilon)


def rms_norm(value, gain):
    return value * inverse_rms(value) * gain


def layout(lengths_row, row_index):
    ends = jnp.cumsum(lengths_row, dtype=jnp.int32)
    starts = ends - lengths_row
    segment = jnp.sum((row_index[:, None] >= ends[None, :]).astype(jnp.int32), axis=1)
    member = segment[:, None] == jnp.arange(ends.shape[0], dtype=jnp.int32)[None, :]
    return segment, row_index - jnp.sum(jnp.where(member, starts[None, :], 0), axis=1)


def make_tables(length_pair, row_index, head):
    half = head // 2
    inverse = np.power(rope_base, -(np.arange(half) * 2.0) / head).astype(np.float32)
    segments, angles = [], []
    for number, one in enumerate(length_pair):
        segment, position = layout(one, row_index)
        segments.append(segment + number * (one.shape[0] + 1))
        angles.append(position.astype(f32)[:, None] * inverse[None, :])
    segment, angle = cat(*segments), cat(*angles)
    order = cat(row_index, row_index)
    allowed = (segment[:, None] == segment[None, :]) & (order[None, :] <= order[:, None])
    cosine, sine = jnp.cos(angle), jnp.sin(angle)
    return cat(cosine, cosine, axis=1), cat(-sine, sine, axis=1), allowed.astype(f32)


def rope(value, cosine, sine):
    return value * cosine + pltpu.roll(value, value.shape[1] // 2, 1) * sine


def rope_back(value, cosine, sine):
    return value * cosine + pltpu.roll(value * sine, value.shape[1] // 2, 1)


def from_heads(row, split, share):
    wide, head = row.shape[1], split * share
    part = wide // split
    lane = lax.broadcasted_iota(jnp.int32, (wide, head), 0)
    place = lax.broadcasted_iota(jnp.int32, (wide, head), 1)
    found = (lane // part == place // share) & (lane % part == place % share)
    chosen = jnp.where(found, 1.0, 0.0).astype(bf16)
    return dot(jnp.broadcast_to(row, (8, wide)).astype(bf16), chosen)[:1]


def attend_kernel(plan, rows, layer, split, experts, *refs):
    count = len(plan)
    pieces, refs = refs[:count], refs[count:]
    if layer == 0:
        (x_hat, cosine, sine, allowed), refs = refs[:4], refs[4:]
        tiny, normed, *refs = refs
    else:
        normed_pieces, (tiny, cosine, sine, allowed), refs = refs[:4], refs[4:8], refs[8:]
        normed, *refs = refs
    mixed, raw_out, probs_out, out_own, out_other, weights, sems = refs
    head = cosine.shape[1]
    group = probs_out.shape[0]
    near_columns = raw_out.shape[1]
    far_columns = mixed.shape[1]
    breadth = near_columns + far_columns
    near = copy_pieces(pieces, plan, rows, pl.ds(0, near_columns), weights, sems)
    far = copy_pieces(pieces, plan, rows, pl.ds(near_columns, far_columns), weights, sems, count)
    if layer == 0:
        last = pl.ds(breadth, weights.shape[1] - breadth)
        small = copy_pieces(pieces, plan, rows, last, weights, sems, 2 * count)
        start_all(small)
    start_all(near)
    start_all(far)
    share = head // split
    size = experts + 4
    if layer == 0:
        wait_all(small)
        tiny[...] = jnp.transpose(weights[:, breadth:].astype(f32))
        normed[...] = (x_hat[...] * tiny[experts : experts + 1]).astype(bf16)
    else:
        half = normed_pieces[0].shape[0]
        for number, piece in enumerate(normed_pieces):
            normed[number * half : (number + 1) * half] = piece[...]
    start = layer * size + experts
    query_gain = from_heads(tiny[start + 2 : start + 3], split, share)
    key_gain = from_heads(tiny[start + 3 : start + 4], split, share)
    wait_all(near)
    raw = dot(normed[...], weights[:, :near_columns])
    raw_out[...] = raw
    cos, sin, allow = cosine[...], sine[...], allowed[...] > 0.0
    k_raw = raw[:, group * head : (group + 1) * head]
    keys = rope(k_raw * inverse_rms(k_raw) * key_gain, cos, sin).astype(bf16)
    values = raw[:, (group + 1) * head :].astype(bf16)
    for number in range(group):
        q_raw = raw[:, number * head : (number + 1) * head]
        query = rope(q_raw * inverse_rms(q_raw) * query_gain, cos, sin) * head ** (-0.5)
        scores = jnp.where(allow, dot_cols(query.astype(bf16), keys), masked_score)
        unscaled = jnp.exp(scores - jnp.max(scores, axis=-1, keepdims=True))
        probs = unscaled / jnp.sum(unscaled, axis=-1, keepdims=True)
        probs_out[number] = probs
        mixed[:, number * head : (number + 1) * head] = dot(probs.astype(bf16), values).astype(
            bf16
        )
    wait_all(far)
    out = dot_cols(mixed[...], weights[:, near_columns:breadth])
    half = out_own.shape[0]
    out_own[...] = out[:half]
    out_other[...] = out[half:].astype(bf16)


def attend(layer, ring, breadth, split, experts, inputs, tables):
    head = tables[0].shape[1]
    rows = tables[0].shape[0]
    width = inputs[0].shape[1]
    group = (breadth // head - 2) // 2
    near = (group + 2) * head
    columns = breadth if layer else ring.shard.shape[1]
    small = (*inputs, *tables)
    shapes = (
        array((rows, width), bf16),
        array((rows, group * head), bf16),
        array((rows, near), f32),
        array((group, rows, rows), f32),
        array((rows // 2, width), f32),
        array((rows // 2, width), bf16),
    )
    if layer == 0:
        shapes = (array((columns - breadth, width), f32), *shapes)
    count = len(ring.pieces)
    return pl.pallas_call(
        functools.partial(attend_kernel, ring.plan, ring.rows, layer, split, experts),
        in_specs=[anywhere] * count + [full(one) for one in small],
        out_specs=tuple(full(one) for one in shapes),
        out_shape=shapes,
        scratch_shapes=[pltpu.VMEM((width, columns), bf16), pltpu.SemaphoreType.DMA((3 * count,))],
        compiler_params=kernel_params(26),
        cost_estimate=cost(12 * rows * width * breadth, 2 * width * breadth),
    )(*ring.pieces, *small)


def attend_back_kernel(plan, rows, layer, axis, experts, *refs):
    count = len(plan)
    pieces, refs = refs[:count], refs[count:]
    d_pieces, refs = refs[:4], refs[4:]
    raw_in, probs_in, tiny, cosine, sine = refs[:5]
    d_attn, d_qkv, d_own, d_other, g_query_gain, g_key_gain, weights, sems = refs[5:]
    head = cosine.shape[1]
    start = layer * (experts + 4) + experts
    query_gain = from_heads(tiny[start + 2 : start + 3], axis, head // axis)
    key_gain = from_heads(tiny[start + 3 : start + 4], axis, head // axis)
    half = d_pieces[0].shape[0]
    for number, piece in enumerate(d_pieces):
        d_attn[number * half : (number + 1) * half] = piece[...]
    group = probs_in.shape[0]
    split = raw_in.shape[1]
    rest = weights.shape[1] - split
    near = copy_pieces(pieces, plan, rows, pl.ds(split, rest), weights, sems)
    far = copy_pieces(pieces, plan, rows, pl.ds(0, split), weights, sems, count)
    start_all(near)
    start_all(far)
    cos, sin = cosine[...], sine[...]
    wait_all(near)
    d_mixed = dot(d_attn[...], weights[:, split:]).astype(bf16)
    k_raw = raw_in[:, group * head : (group + 1) * head]
    k_inverse = inverse_rms(k_raw)
    k_hat = k_raw * k_inverse
    keys = rope(k_hat * key_gain, cos, sin).astype(bf16)
    values = raw_in[:, (group + 1) * head :].astype(bf16)
    factor = head ** (-0.5)
    d_keys = jnp.zeros_like(k_raw)
    d_values = jnp.zeros_like(k_raw)
    gain_sum = jnp.zeros_like(query_gain)
    for number in range(group):
        span = slice(number * head, (number + 1) * head)
        q_raw = raw_in[:, span]
        q_inverse = inverse_rms(q_raw)
        q_hat = q_raw * q_inverse
        query = (rope(q_hat * query_gain, cos, sin) * factor).astype(bf16)
        probs = probs_in[number]
        d_one = d_mixed[:, span]
        d_probs = dot_cols(d_one, values)
        d_scores = probs * (d_probs - jnp.sum(probs * d_probs, axis=-1, keepdims=True))
        d_scores = d_scores.astype(bf16)
        d_values = d_values + dot_rows(probs.astype(bf16), d_one)
        d_keys = d_keys + dot_rows(d_scores, query)
        d_gained = rope_back(dot(d_scores, keys) * factor, cos, sin)
        gain_sum = gain_sum + jnp.sum(d_gained * q_hat, axis=0, keepdims=True)
        d_hat = d_gained * query_gain
        d_q = q_inverse * (d_hat - q_hat * jnp.mean(d_hat * q_hat, axis=-1, keepdims=True))
        d_qkv[:, span] = d_q.astype(bf16)
    g_query_gain[...] = gain_sum
    d_gained = rope_back(d_keys, cos, sin)
    g_key_gain[...] = jnp.sum(d_gained * k_hat, axis=0, keepdims=True)
    d_hat = d_gained * key_gain
    d_k = k_inverse * (d_hat - k_hat * jnp.mean(d_hat * k_hat, axis=-1, keepdims=True))
    d_qkv[:, group * head : (group + 1) * head] = d_k.astype(bf16)
    d_qkv[:, (group + 1) * head :] = d_values.astype(bf16)
    wait_all(far)
    d_normed = dot_cols(d_qkv[...], weights[:, :split])
    half = d_own.shape[0]
    d_own[...] = d_normed[:half]
    d_other[...] = d_normed[half:].astype(bf16)


def attend_back(layer, ring, breadth, split, experts, pieces, raw, probs, tiny, tables):
    head = tables[0].shape[1]
    width = pieces[0].shape[1]
    rows = raw.shape[0]
    small = (*pieces, raw, probs, tiny, tables[0], tables[1])
    shapes = (
        array((rows, width), bf16),
        array(raw.shape, bf16),
        array((rows // 2, width), f32),
        array((rows // 2, width), bf16),
        array((1, head), f32),
        array((1, head), f32),
    )
    count = len(ring.pieces)
    return pl.pallas_call(
        functools.partial(attend_back_kernel, ring.plan, ring.rows, layer, split, experts),
        in_specs=[anywhere] * count + [full(one) for one in small],
        out_specs=tuple(full(one) for one in shapes),
        out_shape=shapes,
        scratch_shapes=[pltpu.VMEM((width, breadth), bf16), pltpu.SemaphoreType.DMA((2 * count,))],
        compiler_params=kernel_params(26),
        cost_estimate=cost(12 * rows * width * breadth, 2 * width * breadth),
    )(*ring.pieces, *small)


def start_expert_weights(layer, refs, w_both, w_down, sems):
    is_own = lax.axis_index("section") == layer
    units = w_down.shape[0] // refs[0].shape[0]
    waits = []
    for number in range(refs[0].shape[0]):
        gate = pl.ds(2 * number * units, units)
        up = pl.ds((2 * number + 1) * units, units)
        targets = [w_both.at[:, gate], w_both.at[:, up], w_down.at[pl.ds(number * units, units)]]
        makers = [
            lambda ref, target=target, sem=sems.at[3 * number + i]: pltpu.make_async_copy(
                ref.at[number], target, sem
            )
            for i, target in enumerate(targets)
        ]

        @pl.when(is_own)
        def _():
            start_all([make(ref) for make, ref in zip(makers, refs[:3])])

        @pl.when(jnp.logical_not(is_own))
        def _():
            start_all([make(ref) for make, ref in zip(makers, refs[3:])])

        waits.append([make(ref) for make, ref in zip(makers, refs[:3])])
    return waits


def load_pieces(pieces, tile, scratch, sems):
    if len(pieces) == 1:
        pieces = [pieces[0].at[pl.ds(tile * tile_rows, tile_rows)]]
    copies, start = [], 0
    for number, piece in enumerate(pieces):
        rows = piece.shape[0]
        target = scratch.at[pl.ds(start, rows)]
        copies.append(pltpu.make_async_copy(piece, target, sems.at[number]))
        start += rows
    start_all(copies)
    return copies


def store_pieces(value, outs, columns):
    start = 0
    for out in outs:
        rows = out.shape[0]
        out[:, columns] = value[start : start + rows]
        start += rows


def experts_kernel(count, layer, tile, before, *refs):
    pieces, refs = refs[:count], refs[count:]
    weight_refs, ones, refs = refs[:6], refs[6], refs[7 + before :]
    outs, refs = refs[:count], refs[count:]
    act_out, gates_out, rows_store, scaled_store = refs[:4]
    rows_in, scaled, w_both, w_down, sems, weight_sems, store_sems = refs[4:]
    width = w_both.shape[0]
    experts = ones.shape[0]
    units = w_down.shape[0] // experts
    loads = load_pieces(pieces, tile, rows_in, sems)
    waits = start_expert_weights(layer, weight_refs, w_both, w_down, weight_sems)
    place = pl.ds(tile * tile_rows, tile_rows)
    stores = [
        pltpu.make_async_copy(
            rows_in.at[:, pl.ds(0, width)], rows_store.at[place], store_sems.at[0]
        ),
        pltpu.make_async_copy(scaled, scaled_store.at[place], store_sems.at[1]),
    ]
    wait_all(loads)
    stores[0].start()
    extra = rows_in[:, width:].astype(f32)
    gates = extra + pltpu.roll(extra, lanes // 2, 1)
    gates_out[...] = gates
    for number in range(experts):
        wait_all(waits[number])
        span = slice(2 * number * units, 2 * (number + 1) * units)
        act = dot(rows_in[:, :width], w_both[:, span])
        act_out[:, span] = act.astype(act_out.dtype)
        gate_act, up_act = act[:, :units], act[:, units:]
        hidden = (gate_act / (1.0 + jnp.exp(-gate_act)) * up_act).astype(bf16)
        gate = jnp.sum(gates * ones[number : number + 1], axis=1, keepdims=True)
        scaled[:, number * units : (number + 1) * units] = (hidden.astype(f32) * gate).astype(bf16)
    stores[1].start()
    step = width // 4
    for number in range(4):
        span = slice(number * step, (number + 1) * step)
        store_pieces(dot(scaled[...], w_down[:, span]).astype(bf16), outs, span)
    wait_all(stores)


def expert_scratch(wide, width, total_units, kind, count, experts):
    return [
        pltpu.VMEM((tile_rows, wide), bf16),
        kind,
        pltpu.VMEM((width, 2 * total_units), bf16),
        pltpu.VMEM((total_units, width), bf16),
        pltpu.SemaphoreType.DMA((count,)),
        pltpu.SemaphoreType.DMA((3 * experts,)),
        pltpu.SemaphoreType.DMA((2,)),
    ]


def run_experts(pieces, weights, ones, layer, tile, rows, stores):
    count = len(pieces)
    experts, width, units = weights[0].shape
    total_units = experts * units
    stores = stores or ()
    sizes = [min(one.shape[0], tile_rows) for one in pieces]
    shapes = tuple([array((one, width), bf16) for one in sizes]) + (
        array((tile_rows, 2 * total_units), f32 if small_grid() else bf16),
        array((tile_rows, lanes), f32),
        array((rows, width), bf16),
        array((rows, total_units), bf16),
    )
    outs = pl.pallas_call(
        functools.partial(experts_kernel, count, layer, tile, len(stores)),
        in_specs=[anywhere] * (count + 6) + [full(ones)] + [anywhere] * len(stores),
        out_specs=tuple(full(one) for one in shapes[: count + 2]) + (anywhere,) * 2,
        out_shape=shapes,
        scratch_shapes=expert_scratch(
            pieces[0].shape[1],
            width,
            total_units,
            pltpu.VMEM((tile_rows, total_units), bf16),
            count,
            experts,
        ),
        input_output_aliases={count + 7: count + 2, count + 8: count + 3} if stores else {},
        compiler_params=kernel_params(32),
        cost_estimate=cost(12 * tile_rows * width * total_units, 6 * width * total_units),
    )(*pieces, *weights, ones, *stores)
    return list(outs[:count]), outs[count : count + 2], outs[count + 2 :]


def experts_back_kernel(count, layer, tile, before, *refs):
    pieces, refs = refs[:count], refs[count:]
    weight_refs, ones, act, gates_in = refs[:6], refs[6], refs[7], refs[8]
    refs = refs[9 + before :]
    outs, refs = refs[:count], refs[count:]
    d_store, grad_store = refs[:2]
    rows_in, d_act, w_both, w_down, sems, weight_sems, store_sems = refs[2:]
    width = w_both.shape[0]
    experts = ones.shape[0]
    units = w_down.shape[0] // experts
    loads = load_pieces(pieces, tile, rows_in, sems)
    waits = start_expert_weights(layer, weight_refs, w_both, w_down, weight_sems)
    place = pl.ds(tile * tile_rows, tile_rows)
    stores = [
        pltpu.make_async_copy(rows_in, grad_store.at[place], store_sems.at[0]),
        pltpu.make_async_copy(d_act, d_store.at[place], store_sems.at[1]),
    ]
    wait_all(loads)
    stores[0].start()
    gates = gates_in[...]
    placed = jnp.zeros_like(gates)
    for number in range(experts):
        wait_all(waits[number])
        base = 2 * number * units
        plain = dot_cols(rows_in[...], w_down[number * units : (number + 1) * units])
        one = ones[number : number + 1]
        gate = jnp.sum(gates * one, axis=1, keepdims=True)
        gate_act = act[:, base : base + units].astype(f32)
        up_act = act[:, base + units : base + 2 * units].astype(f32)
        sigmoid = 1.0 / (1.0 + jnp.exp(-gate_act))
        silu = gate_act * sigmoid
        hidden = (silu * up_act).astype(bf16).astype(f32)
        placed = placed + jnp.sum(plain * hidden, axis=1, keepdims=True) * one
        d_hidden = plain * gate
        d_act[:, base + units : base + 2 * units] = (d_hidden * silu).astype(bf16)
        d_gate = d_hidden * up_act * (sigmoid + silu * (1.0 - sigmoid))
        d_act[:, base : base + units] = d_gate.astype(bf16)
    stores[1].start()
    step = width // 4
    for number in range(4):
        span = slice(number * step, (number + 1) * step)
        store_pieces(dot_cols(d_act[...], w_both[span]).astype(bf16), outs, span)
    store_pieces(placed.astype(bf16), outs, slice(width, width + lanes))
    wait_all(stores)


def run_experts_back(pieces, weights, ones, kept, layer, tile, rows, stores):
    count = len(pieces)
    experts, width, units = weights[0].shape
    total_units = experts * units
    stores = stores or ()
    act, gates = kept
    sizes = [min(one.shape[0], tile_rows) for one in pieces]
    shapes = tuple([array((one, width + lanes), bf16) for one in sizes]) + (
        array((rows, 2 * total_units), bf16),
        array((rows, width), bf16),
    )
    outs = pl.pallas_call(
        functools.partial(experts_back_kernel, count, layer, tile, len(stores)),
        in_specs=[anywhere] * (count + 6)
        + [full(ones), full(act), full(gates)]
        + [anywhere] * len(stores),
        out_specs=tuple(full(one) for one in shapes[:count]) + (anywhere,) * 2,
        out_shape=shapes,
        scratch_shapes=expert_scratch(
            width,
            width,
            total_units,
            pltpu.VMEM((tile_rows, 2 * total_units), bf16),
            count,
            experts,
        ),
        input_output_aliases={count + 9: count, count + 10: count + 1} if stores else {},
        compiler_params=kernel_params(32),
        cost_estimate=cost(12 * tile_rows * width * total_units, 6 * width * total_units),
    )(*pieces, *weights, ones, act, gates, *stores)
    return list(outs[:count]), outs[count:]


def grads_kernel(column, before, count, *refs):
    sources, refs = refs[:8], refs[8 + before :]
    outs, (left, right, result, sems, out_sems) = refs[:count], refs[count:]
    core = lax.axis_index("section")
    rows = left.shape[0] // 2
    place, step = column
    spans = [pl.ds(0, left.shape[1]), pl.ds(0, right.shape[1])]
    spans[place] = pl.ds(step * 512, 512)

    def copies(layer):
        made = []
        for number, target in enumerate((left, right)):
            for got in range(2):
                source = sources[4 * number + 2 * got + layer]
                made.append(
                    pltpu.make_async_copy(
                        source.at[:, spans[number]],
                        target.at[pl.ds(got * rows, rows)],
                        sems.at[2 * number + got],
                    )
                )
        return made

    for layer in range(2):

        @pl.when(core == layer)
        def _():
            start_all(copies(layer))

    wait_all(copies(0))
    experts = outs[0].shape[0]
    units = result.shape[1 - place] // (experts * count)
    result[...] = dot_rows(left[...], right[...])
    stores = []
    for expert in range(experts):
        for number, out in enumerate(outs):
            start = (expert * len(outs) + number) * units
            if place == 0:
                source = result.at[:, pl.ds(start, units)]
                target = out.at[expert, spans[0]]
            else:
                source = result.at[pl.ds(start, units)]
                target = out.at[expert, :, spans[1]]
            stores.append(pltpu.make_async_copy(source, target, out_sems.at[len(stores)]))
    start_all(stores)
    wait_all(stores)


def run_grads(place, step, left, right, shapes, before):
    before = before or ()
    rows = left[0].shape[0]
    widths = [left[0].shape[1], right[0].shape[1]]
    widths[place] = 512
    experts = shapes[0].shape[0]
    return pl.pallas_call(
        functools.partial(grads_kernel, (place, step), len(before), len(shapes)),
        in_specs=[anywhere] * (8 + len(before)),
        out_specs=(anywhere,) * len(shapes),
        out_shape=shapes,
        scratch_shapes=[
            pltpu.VMEM((2 * rows, widths[0]), bf16),
            pltpu.VMEM((2 * rows, widths[1]), bf16),
            pltpu.VMEM((widths[0], widths[1]), f32),
            pltpu.SemaphoreType.DMA((4,)),
            pltpu.SemaphoreType.DMA((experts * len(shapes),)),
        ],
        input_output_aliases={8 + i: i for i in range(len(before))},
        compiler_params=kernel_params(40),
        cost_estimate=cost(4 * 10**9, 10**7),
    )(*left, *right, *before)


def wide_grads(experts, rows_in, d_act):
    width, units = rows_in[0].shape[1], d_act[0].shape[1] // (2 * experts)
    shapes = (array((experts, width, units), f32),) * 2
    made = []
    for step in range(width // 512):
        made.append(run_grads(0, step, rows_in, d_act, shapes, made[-1] if made else None))
    return made


def down_grads(experts, scaled, grads):
    width, units = grads[0].shape[1], scaled[0].shape[1] // experts
    shapes = (array((experts, units, width), f32),)
    made = []
    for step in range(width // 512):
        made.append(run_grads(1, step, scaled, grads, shapes, made[-1] if made else None))
    return made


def out_grads_kernel(plan, rows, *refs):
    count = len(plan)
    pieces, (d_cols, g_out, mixed, sems) = refs[:count], refs[count:]
    copies = copy_pieces(pieces, plan, rows, pl.ds(0, mixed.shape[1]), mixed, sems)
    start_all(copies)
    wait_all(copies)
    g_out[...] = dot_rows(mixed[...], d_cols[...])


def out_grads(ring, d_cols):
    rows, columns = d_cols.shape
    breadth = ring.shard.shape[1]
    count = len(ring.pieces)
    shape = array((breadth, columns), f32)
    return pl.pallas_call(
        functools.partial(out_grads_kernel, ring.plan, ring.rows),
        in_specs=[anywhere] * count + [full(d_cols)],
        out_specs=full(shape),
        out_shape=shape,
        scratch_shapes=[pltpu.VMEM((rows, breadth), bf16), pltpu.SemaphoreType.DMA((count,))],
        compiler_params=kernel_params(24),
        cost_estimate=cost(2 * rows * columns * breadth, 4 * columns * breadth),
    )(*ring.pieces, d_cols)


def stack_layer_kernel(zero, one, got, out):
    core = lax.axis_index("section")
    columns = zero.shape[1]
    half = zero.shape[0] // 2
    for number, own in ((0, zero), (1, one)):

        @pl.when(core == number)
        def _():
            here = slice(number * columns, (number + 1) * columns)
            there = slice((1 - number) * columns, (2 - number) * columns)
            out[:, here] = own[...]
            out[:half, there] = got[half:]
            out[half:, there] = got[:half]


def stack_layer(core, zero, one, got):
    rows, columns = zero.shape
    return simple(stack_layer_kernel, [array((rows, 2 * columns), zero.dtype)], zero, one, got)[0]


def projection_grads_kernel(plan, rows, *refs):
    count = len(plan)
    pieces, (normed, g_query, g_key, g_value, d_qkv, sems) = refs[:count], refs[count:]
    copies = copy_pieces(pieces, plan, rows, pl.ds(0, d_qkv.shape[1]), d_qkv, sems)
    start_all(copies)
    wait_all(copies)
    wide = g_query.shape[1] // 2
    head = g_key.shape[1] // 2
    both = dot_rows(normed[...], d_qkv[...])
    for side in range(2):
        start = side * (wide + 2 * head)
        g_query[:, side * wide : (side + 1) * wide] = both[:, start : start + wide]
        g_key[:, side * head : (side + 1) * head] = both[:, start + wide : start + wide + head]
        g_value[:, side * head : (side + 1) * head] = both[
            :, start + wide + head : start + wide + 2 * head
        ]


def projection_grads(ring, normed, head):
    rows, part = normed.shape
    breadth = ring.shard.shape[1]
    wide = breadth // 2 - 2 * head
    count = len(ring.pieces)
    shapes = (
        array((part, 2 * wide), f32),
        array((part, 2 * head), f32),
        array((part, 2 * head), f32),
    )
    return pl.pallas_call(
        functools.partial(projection_grads_kernel, ring.plan, ring.rows),
        in_specs=[anywhere] * count + [full(normed)],
        out_specs=tuple(full(one) for one in shapes),
        out_shape=shapes,
        scratch_shapes=[pltpu.VMEM((rows, breadth), bf16), pltpu.SemaphoreType.DMA((count,))],
        compiler_params=kernel_params(24),
        cost_estimate=cost(2 * rows * part * breadth, 4 * rows * breadth),
    )(*ring.pieces, normed)


def both_rows(shard):
    far = swap_x(shard)
    return (shard, far, swap_core(shard), swap_core(far))


def merge_kernel(own, got, kept, given):
    block = own[...] + got[...].astype(f32)
    half = kept.shape[0]
    kept[...] = block[:half]
    given[...] = block[half:].astype(bf16)


def own_rows(own, other):
    rows, width = own.shape
    shapes = [array((rows // 2, width), kind) for kind in (f32, bf16)]
    kept, given = simple(merge_kernel, shapes, own, swap_core(other))
    return kept, swap_x(given)


def route_kernel(layer, x, kept, got, tiny, mask, mid_out, payload, gates_out):
    experts = mask.shape[1]
    width = x.shape[1]
    start = layer * (experts + 4)
    mid = x[...] + kept[...] + got[...].astype(f32)
    mid_out[...] = mid
    gain = tiny[start + experts + 1 : start + experts + 2]
    normed = (mid * inverse_rms(mid) * gain).astype(bf16)
    payload[:, :width] = normed
    logits = dot_cols(normed, tiny[start : start + experts].astype(bf16))
    logits = jnp.where(mask[...] > 0.0, logits, masked_score)
    weights = jnp.exp(logits - jnp.max(logits, axis=-1, keepdims=True))
    gates = weights / jnp.sum(weights, axis=-1, keepdims=True)
    gates_out[...] = gates
    high = gates.astype(bf16)
    low = (gates - high.astype(f32)).astype(bf16)
    payload[:, width:] = jnp.zeros((x.shape[0], lanes), bf16)
    payload[:, width : width + experts] = high
    payload[:, width + lanes // 2 : width + lanes // 2 + experts] = low


def route(layer, x, kept, got, tiny, mask):
    rows, width = x.shape
    shapes = [
        array((rows, width), f32),
        array((rows, width + lanes), bf16),
        array(mask.shape, f32),
    ]
    kernel = functools.partial(route_kernel, layer)
    return simple(kernel, shapes, x, kept, got, tiny, mask)


def sum_parts(parts):
    total = parts[0][...]
    for one in parts[1:]:
        total = total + one[...].astype(f32)
    return total


def enter_kernel(count, experts, mid, *refs):
    parts, (tiny, x_out, normed) = refs[:count], refs[count:]
    x = (mid[...] + sum_parts(parts)).astype(bf16).astype(f32)
    x_out[...] = x
    row = 2 * experts + 4
    normed[...] = (x * inverse_rms(x) * tiny[row : row + 1]).astype(bf16)


def enter(mid, parts, tiny, experts):
    shapes = [array(mid.shape, f32), array(mid.shape, bf16)]
    kernel = functools.partial(enter_kernel, len(parts), experts)
    return simple(kernel, shapes, mid, *parts, tiny)


def finish_kernel(mid, *refs):
    refs[-1][...] = (mid[...] + sum_parts(refs[:-1])).astype(bf16)


def finish(mid, parts):
    return simple(finish_kernel, [array(mid.shape, bf16)], mid, *parts)[0]


def norm_back(value, gain, grad):
    inverse = inverse_rms(value)
    hat = value * inverse
    d_hat = grad * gain
    d_value = inverse * (d_hat - hat * jnp.mean(d_hat * hat, axis=-1, keepdims=True))
    return d_value, jnp.sum(grad * hat, axis=0, keepdims=True)


def unroute_kernel(count, layer, *refs):
    parts, refs = refs[:count], refs[count:]
    grad, mid, tiny, gates_in, payload, d_out, d_low, g_router, g_gain = refs
    width = mid.shape[1]
    experts = gates_in.shape[1]
    start = layer * (experts + 4)
    back = sum_parts(parts)
    gates = gates_in[...]
    gate_grad = back[:, width : width + experts]
    d_logits = gates * (gate_grad - jnp.sum(gates * gate_grad, axis=-1, keepdims=True))
    d_logits = d_logits.astype(bf16)
    d_normed = back[:, :width] + dot(d_logits, tiny[start : start + experts].astype(bf16))
    gain = tiny[start + experts + 1 : start + experts + 2]
    d_mid, gain_sum = norm_back(mid[...], gain, d_normed)
    d_mid = d_mid + grad[...].astype(f32)
    d_out[...] = d_mid
    d_low[...] = d_mid.astype(bf16)
    g_router[...] = dot_rows(d_logits, payload[:, :width])
    g_gain[...] = gain_sum


def unroute(layer, parts, grad, mid, tiny, gates, payload):
    width, experts = mid.shape[1], gates.shape[1]
    shapes = [
        array(mid.shape, f32),
        array(mid.shape, bf16),
        array((experts, width), f32),
        array((1, width), f32),
    ]
    kernel = functools.partial(unroute_kernel, len(parts), layer)
    return simple(kernel, shapes, *parts, grad, mid, tiny, gates, payload)


def leave_kernel(row, kept, got, x, d_mid, tiny, d_out, g_gain):
    d_normed = kept[...] + got[...].astype(f32)
    d_x, gain_sum = norm_back(x[...], tiny[row : row + 1], d_normed)
    d_out[...] = (d_mid[...] + d_x).astype(bf16)
    g_gain[...] = gain_sum


def leave(layer, experts, kept, got, x, d_mid, tiny):
    shapes = [array(x.shape, bf16), array((1, x.shape[1]), f32)]
    kernel = functools.partial(leave_kernel, layer * (experts + 4) + experts)
    return simple(kernel, shapes, kept, got, x, d_mid, tiny)


def count_rows(tiles):
    return max(tile_rows, tiles[0][0].shape[0])


def apply_experts(tiles, weights, ones, layer):
    kept, outs, stores = [], [], None
    for number, pieces in enumerate(tiles):
        out, saved, stores = run_experts(
            pieces, weights, ones, layer, number, count_rows(tiles), stores
        )
        outs.append(out)
        kept.append(saved)
    return outs, kept, stores


def apply_experts_back(tiles, weights, ones, kept, layer):
    backs, stores = [], None
    for number, (pieces, saved) in enumerate(zip(tiles, kept)):
        back, stores = run_experts_back(
            pieces, weights, ones, saved, layer, number, count_rows(tiles), stores
        )
        backs.append(back)
    return backs, stores


def sum_small(own, other):
    value = own + swap_core(other)
    if not small_grid():
        value = lax.psum(value, "tensor")
        return lax.psum_scatter(value, "expert", scatter_dimension=1, tiled=True)
    value = value + swap_x(value)
    index = lax.axis_index("expert")
    for bit in (4, 2, 1):
        middle = value.shape[1] // 2
        lower, upper = value[:, :middle], value[:, middle:]
        high = (index & bit) != 0
        value = jnp.where(high, upper, lower) + swap_e(jnp.where(high, lower, upper), bit)
    return value


def body(
    ends_in,
    attn_gain,
    w_query,
    key_matrix,
    value_matrix,
    query_gain,
    key_gain,
    w_out,
    ffn_gain,
    router,
    w_gate,
    w_up,
    w_down,
    routes,
    lengths,
):
    core = lax.axis_index("section")
    first = core == 0
    side = lax.axis_index("tensor")
    index = lax.axis_index("expert")
    split = lax.axis_size("expert")
    rows, width = ends_in.shape[2:]
    half = rows // 2
    experts = router.shape[2]
    head = query_gain.shape[1] * split

    def pick(zero, one):
        return jnp.where(first, zero, one)

    def mine(pair):
        return pick(pair[0], pair[1])

    def theirs(pair):
        return pick(pair[1], pair[0])

    def by_layer(own):
        got = swap_core(own)
        return pick(own, got), pick(got, own)

    def pick_side(zero, one):
        return jnp.where(side == 0, zero, one)

    def half_rows(block):
        return pick_side(block[:half], block[half:])

    def side_first(block):
        return pick_side(block, cat(block[half:], block[:half]))

    part = w_query.shape[1]
    columns = w_query.shape[2] // 2
    transposed = w_out[0].T
    groups = [
        cat(
            w_query[0][:, g * columns : (g + 1) * columns],
            key_matrix[0][:, g * head : (g + 1) * head],
            value_matrix[0][:, g * head : (g + 1) * head],
            transposed[:, g * columns : (g + 1) * columns],
            axis=1,
        )
        for g in range(2)
    ]
    kept, got = mine(groups), swap_core(theirs(groups))
    breadth = kept.shape[1]

    share = head // split
    gains = cat(query_gain[0][:, None], key_gain[0][:, None], axis=1)
    tiny = cat(
        router[0],
        attn_gain[0][:, None],
        ffn_gain[0][:, None],
        jnp.pad(gains, ((0, part - share), (0, 0))),
        axis=1,
    )
    size = tiny.shape[1]
    tiny = cat(*by_layer(tiny), axis=1)
    tiny = jnp.pad(tiny, ((0, 0), (0, -2 * size % lanes)))
    ring0 = Ring(cat(pick(kept, got), tiny, axis=1))
    ring1 = Ring(pick(got, kept))
    started = ring0.advance()

    ends_in, w_gate, w_up, w_down = lax.optimization_barrier(
        (ends_in, w_gate, w_up, w_down, *started)
    )[:4]
    own_weights = (w_gate[0], w_up[0], w_down[0])
    expert_weights = own_weights + tuple(swap_core(one) for one in own_weights)
    crossed = swap_core(ends_in[0])
    x_all, grad_all = pick(ends_in[0], crossed), pick(crossed, ends_in[0])
    x_own = mine(x_all)
    x_in = half_rows(x_own).astype(f32)
    grad_last = half_rows(mine(grad_all))
    x_both = cat(side_first(x_own), side_first(theirs(x_all))).astype(f32)
    x_hat = x_both * inverse_rms(x_both)

    routes, lengths = lax.optimization_barrier((routes, lengths, *ring0.advance()))[:2]
    routes_crossed = swap_core(pick(routes[0, 1], routes[0, 0]))
    routes_own = [pick(routes[0, 0], routes_crossed), pick(routes_crossed, routes[0, 1])]
    expert_ids = jnp.arange(experts, dtype=jnp.int32)
    masks = [
        jnp.any(half_rows(r)[:, :, None] == expert_ids[None, None, :], axis=1).astype(f32)
        for r in routes_own
    ]
    per_device = w_gate.shape[1]
    lane_ids = jnp.arange(lanes, dtype=jnp.int32)
    local_ids = index * per_device + jnp.arange(per_device, dtype=jnp.int32)
    ones = (lane_ids[None, :] == local_ids[:, None]).astype(f32)
    row_index = (jnp.arange(rows, dtype=jnp.int32) + side * half) % rows
    length_pair = [pick(lengths[0, 0], lengths[1, 0]), pick(lengths[1, 0], lengths[0, 0])]
    tables = make_tables(length_pair, row_index, head)

    ring0.advance()
    ring0.advance()
    ring1.advance(*ring0.latest)

    tiny, normed0, mixed0, raw0, probs0, own, other = attend(
        0, ring0, breadth, split, experts, (x_hat,), tables
    )
    other = after(other, *ring1.latest)
    mid0, payload0, gates0 = route(0, x_in, *own_rows(own, other), tiny, masks[0])
    gather = Gather(payload0)
    gather.along_z()
    gather.near()
    gather.far()
    tiles = gather.tiles()
    ring1.advance(tiles[-1][-1])
    outs0, kept0, stores0 = apply_experts(tiles, expert_weights, ones, 0)
    scatter = Scatter(outs0)
    scatter.far()
    scatter.near(beside=ring1.latest)
    parts = scatter.along_z()
    ring1.advance(*parts)
    ring1.advance()
    x_mid, shard = enter(mid0, parts, tiny, experts)

    normed_pieces = both_rows(shard)
    grad_gather = Gather(grad_last)
    along = grad_gather.along_z(normed_pieces[-1])
    normed1, mixed1, raw1, probs1, own, other = attend(
        1, ring1, breadth, split, experts, (*normed_pieces, tiny), tables
    )
    other = after(other, *along)
    beside = grad_gather.near(own)
    mid1, payload1, gates1 = route(1, x_mid, *own_rows(own, other), tiny, masks[1])
    gather = Gather(after(payload1, *beside))
    gather.along_z()
    gather.near()
    gather.far()
    tiles = gather.tiles()
    beside = grad_gather.far(tiles[-1][-1])
    mixed_got = swap_core(pick(mixed1, mixed0))
    ring_mixed = Ring(stack_layer(core, mixed0, mixed1, mixed_got))
    ring_mixed.advance(tiles[-1][-1])
    outs1, kept1, stores1 = apply_experts(tiles, expert_weights, ones, 1)

    outs1[-1][-1] = after(outs1[-1][-1], *ring_mixed.latest, *beside)
    tiles = grad_gather.tiles(outs1[-1][-1])
    ring_mixed.advance(tiles[-1][-1])
    backs, back_stores1 = apply_experts_back(tiles, expert_weights, ones, kept1, 1)
    scatter = Scatter(backs)
    scatter.far(*ring_mixed.latest)
    reached = scatter.near()
    out_scatter = Scatter(outs1)
    beside = out_scatter.far(*reached)
    parts = scatter.along_z()
    parts[-1] = after(parts[-1], *beside)
    d_mid, d_low, g_router1, g_ffn_gain1 = unroute(
        1, parts, grad_last, mid1, tiny, gates1, payload1
    )
    d_pieces = both_rows(d_low)
    ring_mixed.advance(d_pieces[-1])
    d_attn1, d_qkv1, d_own, d_other, g_query_gain1, g_key_gain1 = attend_back(
        1, ring1, breadth, split, experts, d_pieces, raw1, probs1, tiny, tables
    )
    d_other = after(d_other, *ring_mixed.latest)
    d_one, g_attn_gain1 = leave(1, experts, *own_rows(d_own, d_other), x_mid, d_mid, tiny)

    gather = Gather(d_one)
    gather.along_z()
    beside = out_scatter.near(d_one)
    gather.near(*beside)
    gather.far()
    tiles = gather.tiles()
    backs, back_stores0 = apply_experts_back(tiles, expert_weights, ones, kept0, 0)

    def with_got(zero, one):
        if small_grid():
            to_zero = lax.ppermute(zero, "section", [(1, 0)])
            return zero, one, to_zero, lax.ppermute(one, "section", [(0, 1)])
        got = swap_core(pick(one, zero))
        return zero, one, got, got

    rows_in = with_got(stores0[0], stores1[0])
    scaled = with_got(stores0[1], stores1[1])
    d_act = with_got(back_stores0[0], back_stores1[0])
    grads = with_got(back_stores0[1], back_stores1[1])
    wide = wide_grads(per_device, rows_in, d_act)
    scatter = Scatter(backs)
    scatter.far()
    scatter.near(beside=wide[1])
    parts = scatter.along_z()
    parts[-1] = after(parts[-1], *wide[3])
    d_mid, d_low, g_router0, g_ffn_gain0 = unroute(
        0, parts, d_one, mid0, tiny, gates0, payload0
    )
    d_pieces = both_rows(d_low)
    ring_mixed.advance(d_pieces[-1])
    d_attn0, d_qkv0, d_own, d_other, g_query_gain0, g_key_gain0 = attend_back(
        0, ring0, breadth, split, experts, d_pieces, raw0, probs0, tiny, tables
    )
    d_other = after(d_other, *ring_mixed.latest)

    qkv_got = swap_core(pick(d_qkv1, d_qkv0))
    ring_d = Ring(stack_layer(core, d_qkv0, d_qkv1, qkv_got))
    ring_d.advance()
    out1 = finish(mid1, out_scatter.along_z(qkv_got))
    d_zero, g_attn_gain0 = leave(0, experts, *own_rows(d_own, d_other), x_in, d_mid, tiny)
    down = down_grads(per_device, scaled, (after(grads[0], qkv_got), *grads[1:]))
    down_early, down_late = down[1], down[3]
    ring_d.advance(*down_early)

    def spread(value):
        return lax.all_to_all(value, "expert", split_axis=1, concat_axis=0, tiled=True)

    end_own = pick(d_zero, out1)
    end_got = swap_core(pick(out1, d_zero))
    normed_cols = spread(pick(normed0, normed1))
    g_out = out_grads(ring_mixed, spread(pick(d_attn0, d_attn1)))
    ring_d.advance(*down_late)
    ring_d.advance()
    g_query, g_key, g_value = projection_grads(ring_d, normed_cols, head)
    (g_gate, g_up), (g_down,) = wide[-1], down[-1]

    def stacked(g_router, g_attn_gain, g_ffn_gain, g_query_gain, g_key_gain):
        heads = cat(g_query_gain.reshape(split, share), g_key_gain.reshape(split, share), axis=1)
        heads = jnp.pad(heads, ((0, 0), (0, part - 2 * share))).reshape(1, width)
        return cat(g_router, g_attn_gain, g_ffn_gain, heads)

    small = (
        stacked(g_router0, g_attn_gain0, g_ffn_gain0, g_query_gain0, g_key_gain0),
        stacked(g_router1, g_attn_gain1, g_ffn_gain1, g_query_gain1, g_key_gain1),
    )
    summed = sum_small(mine(small), theirs(small))
    g_router = summed[:experts].T
    g_attn_gain = summed[experts]
    g_ffn_gain = summed[experts + 1]
    g_query_gain = summed[experts + 2, :share]
    g_key_gain = summed[experts + 2, share : 2 * share]

    ends = jnp.stack([pick(end_own, end_got), pick(end_got, end_own)])
    ends_far = swap_x(ends)
    ends_out = cat(pick_side(ends, ends_far), pick_side(ends_far, ends), axis=1)

    outs = (
        ends_out,
        g_attn_gain,
        g_query,
        g_key,
        g_value,
        g_query_gain,
        g_key_gain,
        g_out,
        g_ffn_gain,
        g_router,
        g_gate,
        g_up,
        g_down,
    )
    return tuple(one[None] for one in outs)


def solution(mesh):
    return jax.shard_map(
        body,
        mesh=mesh,
        in_specs=(
            P("section", None, "expert", None),
            P("section", "expert"),
            P("section", "expert", "tensor"),
            P("section", "expert", "tensor"),
            P("section", "expert", "tensor"),
            P("section", "expert"),
            P("section", "expert"),
            P("section", "tensor", "expert"),
            P("section", "expert"),
            P("section", "expert", None),
            P("section", "expert", None, "tensor"),
            P("section", "expert", None, "tensor"),
            P("section", "expert", "tensor", None),
            P("section", None, "expert", None),
            P(None, "expert", None),
        ),
        out_specs=(
            P("section", None, "expert", None),
            P("section", "expert"),
            P("section", "expert", "tensor"),
            P("section", "expert", "tensor"),
            P("section", "expert", "tensor"),
            P("section", "expert"),
            P("section", "expert"),
            P("section", "tensor", "expert"),
            P("section", "expert"),
            P("section", "expert", None),
            P("section", "expert", None, "tensor"),
            P("section", "expert", None, "tensor"),
            P("section", "expert", "tensor", None),
        ),
        check_vma=False,
    )
```

```python
import functools

import jax
import jax.numpy as jnp
import numpy as np
from jax import lax
from jax.experimental import pallas as pl
from jax.experimental.pallas import tpu as pltpu
from jax.sharding import PartitionSpec as P

epsilon = 1e-06
rope_base = 1000000.0
masked_score = -1e30
bf16 = jnp.bfloat16
f32 = jnp.float32
lanes = 128
tile_rows = 512


def dot(left, right):
    return jnp.dot(left, right, preferred_element_type=f32)


def dot_rows(left, right):
    return lax.dot_general(left, right, (((0,), (0,)), ((), ())), preferred_element_type=f32)


def dot_cols(left, right):
    return lax.dot_general(left, right, (((1,), (1,)), ((), ())), preferred_element_type=f32)


def cat(*pieces, axis=0):
    return jnp.concatenate(pieces, axis=axis)


def swap_core(value):
    return lax.ppermute(value, "section", [(0, 1), (1, 0)])


def swap_x(value):
    return lax.ppermute(value, "tensor", [(0, 1), (1, 0)])


def swap_e(value, bits):
    count = lax.axis_size("expert")
    return lax.ppermute(value, "expert", [(i, i ^ bits) for i in range(count)])


def small_grid():
    return lax.axis_size("expert") == 8


def after(value, *others):
    return lax.optimization_barrier((value, *others))[0] if others else value


anywhere = pl.BlockSpec(memory_space=pl.ANY)


def full(one):
    return pl.BlockSpec(one.shape, lambda *_: (0,) * len(one.shape))


def array(shape, kind):
    return jax.ShapeDtypeStruct(shape, kind)


def kernel_params(megabytes):
    return pltpu.CompilerParams(vmem_limit_bytes=megabytes * 2**20)


def cost(flops, moved):
    return pl.CostEstimate(flops=flops, bytes_accessed=moved, transcendentals=0)


def simple(kernel, shapes, *operands):
    return pl.pallas_call(
        kernel,
        in_specs=[full(one) for one in operands],
        out_specs=tuple(full(one) for one in shapes),
        out_shape=tuple(shapes),
        compiler_params=kernel_params(16),
        cost_estimate=cost(1000, 1000),
    )(*operands)


def stack_kernel(*refs):
    start = 0
    for ref in refs[:-1]:
        refs[-1][start : start + ref.shape[0]] = ref[...]
        start += ref.shape[0]


def stack(*pieces):
    rows = sum(one.shape[0] for one in pieces)
    return simple(stack_kernel, [array((rows, pieces[0].shape[1]), pieces[0].dtype)], *pieces)[0]


def near_kernel(to_x, top, to_y, bottom, out_x, out_y):
    half = top.shape[0]
    out_x[:half] = (to_x[:half].astype(f32) + top[...].astype(f32)).astype(bf16)
    out_x[half:] = to_x[half:]
    out_y[:half] = to_y[:half]
    out_y[half:] = (to_y[half:].astype(f32) + bottom[...].astype(f32)).astype(bf16)


def total_kernel(own, from_x, from_y, kept, *blocks):
    total = own[...].astype(f32) + from_x[...].astype(f32) + from_y[...].astype(f32)
    step = kept.shape[0]
    kept[...] = total[:step]
    for number, block in enumerate(blocks):
        block[...] = total[(number + 1) * step : (number + 2) * step].astype(bf16)


class Gather:
    def __init__(self, shard):
        self.shard = shard
        self.small = small_grid()

    def along_z(self, *gate):
        if self.small:
            shard = after(self.shard, *gate)
            self.line = (shard, swap_e(shard, 2), swap_e(shard, 4), swap_e(shard, 6))
            return self.line[1:]
        return ()

    def near(self, *gate):
        if self.small:
            own = after(stack(*self.line), *gate)
            self.near_pieces = (own, swap_x(own), swap_e(own, 1))
            return self.near_pieces[1:]
        return ()

    def far(self, *gate):
        if self.small:
            own, from_x, from_y = self.near_pieces
            half = own.shape[0] // 2
            self.far_pieces = (
                swap_e(after(from_x[:half], *gate), 1),
                swap_x(after(from_y[half:], *gate)),
            )
            return self.far_pieces
        shard = after(self.shard, *gate)
        self.whole = lax.all_gather(shard, ("expert", "tensor"), axis=0, tiled=True)
        return (self.whole,)

    def tiles(self, *gate):
        if self.small:
            top, bottom = self.far_pieces
            return [[*self.near_pieces, top, after(bottom, *gate)]]
        whole = after(self.whole, *gate)
        return [[whole]] * (whole.shape[0] // tile_rows)


class Scatter:
    def __init__(self, tiles):
        self.tiles = tiles
        self.small = small_grid()

    def far(self, *gate):
        if self.small:
            far_top, far_bottom = self.tiles[0][3:]
            self.top = swap_e(after(far_top, *gate), 1)
            self.bottom = swap_x(after(far_bottom, *gate))
            return (self.top, self.bottom)
        return ()

    def near(self, *gate, beside=()):
        if self.small:
            own, to_x, to_y = self.tiles[0][:3]
            shape = array(to_x.shape, bf16)
            to_x, to_y = simple(near_kernel, [shape] * 2, to_x, self.top, to_y, self.bottom)
            from_x, from_y = swap_x(after(to_x, *gate)), swap_e(after(to_y, *gate), 1)
            from_x = after(from_x, *beside)
            rows, columns = own.shape
            shapes = [array((rows // 4, columns), kind) for kind in (f32, bf16, bf16, bf16)]
            self.blocks = simple(total_kernel, shapes, own, from_x, from_y)
            return self.blocks[:1]
        return ()

    def along_z(self, *gate):
        if self.small:
            kept, *blocks = self.blocks
            moved = [swap_e(after(one, *gate), bits) for one, bits in zip(blocks, (2, 4, 6))]
            return [kept, *moved]
        whole = cat(*[one for pieces in self.tiles for one in pieces])
        whole = after(whole, *gate).astype(f32)
        return [lax.psum_scatter(whole, ("expert", "tensor"), scatter_dimension=0, tiled=True)]


cycle = (0, 2, 4, 6, 7, 5, 3, 1)


def owner_at(distance):
    index = lax.axis_index("expert")
    place = jnp.where(index % 2 == 0, index // 2, 7 - index // 2)
    spot = (place + distance) & 7
    return jnp.where(spot < 4, 2 * spot, 15 - 2 * spot)


class Ring:
    def __init__(self, shard):
        self.shard = shard
        self.rows = shard.shape[0]
        self.plus = self.minus = shard
        self.pieces = [shard]
        self.plan = [(0, 0)]
        self.latest = (shard,)
        self.small = small_grid()

    def advance(self, *gate):
        if not self.small:
            if len(self.latest) == 1 and self.latest[0] is self.shard:
                whole = lax.all_gather(after(self.shard, *gate), "expert", axis=0, tiled=True)
                self.pieces, self.plan, self.latest = [whole], [(None, 0)], (whole,)
            return self.latest
        number = len(self.pieces) // 2 + 1
        up = [(a, b) for a, b in zip(cycle, cycle[1:] + cycle[:1])]
        down = [(b, a) for a, b in up]
        plus, minus, middle = self.plus, self.minus, 0
        if number == 4:
            middle = self.rows // 32 * 16
            plus, minus = plus[:middle], minus[middle:]
        self.plus = lax.ppermute(after(plus, *gate), "expert", up)
        self.minus = lax.ppermute(after(minus, *gate), "expert", down)
        self.pieces += [self.plus, self.minus]
        self.plan += [(-number, 0), (number, middle)]
        self.latest = (self.plus, self.minus)
        return self.latest

    def collect(self, part):
        if not self.small:
            return part(self.pieces[0])
        columns = part(self.shard).shape[1]
        whole = jnp.zeros((8 * self.rows, columns), self.shard.dtype)
        for (distance, start), piece in zip(self.plan, self.pieces):
            place = (owner_at(distance) * self.rows + start, 0)
            whole = lax.dynamic_update_slice(whole, part(piece), place)
        return whole


def copy_pieces(pieces, plan, rows, columns, target, sems, first=0):
    copies = []
    for number, ((distance, start), piece) in enumerate(zip(plan, pieces)):
        place = start
        if distance is not None:
            place = pl.multiple_of(owner_at(distance) * rows + start, 16)
        copies.append(
            pltpu.make_async_copy(
                piece.at[:, columns],
                target.at[pl.ds(place, piece.shape[0]), columns],
                sems.at[first + number],
            )
        )
    return copies


def start_all(copies):
    for one in copies:
        one.start()


def wait_all(copies):
    for one in copies:
        one.wait()


def inverse_rms(value):
    return lax.rsqrt(jnp.mean(value * value, axis=-1, keepdims=True) + epsilon)


def rms_norm(value, gain):
    return value * inverse_rms(value) * gain


def layout(lengths_row, row_index):
    ends = jnp.cumsum(lengths_row, dtype=jnp.int32)
    starts = ends - lengths_row
    segment = jnp.sum((row_index[:, None] >= ends[None, :]).astype(jnp.int32), axis=1)
    member = segment[:, None] == jnp.arange(ends.shape[0], dtype=jnp.int32)[None, :]
    return segment, row_index - jnp.sum(jnp.where(member, starts[None, :], 0), axis=1)


def make_tables(length_pair, row_index, head):
    half = head // 2
    inverse = np.power(rope_base, -(np.arange(half) * 2.0) / head).astype(np.float32)
    segments, angles = [], []
    for number, one in enumerate(length_pair):
        segment, position = layout(one, row_index)
        segments.append(segment + number * (one.shape[0] + 1))
        angles.append(position.astype(f32)[:, None] * inverse[None, :])
    segment, angle = cat(*segments), cat(*angles)
    order = cat(row_index, row_index)
    allowed = (segment[:, None] == segment[None, :]) & (order[None, :] <= order[:, None])
    cosine, sine = jnp.cos(angle), jnp.sin(angle)
    return cat(cosine, cosine, axis=1), cat(-sine, sine, axis=1), allowed.astype(f32)


def rope(value, cosine, sine):
    return value * cosine + pltpu.roll(value, value.shape[1] // 2, 1) * sine


def rope_back(value, cosine, sine):
    return value * cosine + pltpu.roll(value * sine, value.shape[1] // 2, 1)


def from_heads(row, split, share):
    wide, head = row.shape[1], split * share
    part = wide // split
    lane = lax.broadcasted_iota(jnp.int32, (wide, head), 0)
    place = lax.broadcasted_iota(jnp.int32, (wide, head), 1)
    found = (lane // part == place // share) & (lane % part == place % share)
    chosen = jnp.where(found, 1.0, 0.0).astype(bf16)
    return dot(jnp.broadcast_to(row, (8, wide)).astype(bf16), chosen)[:1]


def attend_kernel(plan, rows, layer, split, experts, *refs):
    count = len(plan)
    pieces, refs = refs[:count], refs[count:]
    if layer == 0:
        (x_hat, cosine, sine, allowed), refs = refs[:4], refs[4:]
        tiny, normed, *refs = refs
    else:
        normed_pieces, (tiny, cosine, sine, allowed), refs = refs[:4], refs[4:8], refs[8:]
        normed, *refs = refs
    mixed, raw_out, probs_out, out_own, out_other, weights, sems = refs
    head = cosine.shape[1]
    group = probs_out.shape[0]
    near_columns = raw_out.shape[1]
    far_columns = mixed.shape[1]
    breadth = near_columns + far_columns
    near = copy_pieces(pieces, plan, rows, pl.ds(0, near_columns), weights, sems)
    far = copy_pieces(pieces, plan, rows, pl.ds(near_columns, far_columns), weights, sems, count)
    if layer == 0:
        last = pl.ds(breadth, weights.shape[1] - breadth)
        small = copy_pieces(pieces, plan, rows, last, weights, sems, 2 * count)
        start_all(small)
    start_all(near)
    start_all(far)
    share = head // split
    size = experts + 4
    if layer == 0:
        wait_all(small)
        tiny[...] = jnp.transpose(weights[:, breadth:].astype(f32))
        normed[...] = (x_hat[...] * tiny[experts : experts + 1]).astype(bf16)
    else:
        half = normed_pieces[0].shape[0]
        for number, piece in enumerate(normed_pieces):
            normed[number * half : (number + 1) * half] = piece[...]
    start = layer * size + experts
    query_gain = from_heads(tiny[start + 2 : start + 3], split, share)
    key_gain = from_heads(tiny[start + 3 : start + 4], split, share)
    wait_all(near)
    raw = dot(normed[...], weights[:, :near_columns])
    raw_out[...] = raw
    cos, sin, allow = cosine[...], sine[...], allowed[...] > 0.0
    k_raw = raw[:, group * head : (group + 1) * head]
    keys = rope(k_raw * inverse_rms(k_raw) * key_gain, cos, sin).astype(bf16)
    values = raw[:, (group + 1) * head :].astype(bf16)
    for number in range(group):
        q_raw = raw[:, number * head : (number + 1) * head]
        query = rope(q_raw * inverse_rms(q_raw) * query_gain, cos, sin) * head ** (-0.5)
        scores = jnp.where(allow, dot_cols(query.astype(bf16), keys), masked_score)
        unscaled = jnp.exp(scores - jnp.max(scores, axis=-1, keepdims=True))
        probs = unscaled / jnp.sum(unscaled, axis=-1, keepdims=True)
        probs_out[number] = probs
        mixed[:, number * head : (number + 1) * head] = dot(probs.astype(bf16), values).astype(
            bf16
        )
    wait_all(far)
    out = dot_cols(mixed[...], weights[:, near_columns:breadth])
    half = out_own.shape[0]
    out_own[...] = out[:half]
    out_other[...] = out[half:].astype(bf16)


def attend(layer, ring, breadth, split, experts, inputs, tables):
    head = tables[0].shape[1]
    rows = tables[0].shape[0]
    width = inputs[0].shape[1]
    group = (breadth // head - 2) // 2
    near = (group + 2) * head
    columns = breadth if layer else ring.shard.shape[1]
    small = (*inputs, *tables)
    shapes = (
        array((rows, width), bf16),
        array((rows, group * head), bf16),
        array((rows, near), f32),
        array((group, rows, rows), f32),
        array((rows // 2, width), f32),
        array((rows // 2, width), bf16),
    )
    if layer == 0:
        shapes = (array((columns - breadth, width), f32), *shapes)
    count = len(ring.pieces)
    return pl.pallas_call(
        functools.partial(attend_kernel, ring.plan, ring.rows, layer, split, experts),
        in_specs=[anywhere] * count + [full(one) for one in small],
        out_specs=tuple(full(one) for one in shapes),
        out_shape=shapes,
        scratch_shapes=[pltpu.VMEM((width, columns), bf16), pltpu.SemaphoreType.DMA((3 * count,))],
        compiler_params=kernel_params(26),
        cost_estimate=cost(12 * rows * width * breadth, 2 * width * breadth),
    )(*ring.pieces, *small)


extra_rows = 16


def split_rows(out, start, value):
    size = value.shape[1]
    out[start:] = jnp.zeros((extra_rows, out.shape[1]), bf16)
    high = value.astype(bf16)
    out[start : start + 1, :size] = high
    out[start + 1 : start + 2, :size] = (value - high.astype(f32)).astype(bf16)


def joined_rows(rows, start, size):
    return rows[start : start + 1, :size].astype(f32) + rows[
        start + 1 : start + 2, :size
    ].astype(f32)


def attend_back_kernel(plan, block_rows, layer, axis, experts, *refs):
    count = len(plan)
    pieces, refs = refs[:count], refs[count:]
    d_pieces, refs = refs[:4], refs[4:]
    raw_in, probs_in, tiny, cosine, sine = refs[:5]
    d_attn, d_qkv, d_own, d_other, weights, sems = refs[5:]
    head = cosine.shape[1]
    rows = raw_in.shape[0]
    start = layer * (experts + 4) + experts
    query_gain = from_heads(tiny[start + 2 : start + 3], axis, head // axis)
    key_gain = from_heads(tiny[start + 3 : start + 4], axis, head // axis)
    half = d_pieces[0].shape[0]
    for number, piece in enumerate(d_pieces):
        d_attn[number * half : (number + 1) * half] = piece[...]
    group = probs_in.shape[0]
    split = raw_in.shape[1]
    rest = weights.shape[1] - split
    near = copy_pieces(pieces, plan, block_rows, pl.ds(split, rest), weights, sems)
    far = copy_pieces(pieces, plan, block_rows, pl.ds(0, split), weights, sems, count)
    start_all(near)
    cos, sin = cosine[...], sine[...]
    wait_all(near)
    start_all(far)
    d_mixed = dot(d_attn[...], weights[:, split:]).astype(bf16)
    k_raw = raw_in[:, group * head : (group + 1) * head]
    k_inverse = inverse_rms(k_raw)
    k_hat = k_raw * k_inverse
    keys = rope(k_hat * key_gain, cos, sin).astype(bf16)
    values = raw_in[:, (group + 1) * head :].astype(bf16)
    factor = head ** (-0.5)
    d_keys = jnp.zeros_like(k_raw)
    d_values = jnp.zeros_like(k_raw)
    gain_sum = jnp.zeros_like(query_gain)
    for number in range(group):
        span = slice(number * head, (number + 1) * head)
        q_raw = raw_in[:, span]
        q_inverse = inverse_rms(q_raw)
        q_hat = q_raw * q_inverse
        query = (rope(q_hat * query_gain, cos, sin) * factor).astype(bf16)
        probs = probs_in[number]
        d_one = d_mixed[:, span]
        d_probs = dot_cols(d_one, values)
        d_scores = probs * (d_probs - jnp.sum(probs * d_probs, axis=-1, keepdims=True))
        d_scores = d_scores.astype(bf16)
        d_values = d_values + dot_rows(probs.astype(bf16), d_one)
        d_keys = d_keys + dot_rows(d_scores, query)
        d_gained = rope_back(dot(d_scores, keys) * factor, cos, sin)
        gain_sum = gain_sum + jnp.sum(d_gained * q_hat, axis=0, keepdims=True)
        d_hat = d_gained * query_gain
        d_q = q_inverse * (d_hat - q_hat * jnp.mean(d_hat * q_hat, axis=-1, keepdims=True))
        d_qkv[:rows, span] = d_q.astype(bf16)
    d_gained = rope_back(d_keys, cos, sin)
    key_sum = jnp.sum(d_gained * k_hat, axis=0, keepdims=True)
    split_rows(d_qkv, rows, jnp.concatenate([gain_sum, key_sum], axis=1))
    d_hat = d_gained * key_gain
    d_k = k_inverse * (d_hat - k_hat * jnp.mean(d_hat * k_hat, axis=-1, keepdims=True))
    d_qkv[:rows, group * head : (group + 1) * head] = d_k.astype(bf16)
    d_qkv[:rows, (group + 1) * head :] = d_values.astype(bf16)
    wait_all(far)
    d_normed = dot_cols(d_qkv[:rows], weights[:, :split])
    half = d_own.shape[0]
    d_own[...] = d_normed[:half]
    d_other[...] = d_normed[half:].astype(bf16)


def attend_back(layer, ring, breadth, split, experts, pieces, raw, probs, tiny, tables):
    width = pieces[0].shape[1]
    rows = raw.shape[0]
    small = (*pieces, raw, probs, tiny, tables[0], tables[1])
    shapes = (
        array((rows, width), bf16),
        array((rows + extra_rows, raw.shape[1]), bf16),
        array((rows // 2, width), f32),
        array((rows // 2, width), bf16),
    )
    count = len(ring.pieces)
    return pl.pallas_call(
        functools.partial(attend_back_kernel, ring.plan, ring.rows, layer, split, experts),
        in_specs=[anywhere] * count + [full(one) for one in small],
        out_specs=tuple(full(one) for one in shapes),
        out_shape=shapes,
        scratch_shapes=[pltpu.VMEM((width, breadth), bf16), pltpu.SemaphoreType.DMA((2 * count,))],
        compiler_params=kernel_params(56),
        cost_estimate=cost(12 * rows * width * breadth, 2 * width * breadth),
    )(*ring.pieces, *small)


def expert_copies(layer, refs, w_both, w_down, sems):
    is_own = lax.axis_index("section") == layer
    experts = refs[0].shape[0]
    units = w_down.shape[0] // experts
    groups = []
    for number in range(experts):
        gate = pl.ds(2 * number * units, units)
        up = pl.ds((2 * number + 1) * units, units)
        targets = [w_both.at[:, gate], w_both.at[:, up], w_down.at[pl.ds(number * units, units)]]

        def make(source, i, number=number, targets=targets):
            return pltpu.make_async_copy(
                source.at[number], targets[i], sems.at[3 * number + i]
            )

        def start(which, make=make):
            @pl.when(is_own)
            def _():
                start_all([make(refs[i], i) for i in which])

            @pl.when(jnp.logical_not(is_own))
            def _():
                start_all([make(refs[3 + i], i) for i in which])

        def wait(which, make=make):
            wait_all([make(refs[i], i) for i in which])

        groups.append((start, wait))
    return groups


def load_pieces(pieces, tile, scratch, sems):
    if len(pieces) == 1:
        pieces = [pieces[0].at[pl.ds(tile * tile_rows, tile_rows)]]
    copies, start = [], 0
    for number, piece in enumerate(pieces):
        rows = piece.shape[0]
        target = scratch.at[pl.ds(start, rows)]
        copies.append(pltpu.make_async_copy(piece, target, sems.at[number]))
        start += rows
    start_all(copies)
    return copies


def store_pieces(value, outs, columns):
    start = 0
    for out in outs:
        rows = out.shape[0]
        out[:, columns] = value[start : start + rows]
        start += rows


def experts_kernel(count, layer, tile, before, *refs):
    pieces, refs = refs[:count], refs[count:]
    weight_refs, ones, refs = refs[:6], refs[6], refs[7 + before :]
    outs, refs = refs[:count], refs[count:]
    act_store, gates_out, rows_store, scaled_store = refs[:4]
    rows_in, scaled, w_both, w_down, sems, weight_sems, store_sems, act_out = refs[4:]
    width = w_both.shape[0]
    experts = ones.shape[0]
    units = w_down.shape[0] // experts
    loads = load_pieces(pieces, tile, rows_in, sems)
    weights = expert_copies(layer, weight_refs, w_both, w_down, weight_sems)
    weights[0][0]((0, 1))
    place = pl.ds(tile * tile_rows, tile_rows)
    stores = [
        pltpu.make_async_copy(
            rows_in.at[:, pl.ds(0, width)], rows_store.at[place], store_sems.at[0]
        ),
        pltpu.make_async_copy(scaled, scaled_store.at[place], store_sems.at[1]),
        pltpu.make_async_copy(act_out, act_store, store_sems.at[2]),
    ]
    wait_all(loads)
    stores[0].start()
    extra = rows_in[:, width:].astype(f32)
    gates = extra + pltpu.roll(extra, lanes // 2, 1)
    gates_out[...] = gates
    for number in range(experts):
        weights[number][1]((0, 1))
        if number + 1 < experts:
            weights[number + 1][0]((0, 1))
        weights[number][0]((2,))
        span = slice(2 * number * units, 2 * (number + 1) * units)
        act = dot(rows_in[:, :width], w_both[:, span])
        act_out[:, span] = act.astype(act_out.dtype)
        gate_act, up_act = act[:, :units], act[:, units:]
        hidden = (gate_act / (1.0 + jnp.exp(-gate_act)) * up_act).astype(bf16)
        gate = jnp.sum(gates * ones[number : number + 1], axis=1, keepdims=True)
        scaled[:, number * units : (number + 1) * units] = (hidden.astype(f32) * gate).astype(bf16)
    stores[1].start()
    stores[2].start()
    for number in range(experts):
        weights[number][1]((2,))
    step = width // 4
    for number in range(4):
        span = slice(number * step, (number + 1) * step)
        store_pieces(dot(scaled[...], w_down[:, span]).astype(bf16), outs, span)
    wait_all(stores)


def expert_scratch(wide, width, total_units, kind, count, experts):
    return [
        pltpu.VMEM((tile_rows, wide), bf16),
        kind,
        pltpu.VMEM((width, 2 * total_units), bf16),
        pltpu.VMEM((total_units, width), bf16),
        pltpu.SemaphoreType.DMA((count,)),
        pltpu.SemaphoreType.DMA((3 * experts,)),
        pltpu.SemaphoreType.DMA((3,)),
    ]


def run_experts(pieces, weights, ones, layer, tile, rows, stores):
    count = len(pieces)
    experts, width, units = weights[0].shape
    total_units = experts * units
    stores = stores or ()
    sizes = [min(one.shape[0], tile_rows) for one in pieces]
    shapes = tuple([array((one, width), bf16) for one in sizes]) + (
        array((tile_rows, 2 * total_units), f32 if small_grid() else bf16),
        array((tile_rows, lanes), f32),
        array((rows, width), bf16),
        array((rows, total_units), bf16),
    )
    outs = pl.pallas_call(
        functools.partial(experts_kernel, count, layer, tile, len(stores)),
        in_specs=[anywhere] * (count + 6) + [full(ones)] + [anywhere] * len(stores),
        out_specs=tuple(full(one) for one in shapes[:count])
        + (anywhere, full(shapes[count + 1]), anywhere, anywhere),
        out_shape=shapes,
        scratch_shapes=expert_scratch(
            pieces[0].shape[1],
            width,
            total_units,
            pltpu.VMEM((tile_rows, total_units), bf16),
            count,
            experts,
        )
        + [pltpu.VMEM(shapes[count].shape, shapes[count].dtype)],
        input_output_aliases={count + 7: count + 2, count + 8: count + 3} if stores else {},
        compiler_params=kernel_params(56),
        cost_estimate=cost(12 * tile_rows * width * total_units, 6 * width * total_units),
    )(*pieces, *weights, ones, *stores)
    return list(outs[:count]), outs[count : count + 2], outs[count + 2 :]


def experts_back_kernel(count, layer, tile, before, *refs):
    pieces, refs = refs[:count], refs[count:]
    weight_refs, ones, act_in, gates_in = refs[:6], refs[6], refs[7], refs[8]
    refs = refs[9 + before :]
    outs, refs = refs[:count], refs[count:]
    d_store, grad_store = refs[:2]
    rows_in, d_act, w_both, w_down, sems, weight_sems, store_sems, act = refs[2:]
    width = w_both.shape[0]
    experts = ones.shape[0]
    units = w_down.shape[0] // experts
    loads = load_pieces(pieces, tile, rows_in, sems)
    weights = expert_copies(layer, weight_refs, w_both, w_down, weight_sems)
    weights[0][0]((2,))
    act_copy = pltpu.make_async_copy(act_in, act, store_sems.at[2])
    act_copy.start()
    place = pl.ds(tile * tile_rows, tile_rows)
    stores = [
        pltpu.make_async_copy(rows_in, grad_store.at[place], store_sems.at[0]),
        pltpu.make_async_copy(d_act, d_store.at[place], store_sems.at[1]),
    ]
    wait_all(loads)
    stores[0].start()
    gates = gates_in[...]
    placed = jnp.zeros_like(gates)
    for number in range(experts):
        weights[number][1]((2,))
        if number + 1 < experts:
            weights[number + 1][0]((2,))
        weights[number][0]((0, 1))
        base = 2 * number * units
        plain = dot_cols(rows_in[...], w_down[number * units : (number + 1) * units])
        if number == 0:
            act_copy.wait()
        one = ones[number : number + 1]
        gate = jnp.sum(gates * one, axis=1, keepdims=True)
        gate_act = act[:, base : base + units].astype(f32)
        up_act = act[:, base + units : base + 2 * units].astype(f32)
        sigmoid = 1.0 / (1.0 + jnp.exp(-gate_act))
        silu = gate_act * sigmoid
        hidden = (silu * up_act).astype(bf16).astype(f32)
        placed = placed + jnp.sum(plain * hidden, axis=1, keepdims=True) * one
        d_hidden = plain * gate
        d_act[:, base + units : base + 2 * units] = (d_hidden * silu).astype(bf16)
        d_gate = d_hidden * up_act * (sigmoid + silu * (1.0 - sigmoid))
        d_act[:, base : base + units] = d_gate.astype(bf16)
    stores[1].start()
    for number in range(experts):
        weights[number][1]((0, 1))
    step = width // 4
    for number in range(4):
        span = slice(number * step, (number + 1) * step)
        store_pieces(dot_cols(d_act[...], w_both[span]).astype(bf16), outs, span)
    store_pieces(placed.astype(bf16), outs, slice(width, width + lanes))
    wait_all(stores)


def run_experts_back(pieces, weights, ones, kept, layer, tile, rows, stores):
    count = len(pieces)
    experts, width, units = weights[0].shape
    total_units = experts * units
    stores = stores or ()
    act, gates = kept
    sizes = [min(one.shape[0], tile_rows) for one in pieces]
    shapes = tuple([array((one, width + lanes), bf16) for one in sizes]) + (
        array((rows, 2 * total_units), bf16),
        array((rows, width), bf16),
    )
    outs = pl.pallas_call(
        functools.partial(experts_back_kernel, count, layer, tile, len(stores)),
        in_specs=[anywhere] * (count + 6)
        + [full(ones), anywhere, full(gates)]
        + [anywhere] * len(stores),
        out_specs=tuple(full(one) for one in shapes[:count]) + (anywhere,) * 2,
        out_shape=shapes,
        scratch_shapes=expert_scratch(
            width,
            width,
            total_units,
            pltpu.VMEM((tile_rows, 2 * total_units), bf16),
            count,
            experts,
        )
        + [pltpu.VMEM(act.shape, act.dtype)],
        input_output_aliases={count + 9: count, count + 10: count + 1} if stores else {},
        compiler_params=kernel_params(56),
        cost_estimate=cost(12 * tile_rows * width * total_units, 6 * width * total_units),
    )(*pieces, *weights, ones, act, gates, *stores)
    return list(outs[:count]), outs[count:]


def grads_kernel(column, before, count, *refs):
    sources, refs = refs[:8], refs[8 + before :]
    outs, (left, right, result, sems, out_sems) = refs[:count], refs[count:]
    core = lax.axis_index("section")
    rows = left.shape[0] // 2
    place, step = column
    spans = [pl.ds(0, left.shape[1]), pl.ds(0, right.shape[1])]
    spans[place] = pl.ds(step * 512, 512)

    def copies(layer):
        made = []
        for number, target in enumerate((left, right)):
            for got in range(2):
                source = sources[4 * number + 2 * got + layer]
                made.append(
                    pltpu.make_async_copy(
                        source.at[:, spans[number]],
                        target.at[pl.ds(got * rows, rows)],
                        sems.at[2 * number + got],
                    )
                )
        return made

    for layer in range(2):

        @pl.when(core == layer)
        def _():
            start_all(copies(layer))

    wait_all(copies(0))
    experts = outs[0].shape[0]
    units = result.shape[1 - place] // (experts * count)
    result[...] = dot_rows(left[...], right[...])
    stores = []
    for expert in range(experts):
        for number, out in enumerate(outs):
            start = (expert * len(outs) + number) * units
            if place == 0:
                source = result.at[:, pl.ds(start, units)]
                target = out.at[expert, spans[0]]
            else:
                source = result.at[pl.ds(start, units)]
                target = out.at[expert, :, spans[1]]
            stores.append(pltpu.make_async_copy(source, target, out_sems.at[len(stores)]))
    start_all(stores)
    wait_all(stores)


def run_grads(place, step, left, right, shapes, before):
    before = before or ()
    rows = left[0].shape[0]
    widths = [left[0].shape[1], right[0].shape[1]]
    widths[place] = 512
    experts = shapes[0].shape[0]
    return pl.pallas_call(
        functools.partial(grads_kernel, (place, step), len(before), len(shapes)),
        in_specs=[anywhere] * (8 + len(before)),
        out_specs=(anywhere,) * len(shapes),
        out_shape=shapes,
        scratch_shapes=[
            pltpu.VMEM((2 * rows, widths[0]), bf16),
            pltpu.VMEM((2 * rows, widths[1]), bf16),
            pltpu.VMEM((widths[0], widths[1]), f32),
            pltpu.SemaphoreType.DMA((4,)),
            pltpu.SemaphoreType.DMA((experts * len(shapes),)),
        ],
        input_output_aliases={8 + i: i for i in range(len(before))},
        compiler_params=kernel_params(56),
        cost_estimate=cost(10**8, 10**5),
    )(*left, *right, *before)


def wide_grads(experts, rows_in, d_act):
    width, units = rows_in[0].shape[1], d_act[0].shape[1] // (2 * experts)
    shapes = (array((experts, width, units), f32),) * 2
    made = []
    for step in range(width // 512):
        made.append(run_grads(0, step, rows_in, d_act, shapes, made[-1] if made else None))
    return made


def down_grads(experts, scaled, grads):
    width, units = grads[0].shape[1], scaled[0].shape[1] // experts
    shapes = (array((experts, units, width), f32),)
    made = []
    for step in range(width // 512):
        made.append(run_grads(1, step, scaled, grads, shapes, made[-1] if made else None))
    return made


def out_grads_kernel(plan, rows, *refs):
    count = len(plan)
    pieces, (spread, g_out, mixed, d_cols, sems) = refs[:count], refs[count:]
    copies = copy_pieces(pieces, plan, rows, pl.ds(0, mixed.shape[1]), mixed, sems)
    copies.append(pltpu.make_async_copy(spread.at[:, pl.ds(0, rows)], d_cols, sems.at[count]))
    start_all(copies)
    wait_all(copies)
    g_out[...] = dot_rows(mixed[...], d_cols[...].reshape(mixed.shape[0], d_cols.shape[2]))


def out_grads(ring, spread):
    blocks, _, columns = spread.shape
    breadth = ring.shard.shape[1]
    count = len(ring.pieces)
    shape = array((breadth, columns), f32)
    total = blocks * ring.rows
    return pl.pallas_call(
        functools.partial(out_grads_kernel, ring.plan, ring.rows),
        in_specs=[anywhere] * (count + 1),
        out_specs=full(shape),
        out_shape=shape,
        scratch_shapes=[
            pltpu.VMEM((total, breadth), bf16),
            pltpu.VMEM((blocks, ring.rows, columns), bf16),
            pltpu.SemaphoreType.DMA((count + 1,)),
        ],
        compiler_params=kernel_params(56),
        cost_estimate=cost(10**8, 10**5),
    )(*ring.pieces, spread)


def stack_layer_kernel(sums, zero, one, got, out):
    core = lax.axis_index("section")
    columns = zero.shape[1]
    rows = zero.shape[0] - (extra_rows if sums else 0)
    half = rows // 2
    for number, own in ((0, zero), (1, one)):

        @pl.when(core == number)
        def _():
            here = slice(number * columns, (number + 1) * columns)
            there = slice((1 - number) * columns, (2 - number) * columns)
            out[:rows, here] = own[:rows]
            out[:half, there] = got[half:rows]
            out[half:rows, there] = got[:half]
            if sums:
                total = joined_rows(own, rows, sums) + joined_rows(got, rows, sums)
                split_rows(out, rows, total)


def stack_layer(zero, one, got, sums=0):
    rows, columns = zero.shape
    kernel = functools.partial(stack_layer_kernel, sums)
    return simple(kernel, [array((rows, 2 * columns), zero.dtype)], zero, one, got)[0]


def projection_grads_kernel(plan, rows, *refs):
    count = len(plan)
    pieces, (spread, late_spread, w_query, w_key, w_value), refs = (
        refs[:count],
        refs[count : count + 5],
        refs[count + 5 :],
    )
    g_query, g_key, g_value, late, d_qkv, normed, parts, sems = refs
    tokens = rows - extra_rows
    copies = copy_pieces(pieces, plan, rows, pl.ds(0, d_qkv.shape[1]), d_qkv, sems)
    target = normed.at[:, pl.ds(0, tokens)]
    copies.append(pltpu.make_async_copy(spread, target, sems.at[count]))
    source = late_spread.at[:, pl.ds(tokens, parts.shape[1])]
    copies.append(pltpu.make_async_copy(source, parts, sems.at[count + 1]))
    start_all(copies)
    blocks, _, part = normed.shape
    normed[:, tokens:] = jnp.zeros((blocks, extra_rows, part), bf16)
    wait_all(copies)
    wide = g_query.shape[1] // 2
    head = g_key.shape[1] // 2
    both = dot_rows(normed[...].reshape(blocks * rows, part), d_qkv[...])
    for side in range(2):
        start = side * (wide + 2 * head)
        g_query[:, side * wide : (side + 1) * wide] = both[:, start : start + wide]
        g_key[:, side * head : (side + 1) * head] = both[:, start + wide : start + wide + head]
        g_value[:, side * head : (side + 1) * head] = both[
            :, start + wide + head : start + wide + 2 * head
        ]
    products = (
        jnp.sum(w_query[...].astype(f32) * g_query[...], axis=1, keepdims=True)
        + jnp.sum(w_key[...].astype(f32) * g_key[...], axis=1, keepdims=True)
        + jnp.sum(w_value[...].astype(f32) * g_value[...], axis=1, keepdims=True)
    )
    heads = jnp.zeros((1, 2 * head), f32)
    for block in range(blocks):
        heads = heads + joined_rows(d_qkv, block * rows + tokens, 2 * head)
    late[...] = jnp.zeros_like(late)
    late[8:, :part] = jnp.sum(parts[...].astype(f32), axis=0)
    late[:1, :part] = jnp.transpose(jnp.broadcast_to(products, (part, lanes)))[:1]
    late[1:2, : 2 * head] = heads


def projection_grads(ring, spread, late_spread, weights, head):
    blocks, tokens, part = spread.shape
    size = late_spread.shape[1] - tokens
    breadth = ring.shard.shape[1]
    wide = breadth // 2 - 2 * head
    count = len(ring.pieces)
    total = blocks * ring.rows
    shapes = (
        array((part, 2 * wide), f32),
        array((part, 2 * head), f32),
        array((part, 2 * head), f32),
        array((8 + size, max(part, 2 * head)), f32),
    )
    return pl.pallas_call(
        functools.partial(projection_grads_kernel, ring.plan, ring.rows),
        in_specs=[anywhere] * (count + 2) + [full(one) for one in weights],
        out_specs=tuple(full(one) for one in shapes),
        out_shape=shapes,
        scratch_shapes=[
            pltpu.VMEM((total, breadth), bf16),
            pltpu.VMEM((blocks, ring.rows, part), bf16),
            pltpu.VMEM((blocks, size, part), bf16),
            pltpu.SemaphoreType.DMA((count + 2,)),
        ],
        compiler_params=kernel_params(56),
        cost_estimate=cost(20 * total * part * breadth, 4 * total * breadth),
    )(*ring.pieces, spread, late_spread, *weights)


def both_rows(shard):
    far = swap_x(shard)
    return (shard, far, swap_core(shard), swap_core(far))


def merge_kernel(own, got, kept, given):
    block = own[...] + got[...].astype(f32)
    half = kept.shape[0]
    kept[...] = block[:half]
    given[...] = block[half:].astype(bf16)


def own_rows(own, other):
    rows, width = own.shape
    shapes = [array((rows // 2, width), kind) for kind in (f32, bf16)]
    kept, given = simple(merge_kernel, shapes, own, swap_core(other))
    return kept, swap_x(given)


def route_kernel(layer, x, kept, got, tiny, mask, mid_out, payload, gates_out):
    experts = mask.shape[1]
    width = x.shape[1]
    start = layer * (experts + 4)
    mid = x[...] + kept[...] + got[...].astype(f32)
    mid_out[...] = mid
    gain = tiny[start + experts + 1 : start + experts + 2]
    normed = (mid * inverse_rms(mid) * gain).astype(bf16)
    payload[:, :width] = normed
    logits = dot_cols(normed, tiny[start : start + experts].astype(bf16))
    logits = jnp.where(mask[...] > 0.0, logits, masked_score)
    weights = jnp.exp(logits - jnp.max(logits, axis=-1, keepdims=True))
    gates = weights / jnp.sum(weights, axis=-1, keepdims=True)
    gates_out[...] = gates
    high = gates.astype(bf16)
    low = (gates - high.astype(f32)).astype(bf16)
    payload[:, width:] = jnp.zeros((x.shape[0], lanes), bf16)
    payload[:, width : width + experts] = high
    payload[:, width + lanes // 2 : width + lanes // 2 + experts] = low


def route(layer, x, kept, got, tiny, mask):
    rows, width = x.shape
    shapes = [
        array((rows, width), f32),
        array((rows, width + lanes), bf16),
        array(mask.shape, f32),
    ]
    kernel = functools.partial(route_kernel, layer)
    return simple(kernel, shapes, x, kept, got, tiny, mask)


def sum_parts(parts):
    total = parts[0][...]
    for one in parts[1:]:
        total = total + one[...].astype(f32)
    return total


def enter_kernel(count, experts, mid, *refs):
    parts, (tiny, x_out, normed) = refs[:count], refs[count:]
    x = (mid[...] + sum_parts(parts)).astype(bf16).astype(f32)
    x_out[...] = x
    row = 2 * experts + 4
    normed[...] = (x * inverse_rms(x) * tiny[row : row + 1]).astype(bf16)


def enter(mid, parts, tiny, experts):
    shapes = [array(mid.shape, f32), array(mid.shape, bf16)]
    kernel = functools.partial(enter_kernel, len(parts), experts)
    return simple(kernel, shapes, mid, *parts, tiny)


def finish_kernel(mid, *refs):
    refs[-1][...] = (mid[...] + sum_parts(refs[:-1])).astype(bf16)


def finish(mid, parts):
    return simple(finish_kernel, [array(mid.shape, bf16)], mid, *parts)[0]


def norm_back(value, gain, grad):
    inverse = inverse_rms(value)
    hat = value * inverse
    d_hat = grad * gain
    d_value = inverse * (d_hat - hat * jnp.mean(d_hat * hat, axis=-1, keepdims=True))
    return d_value, jnp.sum(grad * hat, axis=0, keepdims=True)


def unroute_kernel(count, layer, *refs):
    parts, refs = refs[:count], refs[count:]
    grad, mid, tiny, gates_in, payload, d_out, d_low, g_router, g_gain = refs
    width = mid.shape[1]
    experts = gates_in.shape[1]
    start = layer * (experts + 4)
    back = sum_parts(parts)
    gates = gates_in[...]
    gate_grad = back[:, width : width + experts]
    d_logits = gates * (gate_grad - jnp.sum(gates * gate_grad, axis=-1, keepdims=True))
    d_logits = d_logits.astype(bf16)
    d_normed = back[:, :width] + dot(d_logits, tiny[start : start + experts].astype(bf16))
    gain = tiny[start + experts + 1 : start + experts + 2]
    d_mid, gain_sum = norm_back(mid[...], gain, d_normed)
    d_mid = d_mid + grad[...].astype(f32)
    d_out[...] = d_mid
    d_low[...] = d_mid.astype(bf16)
    g_router[...] = dot_rows(d_logits, payload[:, :width])
    g_gain[...] = gain_sum


def unroute(layer, parts, grad, mid, tiny, gates, payload):
    width, experts = mid.shape[1], gates.shape[1]
    shapes = [
        array(mid.shape, f32),
        array(mid.shape, bf16),
        array((experts, width), f32),
        array((1, width), f32),
    ]
    kernel = functools.partial(unroute_kernel, len(parts), layer)
    return simple(kernel, shapes, *parts, grad, mid, tiny, gates, payload)


def leave_kernel(row, kept, got, x, d_mid, tiny, d_out):
    d_normed = kept[...] + got[...].astype(f32)
    d_x, _ = norm_back(x[...], tiny[row : row + 1], d_normed)
    d_out[...] = (d_mid[...] + d_x).astype(bf16)


def leave(layer, experts, kept, got, x, d_mid, tiny):
    kernel = functools.partial(leave_kernel, layer * (experts + 4) + experts)
    return simple(kernel, [array(x.shape, bf16)], kept, got, x, d_mid, tiny)[0]


def count_rows(tiles):
    return max(tile_rows, tiles[0][0].shape[0])


def apply_experts(tiles, weights, ones, layer):
    kept, outs, stores = [], [], None
    for number, pieces in enumerate(tiles):
        out, saved, stores = run_experts(
            pieces, weights, ones, layer, number, count_rows(tiles), stores
        )
        outs.append(out)
        kept.append(saved)
    return outs, kept, stores


def apply_experts_back(tiles, weights, ones, kept, layer):
    backs, stores = [], None
    for number, (pieces, saved) in enumerate(zip(tiles, kept)):
        back, stores = run_experts_back(
            pieces, weights, ones, saved, layer, number, count_rows(tiles), stores
        )
        backs.append(back)
    return backs, stores


def choose_kernel(zero, one, out):
    core = lax.axis_index("section")
    for number, own in enumerate((zero, one)):

        @pl.when(core == number)
        def _():
            out[: own.shape[0]] = own[...]


def small_kernel(router0, gain0, router1, gain1, own, other):
    core = lax.axis_index("section")
    layers = ((router0, gain0), (router1, gain1))
    experts = router0.shape[0]
    for number in range(2):

        @pl.when(core == number)
        def _():
            for out, layer in ((own, number), (other, 1 - number)):
                router, gain = layers[layer]
                out[...] = jnp.zeros_like(out)
                out[:experts] = router[...]
                out[experts : experts + 1] = gain[...]


def late_kernel(zero, one, own, got, out):
    rows = zero.shape[0]
    choose_kernel(zero, one, out)
    out[rows:] = (own[...] + got[...]).astype(bf16)


def other_layer_kernel(zero, one, out, sem):
    core = lax.axis_index("section")
    for number, source in enumerate((one, zero)):

        @pl.when(core == number)
        def _():
            pltpu.make_async_copy(source, out, sem).start()

    pltpu.make_async_copy(zero, out, sem).wait()


def exchange(zero, one):
    sent = pl.pallas_call(
        other_layer_kernel,
        in_specs=[anywhere] * 2,
        out_specs=anywhere,
        out_shape=array(zero.shape, zero.dtype),
        scratch_shapes=[pltpu.SemaphoreType.DMA],
        compiler_params=kernel_params(8),
        cost_estimate=cost(1000, 1000),
    )(zero, one)
    got = swap_core(sent)
    return zero, one, got, got


def by_columns(value, split):
    columns = value.shape[1] // split
    return jnp.stack([value[:, i * columns : (i + 1) * columns] for i in range(split)])


def to_owners(blocks):
    return lax.all_to_all(blocks, "expert", split_axis=0, concat_axis=0, tiled=True)


def body(
    ends_in,
    attn_gain,
    w_query,
    key_matrix,
    value_matrix,
    query_gain,
    key_gain,
    w_out,
    ffn_gain,
    router,
    w_gate,
    w_up,
    w_down,
    routes,
    lengths,
):
    core = lax.axis_index("section")
    first = core == 0
    side = lax.axis_index("tensor")
    index = lax.axis_index("expert")
    split = lax.axis_size("expert")
    rows, width = ends_in.shape[2:]
    half = rows // 2
    experts = router.shape[2]
    head = query_gain.shape[1] * split

    def pick(zero, one):
        return jnp.where(first, zero, one)

    def mine(pair):
        return pick(pair[0], pair[1])

    def theirs(pair):
        return pick(pair[1], pair[0])

    def by_layer(own):
        got = swap_core(own)
        return pick(own, got), pick(got, own)

    def pick_side(zero, one):
        return jnp.where(side == 0, zero, one)

    def half_rows(block):
        return pick_side(block[:half], block[half:])

    def side_first(block):
        return pick_side(block, cat(block[half:], block[:half]))

    part = w_query.shape[1]
    columns = w_query.shape[2] // 2
    transposed = w_out[0].T
    groups = [
        cat(
            w_query[0][:, g * columns : (g + 1) * columns],
            key_matrix[0][:, g * head : (g + 1) * head],
            value_matrix[0][:, g * head : (g + 1) * head],
            transposed[:, g * columns : (g + 1) * columns],
            axis=1,
        )
        for g in range(2)
    ]
    kept, got = mine(groups), swap_core(theirs(groups))
    breadth = kept.shape[1]

    share = head // split
    gains = cat(query_gain[0][:, None], key_gain[0][:, None], axis=1)
    tiny = cat(
        router[0],
        attn_gain[0][:, None],
        ffn_gain[0][:, None],
        jnp.pad(gains, ((0, part - share), (0, 0))),
        axis=1,
    )
    size = tiny.shape[1]
    tiny = cat(*by_layer(tiny), axis=1)
    tiny = jnp.pad(tiny, ((0, 0), (0, -2 * size % lanes)))
    ring0 = Ring(cat(pick(kept, got), tiny, axis=1))
    ring1 = Ring(pick(got, kept))
    started = ring0.advance()

    ends_in, w_gate, w_up, w_down = lax.optimization_barrier(
        (ends_in, w_gate, w_up, w_down, *started)
    )[:4]
    own_weights = (w_gate[0], w_up[0], w_down[0])
    expert_weights = own_weights + tuple(swap_core(one) for one in own_weights)
    crossed = swap_core(ends_in[0])
    x_all, grad_all = pick(ends_in[0], crossed), pick(crossed, ends_in[0])
    x_own = mine(x_all)
    x_in = half_rows(x_own).astype(f32)
    grad_last = half_rows(mine(grad_all))
    x_both = cat(side_first(x_own), side_first(theirs(x_all))).astype(f32)
    x_hat = x_both * inverse_rms(x_both)

    routes, lengths = lax.optimization_barrier((routes, lengths, *ring0.advance()))[:2]
    routes_crossed = swap_core(pick(routes[0, 1], routes[0, 0]))
    routes_own = [pick(routes[0, 0], routes_crossed), pick(routes_crossed, routes[0, 1])]
    expert_ids = jnp.arange(experts, dtype=jnp.int32)
    masks = [
        jnp.any(half_rows(r)[:, :, None] == expert_ids[None, None, :], axis=1).astype(f32)
        for r in routes_own
    ]
    per_device = w_gate.shape[1]
    lane_ids = jnp.arange(lanes, dtype=jnp.int32)
    local_ids = index * per_device + jnp.arange(per_device, dtype=jnp.int32)
    ones = (lane_ids[None, :] == local_ids[:, None]).astype(f32)
    row_index = (jnp.arange(rows, dtype=jnp.int32) + side * half) % rows
    length_pair = [pick(lengths[0, 0], lengths[1, 0]), pick(lengths[1, 0], lengths[0, 0])]
    tables = make_tables(length_pair, row_index, head)

    ring0.advance()
    ring0.advance()
    ring1.advance(*ring0.latest)

    tiny, normed0, mixed0, raw0, probs0, own, other = attend(
        0, ring0, breadth, split, experts, (x_hat,), tables
    )
    other = after(other, *ring1.latest)
    mid0, payload0, gates0 = route(0, x_in, *own_rows(own, other), tiny, masks[0])
    gather = Gather(payload0)
    gather.along_z()
    gather.near()
    gather.far()
    tiles = gather.tiles()
    ring1.advance(tiles[-1][-1])
    outs0, kept0, stores0 = apply_experts(tiles, expert_weights, ones, 0)
    scatter = Scatter(outs0)
    scatter.far()
    scatter.near(beside=ring1.latest)
    parts = scatter.along_z()
    ring1.advance(*parts)
    ring1.advance()
    x_mid, shard = enter(mid0, parts, tiny, experts)

    normed_pieces = both_rows(shard)
    grad_gather = Gather(grad_last)
    along = grad_gather.along_z(normed_pieces[-1])
    normed1, mixed1, raw1, probs1, own, other = attend(
        1, ring1, breadth, split, experts, (*normed_pieces, tiny), tables
    )
    other = after(other, *along)
    beside = grad_gather.near(own)
    mid1, payload1, gates1 = route(1, x_mid, *own_rows(own, other), tiny, masks[1])
    gather = Gather(after(payload1, *beside))
    gather.along_z()
    gather.near()
    gather.far()
    tiles = gather.tiles()
    beside = grad_gather.far(tiles[-1][-1])
    mixed_got = swap_core(pick(mixed1, mixed0))
    ring_mixed = Ring(stack_layer(mixed0, mixed1, mixed_got))
    ring_mixed.advance(tiles[-1][-1])
    outs1, kept1, stores1 = apply_experts(tiles, expert_weights, ones, 1)

    outs1[-1][-1] = after(outs1[-1][-1], *ring_mixed.latest, *beside)
    tiles = grad_gather.tiles(outs1[-1][-1])
    ring_mixed.advance(tiles[-1][-1])
    backs, back_stores1 = apply_experts_back(tiles, expert_weights, ones, kept1, 1)
    scatter = Scatter(backs)
    scatter.far(*ring_mixed.latest)
    reached = scatter.near()
    out_scatter = Scatter(outs1)
    beside = out_scatter.far(*reached)
    parts = scatter.along_z()
    parts[-1] = after(parts[-1], *beside)
    d_mid, d_low, g_router1, g_ffn_gain1 = unroute(
        1, parts, grad_last, mid1, tiny, gates1, payload1
    )
    d_pieces = both_rows(d_low)
    ring_mixed.advance(d_pieces[-1])

    if small_grid():
        rows_in = exchange(after(stores0[0], d_pieces[-1]), stores1[0])
        early = (rows_in[2],)
    else:
        early = ()
    d_attn1, d_qkv1, d_own, d_other = attend_back(
        1, ring1, breadth, split, experts, d_pieces, raw1, probs1, tiny, tables
    )
    d_other = after(d_other, *ring_mixed.latest, *early)
    d_one = leave(1, experts, *own_rows(d_own, d_other), x_mid, d_mid, tiny)

    gather = Gather(d_one)
    gather.along_z()
    beside = out_scatter.near(d_one)
    gather.near(*beside)
    gather.far()
    tiles = gather.tiles()
    backs, back_stores0 = apply_experts_back(tiles, expert_weights, ones, kept0, 0)

    if not small_grid():
        rows_in = exchange(after(stores0[0], back_stores0[0]), stores1[0])
    d_act = exchange(after(back_stores0[0], rows_in[2]), back_stores1[0])
    wide = wide_grads(per_device, rows_in, d_act)
    scatter = Scatter(backs)
    normed_own = simple(
        choose_kernel, [array(normed0.shape, bf16)], normed0, after(normed1, *scatter.far())
    )[0]
    normed_blocks = by_columns(normed_own, split)
    scatter.near(beside=(*wide[1], normed_blocks))
    parts = scatter.along_z()
    parts[-1] = after(parts[-1], *wide[3])
    d_mid, d_low, g_router0, g_ffn_gain0 = unroute(
        0, parts, d_one, mid0, tiny, gates0, payload0
    )
    d_pieces = both_rows(d_low)
    normed_spread = to_owners(after(normed_blocks, d_pieces[-1]))
    out_parts = out_scatter.along_z(d_pieces[-1])
    d_attn0, d_qkv0, d_own, d_other = attend_back(
        0, ring0, breadth, split, experts, d_pieces, raw0, probs0, tiny, tables
    )

    qkv_got = swap_core(pick(d_qkv1, after(d_qkv0, normed_spread, *out_parts)))
    ring_d = Ring(stack_layer(d_qkv0, d_qkv1, qkv_got, 2 * head))
    one_round = ring_d.advance()
    d_other = after(d_other, ring_d.shard)
    d_zero = leave(0, experts, *own_rows(d_own, d_other), x_in, d_mid, tiny)
    scaled = exchange(after(stores0[1], ring_d.shard), stores1[1])
    gate = ring_d.shard if small_grid() else scaled[2]
    late = (scaled, exchange(after(back_stores0[1], gate), back_stores1[1]))
    down = down_grads(per_device, *late)
    ring_d.advance()
    rows_small = -(-(experts + 1) // 16) * 16
    small_own, small_other = simple(
        small_kernel,
        [array((rows_small, width), f32)] * 2,
        after(g_router0, *one_round),
        g_ffn_gain0,
        g_router1,
        g_ffn_gain1,
    )
    late_rows = simple(
        late_kernel,
        [array((2 * rows + rows_small, width), bf16)],
        d_attn0,
        d_attn1,
        small_own,
        swap_core(small_other),
    )[0]
    late_spread = to_owners(by_columns(late_rows, split))
    three_rounds = ring_d.advance(*down[1])
    ring_d.advance(*down[3])
    ring_mixed.advance(*three_rounds)
    g_out = out_grads(ring_mixed, late_spread)
    out1 = finish(mid1, out_parts)
    end_own = pick(d_zero, out1)
    end_got = swap_core(pick(out1, d_zero))
    projections = (w_query[0], key_matrix[0], value_matrix[0])
    g_query, g_key, g_value, late = projection_grads(
        ring_d, normed_spread, after(late_spread, *ring_mixed.latest), projections, head
    )
    (g_gate, g_up), (g_down,) = wide[-1], down[-1]

    small = late + swap_x(late)
    g_attn_gain = small[0, :part] / attn_gain[0].astype(f32)
    g_query_gain = lax.dynamic_slice(small[1], (index * share,), (share,))
    g_key_gain = lax.dynamic_slice(small[1], (head + index * share,), (share,))
    g_router = small[8 : 8 + experts, :part].T
    g_ffn_gain = small[8 + experts, :part]

    ends = jnp.stack([pick(end_own, end_got), pick(end_got, end_own)])
    ends_far = swap_x(ends)
    ends_out = cat(pick_side(ends, ends_far), pick_side(ends_far, ends), axis=1)

    outs = (
        ends_out,
        g_attn_gain,
        g_query,
        g_key,
        g_value,
        g_query_gain,
        g_key_gain,
        g_out,
        g_ffn_gain,
        g_router,
        g_gate,
        g_up,
        g_down,
    )
    return tuple(one[None] for one in outs)


def solution(mesh):
    return jax.shard_map(
        body,
        mesh=mesh,
        in_specs=(
            P("section", None, "expert", None),
            P("section", "expert"),
            P("section", "expert", "tensor"),
            P("section", "expert", "tensor"),
            P("section", "expert", "tensor"),
            P("section", "expert"),
            P("section", "expert"),
            P("section", "tensor", "expert"),
            P("section", "expert"),
            P("section", "expert", None),
            P("section", "expert", None, "tensor"),
            P("section", "expert", None, "tensor"),
            P("section", "expert", "tensor", None),
            P("section", None, "expert", None),
            P(None, "expert", None),
        ),
        out_specs=(
            P("section", None, "expert", None),
            P("section", "expert"),
            P("section", "expert", "tensor"),
            P("section", "expert", "tensor"),
            P("section", "expert", "tensor"),
            P("section", "expert"),
            P("section", "expert"),
            P("section", "tensor", "expert"),
            P("section", "expert"),
            P("section", "expert", None),
            P("section", "expert", None, "tensor"),
            P("section", "expert", None, "tensor"),
            P("section", "expert", "tensor", None),
        ),
        check_vma=False,
    )
```

```python
import functools

import jax
import jax.numpy as jnp
import numpy as np
from jax import lax
from jax.experimental import pallas as pl
from jax.experimental.pallas import tpu as pltpu
from jax.sharding import PartitionSpec as P

epsilon = 1e-06
rope_base = 1000000.0
masked_score = -1e30
bf16 = jnp.bfloat16
f32 = jnp.float32
lanes = 128
tile_rows = 512
grad_columns = 1024


def dot(left, right):
    return jnp.dot(left, right, preferred_element_type=f32)


def dot_rows(left, right):
    return lax.dot_general(left, right, (((0,), (0,)), ((), ())), preferred_element_type=f32)


def dot_cols(left, right):
    return lax.dot_general(left, right, (((1,), (1,)), ((), ())), preferred_element_type=f32)


def cat(*pieces, axis=0):
    return jnp.concatenate(pieces, axis=axis)


def swap_core(value):
    return lax.ppermute(value, "section", [(0, 1), (1, 0)])


def swap_x(value):
    return lax.ppermute(value, "tensor", [(0, 1), (1, 0)])


def swap_e(value, bits):
    count = lax.axis_size("expert")
    return lax.ppermute(value, "expert", [(i, i ^ bits) for i in range(count)])


def small_grid():
    return lax.axis_size("expert") == 8


def after(value, *others):
    return lax.optimization_barrier((value, *others))[0] if others else value


anywhere = pl.BlockSpec(memory_space=pl.ANY)


def full(one):
    return pl.BlockSpec(one.shape, lambda *_: (0,) * len(one.shape))


def array(shape, kind):
    return jax.ShapeDtypeStruct(shape, kind)


def kernel_params(megabytes):
    return pltpu.CompilerParams(vmem_limit_bytes=megabytes * 2**20)


def cost(flops, moved):
    return pl.CostEstimate(flops=flops, bytes_accessed=moved, transcendentals=0)


def simple(kernel, shapes, *operands):
    return pl.pallas_call(
        kernel,
        in_specs=[full(one) for one in operands],
        out_specs=tuple(full(one) for one in shapes),
        out_shape=tuple(shapes),
        compiler_params=kernel_params(16),
        cost_estimate=cost(1000, 1000),
    )(*operands)


def stack_kernel(*refs):
    start = 0
    for ref in refs[:-1]:
        refs[-1][start : start + ref.shape[0]] = ref[...]
        start += ref.shape[0]


def stack(*pieces):
    rows = sum(one.shape[0] for one in pieces)
    return simple(stack_kernel, [array((rows, pieces[0].shape[1]), pieces[0].dtype)], *pieces)[0]


def near_kernel(to_x, top, to_y, bottom, out_x, out_y):
    half = top.shape[0]
    out_x[:half] = (to_x[:half].astype(f32) + top[...].astype(f32)).astype(bf16)
    out_x[half:] = to_x[half:]
    out_y[:half] = to_y[:half]
    out_y[half:] = (to_y[half:].astype(f32) + bottom[...].astype(f32)).astype(bf16)


def total_kernel(own, from_x, from_y, kept, *blocks):
    total = own[...].astype(f32) + from_x[...].astype(f32) + from_y[...].astype(f32)
    step = kept.shape[0]
    kept[...] = total[:step]
    for number, block in enumerate(blocks):
        block[...] = total[(number + 1) * step : (number + 2) * step].astype(bf16)


class Gather:
    def __init__(self, shard):
        self.shard = shard
        self.small = small_grid()

    def along_z(self, *gate):
        if self.small:
            shard = after(self.shard, *gate)
            self.line = (shard, swap_e(shard, 2), swap_e(shard, 4), swap_e(shard, 6))
            return self.line[1:]
        return ()

    def near(self, *gate):
        if self.small:
            own = after(stack(*self.line), *gate)
            self.near_pieces = (own, swap_x(own), swap_e(own, 1))
            return self.near_pieces[1:]
        return ()

    def far(self, *gate):
        if self.small:
            own, from_x, from_y = self.near_pieces
            half = own.shape[0] // 2
            self.far_pieces = (
                swap_e(after(from_x[:half], *gate), 1),
                swap_x(after(from_y[half:], *gate)),
            )
            return self.far_pieces
        shard = after(self.shard, *gate)
        self.whole = lax.all_gather(shard, ("expert", "tensor"), axis=0, tiled=True)
        return (self.whole,)

    def tiles(self, *gate):
        if self.small:
            top, bottom = self.far_pieces
            return [[*self.near_pieces, top, after(bottom, *gate)]]
        whole = after(self.whole, *gate)
        return [[whole]] * (whole.shape[0] // tile_rows)


class Scatter:
    def __init__(self, tiles):
        self.tiles = tiles
        self.small = small_grid()

    def far(self, *gate):
        if self.small:
            far_top, far_bottom = self.tiles[0][3:]
            self.top = swap_e(after(far_top, *gate), 1)
            self.bottom = swap_x(after(far_bottom, *gate))
            return (self.top, self.bottom)
        return ()

    def near(self, *gate, beside=()):
        if self.small:
            own, to_x, to_y = self.tiles[0][:3]
            shape = array(to_x.shape, bf16)
            to_x, to_y = simple(near_kernel, [shape] * 2, to_x, self.top, to_y, self.bottom)
            from_x, from_y = swap_x(after(to_x, *gate)), swap_e(after(to_y, *gate), 1)
            from_x = after(from_x, *beside)
            rows, columns = own.shape
            shapes = [array((rows // 4, columns), kind) for kind in (f32, bf16, bf16, bf16)]
            self.blocks = simple(total_kernel, shapes, own, from_x, from_y)
            return self.blocks[:1]
        return ()

    def along_z(self, *gate):
        if self.small:
            kept, *blocks = self.blocks
            moved = [swap_e(after(one, *gate), bits) for one, bits in zip(blocks, (2, 4, 6))]
            return [kept, *moved]
        whole = cat(*[one for pieces in self.tiles for one in pieces])
        whole = after(whole, *gate).astype(f32)
        return [lax.psum_scatter(whole, ("expert", "tensor"), scatter_dimension=0, tiled=True)]


cycle = (0, 2, 4, 6, 7, 5, 3, 1)


def owner_at(distance):
    index = lax.axis_index("expert")
    place = jnp.where(index % 2 == 0, index // 2, 7 - index // 2)
    spot = (place + distance) & 7
    return jnp.where(spot < 4, 2 * spot, 15 - 2 * spot)


class Ring:
    def __init__(self, shard):
        self.shard = shard
        self.rows = shard.shape[0]
        self.plus = self.minus = shard
        self.pieces = [shard]
        self.plan = [(0, 0)]
        self.latest = (shard,)
        self.small = small_grid()

    def advance(self, *gate):
        if not self.small:
            if len(self.latest) == 1 and self.latest[0] is self.shard:
                whole = lax.all_gather(after(self.shard, *gate), "expert", axis=0, tiled=True)
                self.pieces, self.plan, self.latest = [whole], [(None, 0)], (whole,)
            return self.latest
        number = len(self.pieces) // 2 + 1
        up = [(a, b) for a, b in zip(cycle, cycle[1:] + cycle[:1])]
        down = [(b, a) for a, b in up]
        plus, minus, middle = self.plus, self.minus, 0
        if number == 4:
            middle = self.rows // 32 * 16
            plus, minus = plus[:middle], minus[middle:]
        self.plus = lax.ppermute(after(plus, *gate), "expert", up)
        self.minus = lax.ppermute(after(minus, *gate), "expert", down)
        self.pieces += [self.plus, self.minus]
        self.plan += [(-number, 0), (number, middle)]
        self.latest = (self.plus, self.minus)
        return self.latest

    def collect(self, part):
        if not self.small:
            return part(self.pieces[0])
        columns = part(self.shard).shape[1]
        whole = jnp.zeros((8 * self.rows, columns), self.shard.dtype)
        for (distance, start), piece in zip(self.plan, self.pieces):
            place = (owner_at(distance) * self.rows + start, 0)
            whole = lax.dynamic_update_slice(whole, part(piece), place)
        return whole


def copy_pieces(pieces, plan, rows, columns, target, sems, first=0):
    copies = []
    for number, ((distance, start), piece) in enumerate(zip(plan, pieces)):
        place = start
        if distance is not None:
            place = pl.multiple_of(owner_at(distance) * rows + start, 16)
        copies.append(
            pltpu.make_async_copy(
                piece.at[:, columns],
                target.at[pl.ds(place, piece.shape[0]), columns],
                sems.at[first + number],
            )
        )
    return copies


def start_all(copies):
    for one in copies:
        one.start()


def wait_all(copies):
    for one in copies:
        one.wait()


def inverse_rms(value):
    return lax.rsqrt(jnp.mean(value * value, axis=-1, keepdims=True) + epsilon)


def rms_norm(value, gain):
    return value * inverse_rms(value) * gain


def layout(lengths_row, row_index):
    ends = jnp.cumsum(lengths_row, dtype=jnp.int32)
    starts = ends - lengths_row
    segment = jnp.sum((row_index[:, None] >= ends[None, :]).astype(jnp.int32), axis=1)
    member = segment[:, None] == jnp.arange(ends.shape[0], dtype=jnp.int32)[None, :]
    return segment, row_index - jnp.sum(jnp.where(member, starts[None, :], 0), axis=1)


def make_tables(length_pair, row_index, head):
    half = head // 2
    inverse = np.power(rope_base, -(np.arange(half) * 2.0) / head).astype(np.float32)
    segments, angles = [], []
    for number, one in enumerate(length_pair):
        segment, position = layout(one, row_index)
        segments.append(segment + number * (one.shape[0] + 1))
        angles.append(position.astype(f32)[:, None] * inverse[None, :])
    segment, angle = cat(*segments), cat(*angles)
    order = cat(row_index, row_index)
    allowed = (segment[:, None] == segment[None, :]) & (order[None, :] <= order[:, None])
    cosine, sine = jnp.cos(angle), jnp.sin(angle)
    return cat(cosine, cosine, axis=1), cat(-sine, sine, axis=1), allowed.astype(f32)


def rope(value, cosine, sine):
    return value * cosine + pltpu.roll(value, value.shape[1] // 2, 1) * sine


def rope_back(value, cosine, sine):
    return value * cosine + pltpu.roll(value * sine, value.shape[1] // 2, 1)


def from_heads(row, split, share):
    wide, head = row.shape[1], split * share
    part = wide // split
    lane = lax.broadcasted_iota(jnp.int32, (wide, head), 0)
    place = lax.broadcasted_iota(jnp.int32, (wide, head), 1)
    found = (lane // part == place // share) & (lane % part == place % share)
    chosen = jnp.where(found, 1.0, 0.0).astype(bf16)
    return dot(jnp.broadcast_to(row, (8, wide)).astype(bf16), chosen)[:1]


def attend_kernel(plan, rows, layer, split, experts, *refs):
    count = len(plan)
    pieces, refs = refs[:count], refs[count:]
    if layer == 0:
        (x_hat, cosine, sine, allowed), refs = refs[:4], refs[4:]
        tiny, normed, *refs = refs
    else:
        normed_pieces, (tiny, cosine, sine, allowed), refs = refs[:4], refs[4:8], refs[8:]
        normed, *refs = refs
    mixed, raw_out, probs_out, out_own, out_other, weights, sems = refs
    head = cosine.shape[1]
    group = probs_out.shape[0]
    near_columns = raw_out.shape[1]
    far_columns = mixed.shape[1]
    breadth = near_columns + far_columns
    near = copy_pieces(pieces, plan, rows, pl.ds(0, near_columns), weights, sems)
    far = copy_pieces(pieces, plan, rows, pl.ds(near_columns, far_columns), weights, sems, count)
    if layer == 0:
        last = pl.ds(breadth, weights.shape[1] - breadth)
        small = copy_pieces(pieces, plan, rows, last, weights, sems, 2 * count)
        start_all(small)
    start_all(near)
    start_all(far)
    share = head // split
    size = experts + 4
    if layer == 0:
        wait_all(small)
        tiny[...] = jnp.transpose(weights[:, breadth:].astype(f32))
        normed[...] = (x_hat[...] * tiny[experts : experts + 1]).astype(bf16)
    else:
        half = normed_pieces[0].shape[0]
        for number, piece in enumerate(normed_pieces):
            normed[number * half : (number + 1) * half] = piece[...]
    start = layer * size + experts
    query_gain = from_heads(tiny[start + 2 : start + 3], split, share)
    key_gain = from_heads(tiny[start + 3 : start + 4], split, share)
    wait_all(near)
    raw = dot(normed[...], weights[:, :near_columns])
    raw_out[...] = raw
    cos, sin, allow = cosine[...], sine[...], allowed[...] > 0.0
    k_raw = raw[:, group * head : (group + 1) * head]
    keys = rope(k_raw * inverse_rms(k_raw) * key_gain, cos, sin).astype(bf16)
    values = raw[:, (group + 1) * head :].astype(bf16)
    for number in range(group):
        q_raw = raw[:, number * head : (number + 1) * head]
        query = rope(q_raw * inverse_rms(q_raw) * query_gain, cos, sin) * head ** (-0.5)
        scores = jnp.where(allow, dot_cols(query.astype(bf16), keys), masked_score)
        unscaled = jnp.exp(scores - jnp.max(scores, axis=-1, keepdims=True))
        probs = unscaled / jnp.sum(unscaled, axis=-1, keepdims=True)
        probs_out[number] = probs
        mixed[:, number * head : (number + 1) * head] = dot(probs.astype(bf16), values).astype(
            bf16
        )
    wait_all(far)
    out = dot_cols(mixed[...], weights[:, near_columns:breadth])
    half = out_own.shape[0]
    out_own[...] = out[:half]
    out_other[...] = out[half:].astype(bf16)


def attend(layer, ring, breadth, split, experts, inputs, tables):
    head = tables[0].shape[1]
    rows = tables[0].shape[0]
    width = inputs[0].shape[1]
    group = (breadth // head - 2) // 2
    near = (group + 2) * head
    columns = breadth if layer else ring.shard.shape[1]
    small = (*inputs, *tables)
    shapes = (
        array((rows, width), bf16),
        array((rows, group * head), bf16),
        array((rows, near), f32),
        array((group, rows, rows), f32),
        array((rows // 2, width), f32),
        array((rows // 2, width), bf16),
    )
    if layer == 0:
        shapes = (array((columns - breadth, width), f32), *shapes)
    count = len(ring.pieces)
    return pl.pallas_call(
        functools.partial(attend_kernel, ring.plan, ring.rows, layer, split, experts),
        in_specs=[anywhere] * count + [full(one) for one in small],
        out_specs=tuple(full(one) for one in shapes),
        out_shape=shapes,
        scratch_shapes=[pltpu.VMEM((width, columns), bf16), pltpu.SemaphoreType.DMA((3 * count,))],
        compiler_params=kernel_params(26),
        cost_estimate=cost(12 * rows * width * breadth, 2 * width * breadth),
    )(*ring.pieces, *small)


extra_rows = 16


def split_rows(out, start, value):
    size = value.shape[1]
    out[start:] = jnp.zeros((extra_rows, out.shape[1]), bf16)
    high = value.astype(bf16)
    out[start : start + 1, :size] = high
    out[start + 1 : start + 2, :size] = (value - high.astype(f32)).astype(bf16)


def joined_rows(rows, start, size):
    return rows[start : start + 1, :size].astype(f32) + rows[
        start + 1 : start + 2, :size
    ].astype(f32)


def attend_back_kernel(plan, block_rows, layer, axis, experts, *refs):
    count = len(plan)
    pieces, refs = refs[:count], refs[count:]
    d_pieces, refs = refs[:4], refs[4:]
    raw_in, probs_in, tiny, cosine, sine = refs[:5]
    d_attn, d_qkv, d_own, d_other, weights, sems = refs[5:]
    head = cosine.shape[1]
    rows = raw_in.shape[0]
    start = layer * (experts + 4) + experts
    query_gain = from_heads(tiny[start + 2 : start + 3], axis, head // axis)
    key_gain = from_heads(tiny[start + 3 : start + 4], axis, head // axis)
    half = d_pieces[0].shape[0]
    for number, piece in enumerate(d_pieces):
        d_attn[number * half : (number + 1) * half] = piece[...]
    group = probs_in.shape[0]
    split = raw_in.shape[1]
    rest = weights.shape[1] - split
    near = copy_pieces(pieces, plan, block_rows, pl.ds(split, rest), weights, sems)
    far = copy_pieces(pieces, plan, block_rows, pl.ds(0, split), weights, sems, count)
    start_all(near)
    cos, sin = cosine[...], sine[...]
    wait_all(near)
    start_all(far)
    d_mixed = dot(d_attn[...], weights[:, split:]).astype(bf16)
    k_raw = raw_in[:, group * head : (group + 1) * head]
    k_inverse = inverse_rms(k_raw)
    k_hat = k_raw * k_inverse
    keys = rope(k_hat * key_gain, cos, sin).astype(bf16)
    values = raw_in[:, (group + 1) * head :].astype(bf16)
    factor = head ** (-0.5)
    d_keys = jnp.zeros_like(k_raw)
    d_values = jnp.zeros_like(k_raw)
    gain_sum = jnp.zeros_like(query_gain)
    for number in range(group):
        span = slice(number * head, (number + 1) * head)
        q_raw = raw_in[:, span]
        q_inverse = inverse_rms(q_raw)
        q_hat = q_raw * q_inverse
        query = (rope(q_hat * query_gain, cos, sin) * factor).astype(bf16)
        probs = probs_in[number]
        d_one = d_mixed[:, span]
        d_probs = dot_cols(d_one, values)
        d_scores = probs * (d_probs - jnp.sum(probs * d_probs, axis=-1, keepdims=True))
        d_scores = d_scores.astype(bf16)
        d_values = d_values + dot_rows(probs.astype(bf16), d_one)
        d_keys = d_keys + dot_rows(d_scores, query)
        d_gained = rope_back(dot(d_scores, keys) * factor, cos, sin)
        gain_sum = gain_sum + jnp.sum(d_gained * q_hat, axis=0, keepdims=True)
        d_hat = d_gained * query_gain
        d_q = q_inverse * (d_hat - q_hat * jnp.mean(d_hat * q_hat, axis=-1, keepdims=True))
        d_qkv[:rows, span] = d_q.astype(bf16)
    d_gained = rope_back(d_keys, cos, sin)
    key_sum = jnp.sum(d_gained * k_hat, axis=0, keepdims=True)
    split_rows(d_qkv, rows, jnp.concatenate([gain_sum, key_sum], axis=1))
    d_hat = d_gained * key_gain
    d_k = k_inverse * (d_hat - k_hat * jnp.mean(d_hat * k_hat, axis=-1, keepdims=True))
    d_qkv[:rows, group * head : (group + 1) * head] = d_k.astype(bf16)
    d_qkv[:rows, (group + 1) * head :] = d_values.astype(bf16)
    wait_all(far)
    d_normed = dot_cols(d_qkv[:rows], weights[:, :split])
    half = d_own.shape[0]
    d_own[...] = d_normed[:half]
    d_other[...] = d_normed[half:].astype(bf16)


def attend_back(layer, ring, breadth, split, experts, pieces, raw, probs, tiny, tables):
    width = pieces[0].shape[1]
    rows = raw.shape[0]
    small = (*pieces, raw, probs, tiny, tables[0], tables[1])
    shapes = (
        array((rows, width), bf16),
        array((rows + extra_rows, raw.shape[1]), bf16),
        array((rows // 2, width), f32),
        array((rows // 2, width), bf16),
    )
    count = len(ring.pieces)
    return pl.pallas_call(
        functools.partial(attend_back_kernel, ring.plan, ring.rows, layer, split, experts),
        in_specs=[anywhere] * count + [full(one) for one in small],
        out_specs=tuple(full(one) for one in shapes),
        out_shape=shapes,
        scratch_shapes=[pltpu.VMEM((width, breadth), bf16), pltpu.SemaphoreType.DMA((2 * count,))],
        compiler_params=kernel_params(56),
        cost_estimate=cost(12 * rows * width * breadth, 2 * width * breadth),
    )(*ring.pieces, *small)


def choose_weights_kernel(layer, *refs):
    refs, (w_both, w_down, sems) = refs[:6], refs[6:]
    is_own = lax.axis_index("section") == layer
    experts = refs[0].shape[0]
    units = w_down.shape[0] // experts

    def copies(sources):
        made = []
        for number in range(experts):
            gate = pl.ds(2 * number * units, units)
            up = pl.ds((2 * number + 1) * units, units)
            targets = (
                w_both.at[:, gate],
                w_both.at[:, up],
                w_down.at[pl.ds(number * units, units)],
            )
            for i, target in enumerate(targets):
                sem = sems.at[3 * number + i]
                made.append(pltpu.make_async_copy(sources[i].at[number], target, sem))
        return made

    @pl.when(is_own)
    def _():
        start_all(copies(refs[:3]))

    @pl.when(jnp.logical_not(is_own))
    def _():
        start_all(copies(refs[3:]))

    wait_all(copies(refs[:3]))


def choose_weights(layer, weights):
    experts, width, units = weights[0].shape
    total = experts * units
    return pl.pallas_call(
        functools.partial(choose_weights_kernel, layer),
        in_specs=[anywhere] * 6,
        out_specs=(anywhere,) * 2,
        out_shape=(array((width, 2 * total), bf16), array((total, width), bf16)),
        scratch_shapes=[pltpu.SemaphoreType.DMA((3 * experts,))],
        compiler_params=kernel_params(8),
        cost_estimate=cost(1000, 1000),
    )(*weights)


def expert_copies(experts, sources, w_both, w_down, sems):
    units = w_down.shape[0] // experts
    groups = []
    for number in range(experts):
        wide = pl.ds(2 * number * units, 2 * units)
        narrow = pl.ds(number * units, units)
        groups.append(
            (
                pltpu.make_async_copy(
                    sources[0].at[:, wide], w_both.at[:, wide], sems.at[2 * number]
                ),
                pltpu.make_async_copy(
                    sources[1].at[narrow], w_down.at[narrow], sems.at[2 * number + 1]
                ),
            )
        )
    return groups


def load_pieces(pieces, tile, scratch, sems):
    if len(pieces) == 1:
        pieces = [pieces[0].at[pl.ds(tile * tile_rows, tile_rows)]]
    copies, start = [], 0
    for number, piece in enumerate(pieces):
        rows = piece.shape[0]
        target = scratch.at[pl.ds(start, rows)]
        copies.append(pltpu.make_async_copy(piece, target, sems.at[number]))
        start += rows
    start_all(copies)
    return copies


def store_pieces(value, outs, columns):
    start = 0
    for out in outs:
        rows = out.shape[0]
        out[:, columns] = value[start : start + rows]
        start += rows


def experts_kernel(count, layer, tile, before, *refs):
    pieces, refs = refs[:count], refs[count:]
    weight_refs, ones, refs = refs[:2], refs[2], refs[3 + before :]
    outs, refs = refs[:count], refs[count:]
    act_store, gates_out, rows_store, scaled_store = refs[:4]
    rows_in, scaled, w_both, w_down, sems, weight_sems, store_sems, act_out = refs[4:]
    width = w_both.shape[0]
    experts = ones.shape[0]
    units = w_down.shape[0] // experts
    loads = load_pieces(pieces, tile, rows_in, sems)
    weights = expert_copies(experts, weight_refs, w_both, w_down, weight_sems)
    weights[0][0].start()
    place = pl.ds(tile * tile_rows, tile_rows)
    stores = [
        pltpu.make_async_copy(
            rows_in.at[:, pl.ds(0, width)], rows_store.at[place], store_sems.at[0]
        ),
        pltpu.make_async_copy(scaled, scaled_store.at[place], store_sems.at[1]),
        pltpu.make_async_copy(act_out, act_store, store_sems.at[2]),
    ]
    wait_all(loads)
    stores[0].start()
    extra = rows_in[:, width:].astype(f32)
    gates = extra + pltpu.roll(extra, lanes // 2, 1)
    gates_out[...] = gates
    for number in range(experts):
        weights[number][0].wait()
        if number + 1 < experts:
            weights[number + 1][0].start()
        weights[number][1].start()
        span = slice(2 * number * units, 2 * (number + 1) * units)
        act = dot(rows_in[:, :width], w_both[:, span])
        act_out[:, span] = act.astype(act_out.dtype)
        gate_act, up_act = act[:, :units], act[:, units:]
        hidden = (gate_act / (1.0 + jnp.exp(-gate_act)) * up_act).astype(bf16)
        gate = jnp.sum(gates * ones[number : number + 1], axis=1, keepdims=True)
        scaled[:, number * units : (number + 1) * units] = (hidden.astype(f32) * gate).astype(bf16)
    stores[1].start()
    stores[2].start()
    for number in range(experts):
        weights[number][1].wait()
    step = width // 4
    for number in range(4):
        span = slice(number * step, (number + 1) * step)
        store_pieces(dot(scaled[...], w_down[:, span]).astype(bf16), outs, span)
    wait_all(stores)


def expert_scratch(wide, width, total_units, kind, count, experts):
    return [
        pltpu.VMEM((tile_rows, wide), bf16),
        kind,
        pltpu.VMEM((width, 2 * total_units), bf16),
        pltpu.VMEM((total_units, width), bf16),
        pltpu.SemaphoreType.DMA((count,)),
        pltpu.SemaphoreType.DMA((2 * experts,)),
        pltpu.SemaphoreType.DMA((3,)),
    ]


def run_experts(pieces, weights, ones, layer, tile, rows, stores):
    count = len(pieces)
    experts, total_units, width = ones.shape[0], *weights[1].shape
    stores = stores or ()
    sizes = [min(one.shape[0], tile_rows) for one in pieces]
    shapes = tuple([array((one, width), bf16) for one in sizes]) + (
        array((tile_rows, 2 * total_units), f32 if small_grid() else bf16),
        array((tile_rows, lanes), f32),
        array((rows, width), bf16),
        array((rows, total_units), bf16),
    )
    outs = pl.pallas_call(
        functools.partial(experts_kernel, count, layer, tile, len(stores)),
        in_specs=[anywhere] * (count + 2) + [full(ones)] + [anywhere] * len(stores),
        out_specs=tuple(full(one) for one in shapes[:count])
        + (anywhere, full(shapes[count + 1]), anywhere, anywhere),
        out_shape=shapes,
        scratch_shapes=expert_scratch(
            pieces[0].shape[1],
            width,
            total_units,
            pltpu.VMEM((tile_rows, total_units), bf16),
            count,
            experts,
        )
        + [pltpu.VMEM(shapes[count].shape, shapes[count].dtype)],
        input_output_aliases={count + 3: count + 2, count + 4: count + 3} if stores else {},
        compiler_params=kernel_params(32),
        cost_estimate=cost(12 * tile_rows * width * total_units, 6 * width * total_units),
    )(*pieces, *weights, ones, *stores)
    return list(outs[:count]), outs[count : count + 2], outs[count + 2 :]


def experts_back_kernel(count, layer, tile, before, *refs):
    pieces, refs = refs[:count], refs[count:]
    weight_refs, ones, act_in, gates_in = refs[:2], refs[2], refs[3], refs[4]
    refs = refs[5 + before :]
    outs, refs = refs[:count], refs[count:]
    d_store, grad_store = refs[:2]
    rows_in, d_act, w_both, w_down, sems, weight_sems, store_sems, act = refs[2:]
    width = w_both.shape[0]
    experts = ones.shape[0]
    units = w_down.shape[0] // experts
    loads = load_pieces(pieces, tile, rows_in, sems)
    weights = expert_copies(experts, weight_refs, w_both, w_down, weight_sems)
    weights[0][1].start()
    act_copy = pltpu.make_async_copy(act_in, act, store_sems.at[2])
    act_copy.start()
    place = pl.ds(tile * tile_rows, tile_rows)
    stores = [
        pltpu.make_async_copy(rows_in, grad_store.at[place], store_sems.at[0]),
        pltpu.make_async_copy(d_act, d_store.at[place], store_sems.at[1]),
    ]
    wait_all(loads)
    stores[0].start()
    gates = gates_in[...]
    placed = jnp.zeros_like(gates)
    for number in range(experts):
        weights[number][1].wait()
        if number + 1 < experts:
            weights[number + 1][1].start()
        weights[number][0].start()
        base = 2 * number * units
        plain = dot_cols(rows_in[...], w_down[number * units : (number + 1) * units])
        if number == 0:
            act_copy.wait()
        one = ones[number : number + 1]
        gate = jnp.sum(gates * one, axis=1, keepdims=True)
        gate_act = act[:, base : base + units].astype(f32)
        up_act = act[:, base + units : base + 2 * units].astype(f32)
        sigmoid = 1.0 / (1.0 + jnp.exp(-gate_act))
        silu = gate_act * sigmoid
        hidden = (silu * up_act).astype(bf16).astype(f32)
        placed = placed + jnp.sum(plain * hidden, axis=1, keepdims=True) * one
        d_hidden = plain * gate
        d_act[:, base + units : base + 2 * units] = (d_hidden * silu).astype(bf16)
        d_gate = d_hidden * up_act * (sigmoid + silu * (1.0 - sigmoid))
        d_act[:, base : base + units] = d_gate.astype(bf16)
    stores[1].start()
    for number in range(experts):
        weights[number][0].wait()
    step = width // 4
    for number in range(4):
        span = slice(number * step, (number + 1) * step)
        store_pieces(dot_cols(d_act[...], w_both[span]).astype(bf16), outs, span)
    store_pieces(placed.astype(bf16), outs, slice(width, width + lanes))
    wait_all(stores)


def run_experts_back(pieces, weights, ones, kept, layer, tile, rows, stores):
    count = len(pieces)
    experts, total_units, width = ones.shape[0], *weights[1].shape
    stores = stores or ()
    act, gates = kept
    sizes = [min(one.shape[0], tile_rows) for one in pieces]
    shapes = tuple([array((one, width + lanes), bf16) for one in sizes]) + (
        array((rows, 2 * total_units), bf16),
        array((rows, width), bf16),
    )
    outs = pl.pallas_call(
        functools.partial(experts_back_kernel, count, layer, tile, len(stores)),
        in_specs=[anywhere] * (count + 2)
        + [full(ones), anywhere, full(gates)]
        + [anywhere] * len(stores),
        out_specs=tuple(full(one) for one in shapes[:count]) + (anywhere,) * 2,
        out_shape=shapes,
        scratch_shapes=expert_scratch(
            width,
            width,
            total_units,
            pltpu.VMEM((tile_rows, 2 * total_units), bf16),
            count,
            experts,
        )
        + [pltpu.VMEM(act.shape, act.dtype)],
        input_output_aliases={count + 5: count, count + 6: count + 1} if stores else {},
        compiler_params=kernel_params(32),
        cost_estimate=cost(12 * tile_rows * width * total_units, 6 * width * total_units),
    )(*pieces, *weights, ones, act, gates, *stores)
    return list(outs[:count]), outs[count:]


def grads_kernel(column, before, count, *refs):
    sources, refs = refs[:8], refs[8 + before :]
    outs, (left, right, result, sems, out_sems) = refs[:count], refs[count:]
    core = lax.axis_index("section")
    rows = left.shape[0] // 2
    place, step = column
    spans = [pl.ds(0, left.shape[1]), pl.ds(0, right.shape[1])]
    spans[place] = pl.ds(step * grad_columns, grad_columns)

    def copies(layer):
        made = []
        for number, target in enumerate((left, right)):
            for got in range(2):
                source = sources[4 * number + 2 * got + layer]
                made.append(
                    pltpu.make_async_copy(
                        source.at[:, spans[number]],
                        target.at[pl.ds(got * rows, rows)],
                        sems.at[2 * number + got],
                    )
                )
        return made

    for layer in range(2):

        @pl.when(core == layer)
        def _():
            start_all(copies(layer))

    wait_all(copies(0))
    experts = outs[0].shape[0]
    units = result.shape[1 - place] // (experts * count)
    result[...] = dot_rows(left[...], right[...])
    stores = []
    for expert in range(experts):
        for number, out in enumerate(outs):
            start = (expert * len(outs) + number) * units
            if place == 0:
                source = result.at[:, pl.ds(start, units)]
                target = out.at[expert, spans[0]]
            else:
                source = result.at[pl.ds(start, units)]
                target = out.at[expert, :, spans[1]]
            stores.append(pltpu.make_async_copy(source, target, out_sems.at[len(stores)]))
    start_all(stores)
    wait_all(stores)


def run_grads(place, step, left, right, shapes, before):
    before = before or ()
    rows = left[0].shape[0]
    widths = [left[0].shape[1], right[0].shape[1]]
    widths[place] = grad_columns
    experts = shapes[0].shape[0]
    return pl.pallas_call(
        functools.partial(grads_kernel, (place, step), len(before), len(shapes)),
        in_specs=[anywhere] * (8 + len(before)),
        out_specs=(anywhere,) * len(shapes),
        out_shape=shapes,
        scratch_shapes=[
            pltpu.VMEM((2 * rows, widths[0]), bf16),
            pltpu.VMEM((2 * rows, widths[1]), bf16),
            pltpu.VMEM((widths[0], widths[1]), f32),
            pltpu.SemaphoreType.DMA((4,)),
            pltpu.SemaphoreType.DMA((experts * len(shapes),)),
        ],
        input_output_aliases={8 + i: i for i in range(len(before))},
        compiler_params=kernel_params(56),
        cost_estimate=cost(10**8, 10**5),
    )(*left, *right, *before)


def wide_grads(experts, rows_in, d_act):
    width, units = rows_in[0].shape[1], d_act[0].shape[1] // (2 * experts)
    shapes = (array((experts, width, units), f32),) * 2
    made = []
    for step in range(width // grad_columns):
        made.append(run_grads(0, step, rows_in, d_act, shapes, made[-1] if made else None))
    return made


def down_grads(experts, scaled, grads):
    width, units = grads[0].shape[1], scaled[0].shape[1] // experts
    shapes = (array((experts, units, width), f32),)
    made = []
    for step in range(width // grad_columns):
        made.append(run_grads(1, step, scaled, grads, shapes, made[-1] if made else None))
    return made


def out_grads_kernel(plan, rows, *refs):
    count = len(plan)
    pieces, (spread, g_out, mixed, d_cols, sems) = refs[:count], refs[count:]
    copies = copy_pieces(pieces, plan, rows, pl.ds(0, mixed.shape[1]), mixed, sems)
    copies.append(pltpu.make_async_copy(spread.at[:, pl.ds(0, rows)], d_cols, sems.at[count]))
    start_all(copies)
    wait_all(copies)
    g_out[...] = dot_rows(mixed[...], d_cols[...].reshape(mixed.shape[0], d_cols.shape[2]))


def out_grads(ring, spread):
    blocks, _, columns = spread.shape
    breadth = ring.shard.shape[1]
    count = len(ring.pieces)
    shape = array((breadth, columns), f32)
    total = blocks * ring.rows
    return pl.pallas_call(
        functools.partial(out_grads_kernel, ring.plan, ring.rows),
        in_specs=[anywhere] * (count + 1),
        out_specs=full(shape),
        out_shape=shape,
        scratch_shapes=[
            pltpu.VMEM((total, breadth), bf16),
            pltpu.VMEM((blocks, ring.rows, columns), bf16),
            pltpu.SemaphoreType.DMA((count + 1,)),
        ],
        compiler_params=kernel_params(56),
        cost_estimate=cost(10**8, 10**5),
    )(*ring.pieces, spread)


def stack_layer_kernel(sums, zero, one, got, out):
    core = lax.axis_index("section")
    columns = zero.shape[1]
    rows = zero.shape[0] - (extra_rows if sums else 0)
    half = rows // 2
    for number, own in ((0, zero), (1, one)):

        @pl.when(core == number)
        def _():
            here = slice(number * columns, (number + 1) * columns)
            there = slice((1 - number) * columns, (2 - number) * columns)
            out[:rows, here] = own[:rows]
            out[:half, there] = got[half:rows]
            out[half:rows, there] = got[:half]
            if sums:
                total = joined_rows(own, rows, sums) + joined_rows(got, rows, sums)
                split_rows(out, rows, total)


def stack_layer(zero, one, got, sums=0):
    rows, columns = zero.shape
    kernel = functools.partial(stack_layer_kernel, sums)
    return simple(kernel, [array((rows, 2 * columns), zero.dtype)], zero, one, got)[0]


def projection_grads_kernel(plan, rows, *refs):
    count = len(plan)
    pieces, (spread, late_spread, w_query, w_key, w_value), refs = (
        refs[:count],
        refs[count : count + 5],
        refs[count + 5 :],
    )
    g_query, g_key, g_value, late, d_qkv, normed, parts, sems = refs
    tokens = rows - extra_rows
    copies = copy_pieces(pieces, plan, rows, pl.ds(0, d_qkv.shape[1]), d_qkv, sems)
    target = normed.at[:, pl.ds(0, tokens)]
    copies.append(pltpu.make_async_copy(spread, target, sems.at[count]))
    source = late_spread.at[:, pl.ds(tokens, parts.shape[1])]
    copies.append(pltpu.make_async_copy(source, parts, sems.at[count + 1]))
    start_all(copies)
    blocks, _, part = normed.shape
    normed[:, tokens:] = jnp.zeros((blocks, extra_rows, part), bf16)
    wait_all(copies)
    wide = g_query.shape[1] // 2
    head = g_key.shape[1] // 2
    both = dot_rows(normed[...].reshape(blocks * rows, part), d_qkv[...])
    for side in range(2):
        start = side * (wide + 2 * head)
        g_query[:, side * wide : (side + 1) * wide] = both[:, start : start + wide]
        g_key[:, side * head : (side + 1) * head] = both[:, start + wide : start + wide + head]
        g_value[:, side * head : (side + 1) * head] = both[
            :, start + wide + head : start + wide + 2 * head
        ]
    products = (
        jnp.sum(w_query[...].astype(f32) * g_query[...], axis=1, keepdims=True)
        + jnp.sum(w_key[...].astype(f32) * g_key[...], axis=1, keepdims=True)
        + jnp.sum(w_value[...].astype(f32) * g_value[...], axis=1, keepdims=True)
    )
    heads = jnp.zeros((1, 2 * head), f32)
    for block in range(blocks):
        heads = heads + joined_rows(d_qkv, block * rows + tokens, 2 * head)
    late[...] = jnp.zeros_like(late)
    late[8:, :part] = jnp.sum(parts[...].astype(f32), axis=0)
    late[:1, :part] = jnp.transpose(jnp.broadcast_to(products, (part, lanes)))[:1]
    late[1:2, : 2 * head] = heads


def projection_grads(ring, spread, late_spread, weights, head):
    blocks, tokens, part = spread.shape
    size = late_spread.shape[1] - tokens
    breadth = ring.shard.shape[1]
    wide = breadth // 2 - 2 * head
    count = len(ring.pieces)
    total = blocks * ring.rows
    shapes = (
        array((part, 2 * wide), f32),
        array((part, 2 * head), f32),
        array((part, 2 * head), f32),
        array((8 + size, max(part, 2 * head)), f32),
    )
    return pl.pallas_call(
        functools.partial(projection_grads_kernel, ring.plan, ring.rows),
        in_specs=[anywhere] * (count + 2) + [full(one) for one in weights],
        out_specs=tuple(full(one) for one in shapes),
        out_shape=shapes,
        scratch_shapes=[
            pltpu.VMEM((total, breadth), bf16),
            pltpu.VMEM((blocks, ring.rows, part), bf16),
            pltpu.VMEM((blocks, size, part), bf16),
            pltpu.SemaphoreType.DMA((count + 2,)),
        ],
        compiler_params=kernel_params(56),
        cost_estimate=cost(20 * total * part * breadth, 4 * total * breadth),
    )(*ring.pieces, spread, late_spread, *weights)


def both_rows(shard):
    far = swap_x(shard)
    return (shard, far, swap_core(shard), swap_core(far))


def merge_kernel(own, got, kept, given):
    block = own[...] + got[...].astype(f32)
    half = kept.shape[0]
    kept[...] = block[:half]
    given[...] = block[half:].astype(bf16)


def own_rows(own, other):
    rows, width = own.shape
    shapes = [array((rows // 2, width), kind) for kind in (f32, bf16)]
    kept, given = simple(merge_kernel, shapes, own, swap_core(other))
    return kept, swap_x(given)


def route_kernel(layer, x, kept, got, tiny, mask, mid_out, payload, gates_out):
    experts = mask.shape[1]
    width = x.shape[1]
    start = layer * (experts + 4)
    mid = x[...] + kept[...] + got[...].astype(f32)
    mid_out[...] = mid
    gain = tiny[start + experts + 1 : start + experts + 2]
    normed = (mid * inverse_rms(mid) * gain).astype(bf16)
    payload[:, :width] = normed
    logits = dot_cols(normed, tiny[start : start + experts].astype(bf16))
    logits = jnp.where(mask[...] > 0.0, logits, masked_score)
    weights = jnp.exp(logits - jnp.max(logits, axis=-1, keepdims=True))
    gates = weights / jnp.sum(weights, axis=-1, keepdims=True)
    gates_out[...] = gates
    high = gates.astype(bf16)
    low = (gates - high.astype(f32)).astype(bf16)
    payload[:, width:] = jnp.zeros((x.shape[0], lanes), bf16)
    payload[:, width : width + experts] = high
    payload[:, width + lanes // 2 : width + lanes // 2 + experts] = low


def route(layer, x, kept, got, tiny, mask):
    rows, width = x.shape
    shapes = [
        array((rows, width), f32),
        array((rows, width + lanes), bf16),
        array(mask.shape, f32),
    ]
    kernel = functools.partial(route_kernel, layer)
    return simple(kernel, shapes, x, kept, got, tiny, mask)


def sum_parts(parts):
    total = parts[0][...]
    for one in parts[1:]:
        total = total + one[...].astype(f32)
    return total


def enter_kernel(count, experts, mid, *refs):
    parts, (tiny, x_out, normed) = refs[:count], refs[count:]
    x = (mid[...] + sum_parts(parts)).astype(bf16).astype(f32)
    x_out[...] = x
    row = 2 * experts + 4
    normed[...] = (x * inverse_rms(x) * tiny[row : row + 1]).astype(bf16)


def enter(mid, parts, tiny, experts):
    shapes = [array(mid.shape, f32), array(mid.shape, bf16)]
    kernel = functools.partial(enter_kernel, len(parts), experts)
    return simple(kernel, shapes, mid, *parts, tiny)


def finish_kernel(mid, *refs):
    refs[-1][...] = (mid[...] + sum_parts(refs[:-1])).astype(bf16)


def finish(mid, parts):
    return simple(finish_kernel, [array(mid.shape, bf16)], mid, *parts)[0]


def norm_back(value, gain, grad):
    inverse = inverse_rms(value)
    hat = value * inverse
    d_hat = grad * gain
    d_value = inverse * (d_hat - hat * jnp.mean(d_hat * hat, axis=-1, keepdims=True))
    return d_value, jnp.sum(grad * hat, axis=0, keepdims=True)


def unroute_kernel(count, layer, *refs):
    parts, refs = refs[:count], refs[count:]
    grad, mid, tiny, gates_in, payload, d_out, d_low, g_router, g_gain = refs
    width = mid.shape[1]
    experts = gates_in.shape[1]
    start = layer * (experts + 4)
    back = sum_parts(parts)
    gates = gates_in[...]
    gate_grad = back[:, width : width + experts]
    d_logits = gates * (gate_grad - jnp.sum(gates * gate_grad, axis=-1, keepdims=True))
    d_logits = d_logits.astype(bf16)
    d_normed = back[:, :width] + dot(d_logits, tiny[start : start + experts].astype(bf16))
    gain = tiny[start + experts + 1 : start + experts + 2]
    d_mid, gain_sum = norm_back(mid[...], gain, d_normed)
    d_mid = d_mid + grad[...].astype(f32)
    d_out[...] = d_mid
    d_low[...] = d_mid.astype(bf16)
    g_router[...] = dot_rows(d_logits, payload[:, :width])
    g_gain[...] = gain_sum


def unroute(layer, parts, grad, mid, tiny, gates, payload):
    width, experts = mid.shape[1], gates.shape[1]
    shapes = [
        array(mid.shape, f32),
        array(mid.shape, bf16),
        array((experts, width), f32),
        array((1, width), f32),
    ]
    kernel = functools.partial(unroute_kernel, len(parts), layer)
    return simple(kernel, shapes, *parts, grad, mid, tiny, gates, payload)


def leave_kernel(row, kept, got, x, d_mid, tiny, d_out):
    d_normed = kept[...] + got[...].astype(f32)
    d_x, _ = norm_back(x[...], tiny[row : row + 1], d_normed)
    d_out[...] = (d_mid[...] + d_x).astype(bf16)


def leave(layer, experts, kept, got, x, d_mid, tiny):
    kernel = functools.partial(leave_kernel, layer * (experts + 4) + experts)
    return simple(kernel, [array(x.shape, bf16)], kept, got, x, d_mid, tiny)[0]


def count_rows(tiles):
    return max(tile_rows, tiles[0][0].shape[0])


def apply_experts(tiles, weights, ones, layer):
    kept, outs, stores = [], [], None
    for number, pieces in enumerate(tiles):
        out, saved, stores = run_experts(
            pieces, weights, ones, layer, number, count_rows(tiles), stores
        )
        outs.append(out)
        kept.append(saved)
    return outs, kept, stores


def apply_experts_back(tiles, weights, ones, kept, layer):
    backs, stores = [], None
    for number, (pieces, saved) in enumerate(zip(tiles, kept)):
        back, stores = run_experts_back(
            pieces, weights, ones, saved, layer, number, count_rows(tiles), stores
        )
        backs.append(back)
    return backs, stores


def choose_kernel(zero, one, out):
    core = lax.axis_index("section")
    for number, own in enumerate((zero, one)):

        @pl.when(core == number)
        def _():
            out[: own.shape[0]] = own[...]


def small_kernel(router0, gain0, router1, gain1, own, other):
    core = lax.axis_index("section")
    layers = ((router0, gain0), (router1, gain1))
    experts = router0.shape[0]
    for number in range(2):

        @pl.when(core == number)
        def _():
            for out, layer in ((own, number), (other, 1 - number)):
                router, gain = layers[layer]
                out[...] = jnp.zeros_like(out)
                out[:experts] = router[...]
                out[experts : experts + 1] = gain[...]


def late_kernel(zero, one, own, got, out):
    rows = zero.shape[0]
    choose_kernel(zero, one, out)
    out[rows:] = (own[...] + got[...]).astype(bf16)


def other_layer_kernel(zero, one, out, sem):
    core = lax.axis_index("section")
    for number, source in enumerate((one, zero)):

        @pl.when(core == number)
        def _():
            pltpu.make_async_copy(source, out, sem).start()

    pltpu.make_async_copy(zero, out, sem).wait()


def exchange(zero, one):
    sent = pl.pallas_call(
        other_layer_kernel,
        in_specs=[anywhere] * 2,
        out_specs=anywhere,
        out_shape=array(zero.shape, zero.dtype),
        scratch_shapes=[pltpu.SemaphoreType.DMA],
        compiler_params=kernel_params(8),
        cost_estimate=cost(1000, 1000),
    )(zero, one)
    got = swap_core(sent)
    return zero, one, got, got


def by_columns(value, split):
    columns = value.shape[1] // split
    return jnp.stack([value[:, i * columns : (i + 1) * columns] for i in range(split)])


def to_owners(blocks):
    return lax.all_to_all(blocks, "expert", split_axis=0, concat_axis=0, tiled=True)


def body(
    ends_in,
    attn_gain,
    w_query,
    key_matrix,
    value_matrix,
    query_gain,
    key_gain,
    w_out,
    ffn_gain,
    router,
    w_gate,
    w_up,
    w_down,
    routes,
    lengths,
):
    core = lax.axis_index("section")
    first = core == 0
    side = lax.axis_index("tensor")
    index = lax.axis_index("expert")
    split = lax.axis_size("expert")
    rows, width = ends_in.shape[2:]
    half = rows // 2
    experts = router.shape[2]
    head = query_gain.shape[1] * split

    def pick(zero, one):
        return jnp.where(first, zero, one)

    def mine(pair):
        return pick(pair[0], pair[1])

    def theirs(pair):
        return pick(pair[1], pair[0])

    def by_layer(own):
        got = swap_core(own)
        return pick(own, got), pick(got, own)

    def pick_side(zero, one):
        return jnp.where(side == 0, zero, one)

    def half_rows(block):
        return pick_side(block[:half], block[half:])

    def side_first(block):
        return pick_side(block, cat(block[half:], block[:half]))

    part = w_query.shape[1]
    columns = w_query.shape[2] // 2
    transposed = w_out[0].T
    groups = [
        cat(
            w_query[0][:, g * columns : (g + 1) * columns],
            key_matrix[0][:, g * head : (g + 1) * head],
            value_matrix[0][:, g * head : (g + 1) * head],
            transposed[:, g * columns : (g + 1) * columns],
            axis=1,
        )
        for g in range(2)
    ]
    kept, got = mine(groups), swap_core(theirs(groups))
    breadth = kept.shape[1]

    share = head // split
    gains = cat(query_gain[0][:, None], key_gain[0][:, None], axis=1)
    tiny = cat(
        router[0],
        attn_gain[0][:, None],
        ffn_gain[0][:, None],
        jnp.pad(gains, ((0, part - share), (0, 0))),
        axis=1,
    )
    size = tiny.shape[1]
    tiny = cat(*by_layer(tiny), axis=1)
    tiny = jnp.pad(tiny, ((0, 0), (0, -2 * size % lanes)))
    ring0 = Ring(cat(pick(kept, got), tiny, axis=1))
    ring1 = Ring(pick(got, kept))
    started = ring0.advance()

    ends_in, w_gate, w_up, w_down = lax.optimization_barrier(
        (ends_in, w_gate, w_up, w_down, *started)
    )[:4]
    own_weights = (w_gate[0], w_up[0], w_down[0])
    expert_weights = own_weights + tuple(swap_core(one) for one in own_weights)
    crossed = swap_core(ends_in[0])
    x_all, grad_all = pick(ends_in[0], crossed), pick(crossed, ends_in[0])
    x_own = mine(x_all)
    x_in = half_rows(x_own).astype(f32)
    grad_last = half_rows(mine(grad_all))
    x_both = cat(side_first(x_own), side_first(theirs(x_all))).astype(f32)
    x_hat = x_both * inverse_rms(x_both)

    routes, lengths = lax.optimization_barrier((routes, lengths, *ring0.advance()))[:2]
    routes_crossed = swap_core(pick(routes[0, 1], routes[0, 0]))
    routes_own = [pick(routes[0, 0], routes_crossed), pick(routes_crossed, routes[0, 1])]
    expert_ids = jnp.arange(experts, dtype=jnp.int32)
    masks = [
        jnp.any(half_rows(r)[:, :, None] == expert_ids[None, None, :], axis=1).astype(f32)
        for r in routes_own
    ]
    per_device = w_gate.shape[1]
    lane_ids = jnp.arange(lanes, dtype=jnp.int32)
    local_ids = index * per_device + jnp.arange(per_device, dtype=jnp.int32)
    ones = (lane_ids[None, :] == local_ids[:, None]).astype(f32)
    row_index = (jnp.arange(rows, dtype=jnp.int32) + side * half) % rows
    length_pair = [pick(lengths[0, 0], lengths[1, 0]), pick(lengths[1, 0], lengths[0, 0])]
    tables = make_tables(length_pair, row_index, head)

    ring0.advance()
    ring0.advance()
    ring1.advance(*ring0.latest)

    tiny, normed0, mixed0, raw0, probs0, own, other = attend(
        0, ring0, breadth, split, experts, (x_hat,), tables
    )
    other = after(other, *ring1.latest)
    mid0, payload0, gates0 = route(0, x_in, *own_rows(own, other), tiny, masks[0])
    gather = Gather(payload0)
    gather.along_z()
    weights0 = choose_weights(0, (after(expert_weights[0], payload0), *expert_weights[1:]))
    gather.near(*weights0)
    gather.far()
    tiles = gather.tiles()
    ring1.advance(tiles[-1][-1])
    outs0, kept0, stores0 = apply_experts(tiles, weights0, ones, 0)
    scatter = Scatter(outs0)
    scatter.far()
    scatter.near(beside=ring1.latest)
    parts = scatter.along_z()
    ring1.advance(*parts)
    ring1.advance()
    x_mid, shard = enter(mid0, parts, tiny, experts)

    normed_pieces = both_rows(shard)
    grad_gather = Gather(grad_last)
    along = grad_gather.along_z(normed_pieces[-1])
    normed1, mixed1, raw1, probs1, own, other = attend(
        1, ring1, breadth, split, experts, (*normed_pieces, tiny), tables
    )
    other = after(other, *along)
    beside = grad_gather.near(own)
    mid1, payload1, gates1 = route(1, x_mid, *own_rows(own, other), tiny, masks[1])
    gather = Gather(after(payload1, *beside))
    gather.along_z()
    weights1 = choose_weights(1, (after(expert_weights[0], payload1), *expert_weights[1:]))
    gather.near(*weights1)
    gather.far()
    tiles = gather.tiles()
    beside = grad_gather.far(tiles[-1][-1])
    mixed_got = swap_core(pick(mixed1, mixed0))
    ring_mixed = Ring(stack_layer(mixed0, mixed1, mixed_got))
    ring_mixed.advance(tiles[-1][-1])
    outs1, kept1, stores1 = apply_experts(tiles, weights1, ones, 1)

    outs1[-1][-1] = after(outs1[-1][-1], *ring_mixed.latest, *beside)
    tiles = grad_gather.tiles(outs1[-1][-1])
    ring_mixed.advance(tiles[-1][-1])
    backs, back_stores1 = apply_experts_back(tiles, weights1, ones, kept1, 1)
    scatter = Scatter(backs)
    scatter.far(*ring_mixed.latest)
    reached = scatter.near()
    out_scatter = Scatter(outs1)
    beside = out_scatter.far(*reached)
    parts = scatter.along_z()
    parts[-1] = after(parts[-1], *beside)
    d_mid, d_low, g_router1, g_ffn_gain1 = unroute(
        1, parts, grad_last, mid1, tiny, gates1, payload1
    )
    d_pieces = both_rows(d_low)
    ring_mixed.advance(d_pieces[-1])

    if small_grid():
        rows_in = exchange(after(stores0[0], d_pieces[-1]), stores1[0])
        early = (rows_in[2],)
    else:
        early = ()
    d_attn1, d_qkv1, d_own, d_other = attend_back(
        1, ring1, breadth, split, experts, d_pieces, raw1, probs1, tiny, tables
    )
    d_other = after(d_other, *ring_mixed.latest, *early)
    d_one = leave(1, experts, *own_rows(d_own, d_other), x_mid, d_mid, tiny)

    gather = Gather(d_one)
    gather.along_z()
    beside = out_scatter.near(d_one)
    weights0 = choose_weights(0, (after(expert_weights[0], d_one), *expert_weights[1:]))
    gather.near(*beside, *weights0)
    gather.far()
    tiles = gather.tiles()
    backs, back_stores0 = apply_experts_back(tiles, weights0, ones, kept0, 0)

    if not small_grid():
        rows_in = exchange(after(stores0[0], back_stores0[0]), stores1[0])
    d_act = exchange(after(back_stores0[0], rows_in[2]), back_stores1[0])
    wide = wide_grads(per_device, rows_in, d_act)
    scatter = Scatter(backs)
    normed_own = simple(
        choose_kernel, [array(normed0.shape, bf16)], normed0, after(normed1, *scatter.far())
    )[0]
    normed_blocks = by_columns(normed_own, split)
    scatter.near(beside=(*wide[0], normed_blocks))
    parts = scatter.along_z()
    parts[-1] = after(parts[-1], *wide[1])
    d_mid, d_low, g_router0, g_ffn_gain0 = unroute(
        0, parts, d_one, mid0, tiny, gates0, payload0
    )
    d_pieces = both_rows(d_low)
    normed_spread = to_owners(after(normed_blocks, d_pieces[-1]))
    out_parts = out_scatter.along_z(d_pieces[-1])
    d_attn0, d_qkv0, d_own, d_other = attend_back(
        0, ring0, breadth, split, experts, d_pieces, raw0, probs0, tiny, tables
    )

    qkv_got = swap_core(pick(d_qkv1, after(d_qkv0, normed_spread, *out_parts)))
    ring_d = Ring(stack_layer(d_qkv0, d_qkv1, qkv_got, 2 * head))
    one_round = ring_d.advance()
    d_other = after(d_other, ring_d.shard)
    d_zero = leave(0, experts, *own_rows(d_own, d_other), x_in, d_mid, tiny)
    scaled = exchange(after(stores0[1], ring_d.shard), stores1[1])
    gate = ring_d.shard if small_grid() else scaled[2]
    late = (scaled, exchange(after(back_stores0[1], gate), back_stores1[1]))
    down = down_grads(per_device, *late)
    ring_d.advance()
    rows_small = -(-(experts + 1) // 16) * 16
    small_own, small_other = simple(
        small_kernel,
        [array((rows_small, width), f32)] * 2,
        after(g_router0, *one_round),
        g_ffn_gain0,
        g_router1,
        g_ffn_gain1,
    )
    late_rows = simple(
        late_kernel,
        [array((2 * rows + rows_small, width), bf16)],
        d_attn0,
        d_attn1,
        small_own,
        swap_core(small_other),
    )[0]
    late_spread = to_owners(by_columns(late_rows, split))
    three_rounds = ring_d.advance(*down[0])
    ring_d.advance(*down[1])
    ring_mixed.advance(*three_rounds)
    g_out = out_grads(ring_mixed, late_spread)
    out1 = finish(mid1, out_parts)
    end_own = pick(d_zero, out1)
    end_got = swap_core(pick(out1, d_zero))
    projections = (w_query[0], key_matrix[0], value_matrix[0])
    g_query, g_key, g_value, late = projection_grads(
        ring_d, normed_spread, after(late_spread, *ring_mixed.latest), projections, head
    )
    (g_gate, g_up), (g_down,) = wide[-1], down[-1]

    small = late + swap_x(late)
    g_attn_gain = small[0, :part] / attn_gain[0].astype(f32)
    g_query_gain = lax.dynamic_slice(small[1], (index * share,), (share,))
    g_key_gain = lax.dynamic_slice(small[1], (head + index * share,), (share,))
    g_router = small[8 : 8 + experts, :part].T
    g_ffn_gain = small[8 + experts, :part]

    ends = jnp.stack([pick(end_own, end_got), pick(end_got, end_own)])
    ends_far = swap_x(ends)
    ends_out = cat(pick_side(ends, ends_far), pick_side(ends_far, ends), axis=1)

    outs = (
        ends_out,
        g_attn_gain,
        g_query,
        g_key,
        g_value,
        g_query_gain,
        g_key_gain,
        g_out,
        g_ffn_gain,
        g_router,
        g_gate,
        g_up,
        g_down,
    )
    return tuple(one[None] for one in outs)


def solution(mesh):
    return jax.shard_map(
        body,
        mesh=mesh,
        in_specs=(
            P("section", None, "expert", None),
            P("section", "expert"),
            P("section", "expert", "tensor"),
            P("section", "expert", "tensor"),
            P("section", "expert", "tensor"),
            P("section", "expert"),
            P("section", "expert"),
            P("section", "tensor", "expert"),
            P("section", "expert"),
            P("section", "expert", None),
            P("section", "expert", None, "tensor"),
            P("section", "expert", None, "tensor"),
            P("section", "expert", "tensor", None),
            P("section", None, "expert", None),
            P(None, "expert", None),
        ),
        out_specs=(
            P("section", None, "expert", None),
            P("section", "expert"),
            P("section", "expert", "tensor"),
            P("section", "expert", "tensor"),
            P("section", "expert", "tensor"),
            P("section", "expert"),
            P("section", "expert"),
            P("section", "tensor", "expert"),
            P("section", "expert"),
            P("section", "expert", None),
            P("section", "expert", None, "tensor"),
            P("section", "expert", None, "tensor"),
            P("section", "expert", "tensor", None),
        ),
        check_vma=False,
    )
```

```python
import functools

import jax
import jax.numpy as jnp
import numpy as np
from jax import lax
from jax.experimental import pallas as pl
from jax.experimental.pallas import tpu as pltpu
from jax.sharding import PartitionSpec as P

epsilon = 1e-06
rope_base = 1000000.0
masked_score = -1e30
bf16 = jnp.bfloat16
f32 = jnp.float32
lanes = 128
tile_rows = 512
grad_columns = 1024


def dot(left, right):
    return jnp.dot(left, right, preferred_element_type=f32)


def dot_rows(left, right):
    return lax.dot_general(left, right, (((0,), (0,)), ((), ())), preferred_element_type=f32)


def dot_cols(left, right):
    return lax.dot_general(left, right, (((1,), (1,)), ((), ())), preferred_element_type=f32)


def cat(*pieces, axis=0):
    return jnp.concatenate(pieces, axis=axis)


def swap_core(value):
    return lax.ppermute(value, "section", [(0, 1), (1, 0)])


def swap_x(value):
    return lax.ppermute(value, "tensor", [(0, 1), (1, 0)])


def swap_e(value, bits):
    count = lax.axis_size("expert")
    return lax.ppermute(value, "expert", [(i, i ^ bits) for i in range(count)])


def small_grid():
    return lax.axis_size("expert") == 8


def after(value, *others):
    return lax.optimization_barrier((value, *others))[0] if others else value


anywhere = pl.BlockSpec(memory_space=pl.ANY)


def full(one):
    return pl.BlockSpec(one.shape, lambda *_: (0,) * len(one.shape))


def array(shape, kind):
    return jax.ShapeDtypeStruct(shape, kind)


def kernel_params(megabytes):
    return pltpu.CompilerParams(vmem_limit_bytes=megabytes * 2**20)


def cost(flops, moved):
    return pl.CostEstimate(flops=flops, bytes_accessed=moved, transcendentals=0)


def simple(kernel, shapes, *operands):
    return pl.pallas_call(
        kernel,
        in_specs=[full(one) for one in operands],
        out_specs=tuple(full(one) for one in shapes),
        out_shape=tuple(shapes),
        compiler_params=kernel_params(16),
        cost_estimate=cost(1000, 1000),
    )(*operands)


def stack_kernel(*refs):
    start = 0
    for ref in refs[:-1]:
        refs[-1][start : start + ref.shape[0]] = ref[...]
        start += ref.shape[0]


def stack(*pieces):
    rows = sum(one.shape[0] for one in pieces)
    return simple(stack_kernel, [array((rows, pieces[0].shape[1]), pieces[0].dtype)], *pieces)[0]


def near_kernel(to_x, top, to_y, bottom, out_x, out_y):
    half = top.shape[0]
    out_x[:half] = (to_x[:half].astype(f32) + top[...].astype(f32)).astype(bf16)
    out_x[half:] = to_x[half:]
    out_y[:half] = to_y[:half]
    out_y[half:] = (to_y[half:].astype(f32) + bottom[...].astype(f32)).astype(bf16)


def total_kernel(own, from_x, from_y, kept, *blocks):
    total = own[...].astype(f32) + from_x[...].astype(f32) + from_y[...].astype(f32)
    step = kept.shape[0]
    kept[...] = total[:step]
    for number, block in enumerate(blocks):
        block[...] = total[(number + 1) * step : (number + 2) * step].astype(bf16)


class Gather:
    def __init__(self, shard):
        self.shard = shard
        self.small = small_grid()

    def along_z(self, *gate):
        if self.small:
            shard = after(self.shard, *gate)
            self.line = (shard, swap_e(shard, 2), swap_e(shard, 4), swap_e(shard, 6))
            return self.line[1:]
        return ()

    def near(self, *gate):
        if self.small:
            own = after(stack(*self.line), *gate)
            self.near_pieces = (own, swap_x(own), swap_e(own, 1))
            return self.near_pieces[1:]
        return ()

    def far(self, *gate):
        if self.small:
            own, from_x, from_y = self.near_pieces
            half = own.shape[0] // 2
            self.far_pieces = (
                swap_e(after(from_x[:half], *gate), 1),
                swap_x(after(from_y[half:], *gate)),
            )
            return self.far_pieces
        shard = after(self.shard, *gate)
        self.whole = lax.all_gather(shard, ("expert", "tensor"), axis=0, tiled=True)
        return (self.whole,)

    def tiles(self, *gate):
        if self.small:
            top, bottom = self.far_pieces
            return [[*self.near_pieces, top, after(bottom, *gate)]]
        whole = after(self.whole, *gate)
        return [[whole]] * (whole.shape[0] // tile_rows)


class Scatter:
    def __init__(self, tiles):
        self.tiles = tiles
        self.small = small_grid()

    def far(self, *gate):
        if self.small:
            far_top, far_bottom = self.tiles[0][3:]
            self.top = swap_e(after(far_top, *gate), 1)
            self.bottom = swap_x(after(far_bottom, *gate))
            return (self.top, self.bottom)
        return ()

    def near(self, *gate, beside=()):
        if self.small:
            own, to_x, to_y = self.tiles[0][:3]
            shape = array(to_x.shape, bf16)
            to_x, to_y = simple(near_kernel, [shape] * 2, to_x, self.top, to_y, self.bottom)
            from_x, from_y = swap_x(after(to_x, *gate)), swap_e(after(to_y, *gate), 1)
            from_x = after(from_x, *beside)
            rows, columns = own.shape
            shapes = [array((rows // 4, columns), kind) for kind in (f32, bf16, bf16, bf16)]
            self.blocks = simple(total_kernel, shapes, own, from_x, from_y)
            return self.blocks[:1]
        return ()

    def along_z(self, *gate):
        if self.small:
            kept, *blocks = self.blocks
            moved = [swap_e(after(one, *gate), bits) for one, bits in zip(blocks, (2, 4, 6))]
            return [kept, *moved]
        whole = cat(*[one for pieces in self.tiles for one in pieces])
        whole = after(whole, *gate).astype(f32)
        return [lax.psum_scatter(whole, ("expert", "tensor"), scatter_dimension=0, tiled=True)]


cycle = (0, 2, 4, 6, 7, 5, 3, 1)


def owner_at(distance):
    index = lax.axis_index("expert")
    place = jnp.where(index % 2 == 0, index // 2, 7 - index // 2)
    spot = (place + distance) & 7
    return jnp.where(spot < 4, 2 * spot, 15 - 2 * spot)


class Ring:
    def __init__(self, shard):
        self.shard = shard
        self.rows = shard.shape[0]
        self.plus = self.minus = shard
        self.pieces = [shard]
        self.plan = [(0, 0)]
        self.latest = (shard,)
        self.small = small_grid()

    def advance(self, *gate):
        if not self.small:
            if len(self.latest) == 1 and self.latest[0] is self.shard:
                whole = lax.all_gather(after(self.shard, *gate), "expert", axis=0, tiled=True)
                self.pieces, self.plan, self.latest = [whole], [(None, 0)], (whole,)
            return self.latest
        number = len(self.pieces) // 2 + 1
        up = [(a, b) for a, b in zip(cycle, cycle[1:] + cycle[:1])]
        down = [(b, a) for a, b in up]
        plus, minus, middle = self.plus, self.minus, 0
        if number == 4:
            middle = self.rows // 32 * 16
            plus, minus = plus[:middle], minus[middle:]
        self.plus = lax.ppermute(after(plus, *gate), "expert", up)
        self.minus = lax.ppermute(after(minus, *gate), "expert", down)
        self.pieces += [self.plus, self.minus]
        self.plan += [(-number, 0), (number, middle)]
        self.latest = (self.plus, self.minus)
        return self.latest

    def collect(self, part):
        if not self.small:
            return part(self.pieces[0])
        columns = part(self.shard).shape[1]
        whole = jnp.zeros((8 * self.rows, columns), self.shard.dtype)
        for (distance, start), piece in zip(self.plan, self.pieces):
            place = (owner_at(distance) * self.rows + start, 0)
            whole = lax.dynamic_update_slice(whole, part(piece), place)
        return whole


def copy_pieces(pieces, plan, rows, columns, target, sems, first=0):
    copies = []
    for number, ((distance, start), piece) in enumerate(zip(plan, pieces)):
        place = start
        if distance is not None:
            place = pl.multiple_of(owner_at(distance) * rows + start, 16)
        copies.append(
            pltpu.make_async_copy(
                piece.at[:, columns],
                target.at[pl.ds(place, piece.shape[0]), columns],
                sems.at[first + number],
            )
        )
    return copies


def start_all(copies):
    for one in copies:
        one.start()


def wait_all(copies):
    for one in copies:
        one.wait()


def inverse_rms(value):
    return lax.rsqrt(jnp.mean(value * value, axis=-1, keepdims=True) + epsilon)


def rms_norm(value, gain):
    return value * inverse_rms(value) * gain


def layout(lengths_row, row_index):
    ends = jnp.cumsum(lengths_row, dtype=jnp.int32)
    starts = ends - lengths_row
    segment = jnp.sum((row_index[:, None] >= ends[None, :]).astype(jnp.int32), axis=1)
    member = segment[:, None] == jnp.arange(ends.shape[0], dtype=jnp.int32)[None, :]
    return segment, row_index - jnp.sum(jnp.where(member, starts[None, :], 0), axis=1)


def make_tables(length_pair, row_index, head):
    half = head // 2
    inverse = np.power(rope_base, -(np.arange(half) * 2.0) / head).astype(np.float32)
    segments, angles = [], []
    for number, one in enumerate(length_pair):
        segment, position = layout(one, row_index)
        segments.append(segment + number * (one.shape[0] + 1))
        angles.append(position.astype(f32)[:, None] * inverse[None, :])
    segment, angle = cat(*segments), cat(*angles)
    order = cat(row_index, row_index)
    allowed = (segment[:, None] == segment[None, :]) & (order[None, :] <= order[:, None])
    cosine, sine = jnp.cos(angle), jnp.sin(angle)
    return cat(cosine, cosine, axis=1), cat(-sine, sine, axis=1), allowed.astype(f32)


def rope(value, cosine, sine):
    return value * cosine + pltpu.roll(value, value.shape[1] // 2, 1) * sine


def rope_back(value, cosine, sine):
    return value * cosine + pltpu.roll(value * sine, value.shape[1] // 2, 1)


def from_heads(row, split, share):
    wide, head = row.shape[1], split * share
    part = wide // split
    lane = lax.broadcasted_iota(jnp.int32, (wide, head), 0)
    place = lax.broadcasted_iota(jnp.int32, (wide, head), 1)
    found = (lane // part == place // share) & (lane % part == place % share)
    chosen = jnp.where(found, 1.0, 0.0).astype(bf16)
    return dot(jnp.broadcast_to(row, (8, wide)).astype(bf16), chosen)[:1]


def attend_kernel(plan, rows, layer, split, experts, *refs):
    count = len(plan)
    pieces, refs = refs[:count], refs[count:]
    if layer == 0:
        (x_hat, cosine, sine, allowed), refs = refs[:4], refs[4:]
        tiny, normed, *refs = refs
    else:
        normed_pieces, (tiny, cosine, sine, allowed), refs = refs[:4], refs[4:8], refs[8:]
        normed, *refs = refs
    mixed, raw_out, probs_out, out_own, out_other, weights, sems = refs
    head = cosine.shape[1]
    group = probs_out.shape[0]
    near_columns = raw_out.shape[1]
    far_columns = mixed.shape[1]
    breadth = near_columns + far_columns
    near = copy_pieces(pieces, plan, rows, pl.ds(0, near_columns), weights, sems)
    far = copy_pieces(pieces, plan, rows, pl.ds(near_columns, far_columns), weights, sems, count)
    if layer == 0:
        last = pl.ds(breadth, weights.shape[1] - breadth)
        small = copy_pieces(pieces, plan, rows, last, weights, sems, 2 * count)
        start_all(small)
    start_all(near)
    start_all(far)
    share = head // split
    size = experts + 4
    if layer == 0:
        wait_all(small)
        tiny[...] = jnp.transpose(weights[:, breadth:].astype(f32))
        normed[...] = (x_hat[...] * tiny[experts : experts + 1]).astype(bf16)
    else:
        half = normed_pieces[0].shape[0]
        for number, piece in enumerate(normed_pieces):
            normed[number * half : (number + 1) * half] = piece[...]
    start = layer * size + experts
    query_gain = from_heads(tiny[start + 2 : start + 3], split, share)
    key_gain = from_heads(tiny[start + 3 : start + 4], split, share)
    wait_all(near)
    raw = dot(normed[...], weights[:, :near_columns])
    raw_out[...] = raw
    cos, sin, allow = cosine[...], sine[...], allowed[...] > 0.0
    k_raw = raw[:, group * head : (group + 1) * head]
    keys = rope(k_raw * inverse_rms(k_raw) * key_gain, cos, sin).astype(bf16)
    values = raw[:, (group + 1) * head :].astype(bf16)
    for number in range(group):
        q_raw = raw[:, number * head : (number + 1) * head]
        query = rope(q_raw * inverse_rms(q_raw) * query_gain, cos, sin) * head ** (-0.5)
        scores = jnp.where(allow, dot_cols(query.astype(bf16), keys), masked_score)
        unscaled = jnp.exp(scores - jnp.max(scores, axis=-1, keepdims=True))
        probs = unscaled / jnp.sum(unscaled, axis=-1, keepdims=True)
        probs_out[number] = probs
        mixed[:, number * head : (number + 1) * head] = dot(probs.astype(bf16), values).astype(
            bf16
        )
    wait_all(far)
    out = dot_cols(mixed[...], weights[:, near_columns:breadth])
    half = out_own.shape[0]
    out_own[...] = out[:half]
    out_other[...] = out[half:].astype(bf16)


def attend(layer, ring, breadth, split, experts, inputs, tables):
    head = tables[0].shape[1]
    rows = tables[0].shape[0]
    width = inputs[0].shape[1]
    group = (breadth // head - 2) // 2
    near = (group + 2) * head
    columns = breadth if layer else ring.shard.shape[1]
    small = (*inputs, *tables)
    shapes = (
        array((rows, width), bf16),
        array((rows, group * head), bf16),
        array((rows, near), f32),
        array((group, rows, rows), f32),
        array((rows // 2, width), f32),
        array((rows // 2, width), bf16),
    )
    if layer == 0:
        shapes = (array((columns - breadth, width), f32), *shapes)
    count = len(ring.pieces)
    return pl.pallas_call(
        functools.partial(attend_kernel, ring.plan, ring.rows, layer, split, experts),
        in_specs=[anywhere] * count + [full(one) for one in small],
        out_specs=tuple(full(one) for one in shapes),
        out_shape=shapes,
        scratch_shapes=[pltpu.VMEM((width, columns), bf16), pltpu.SemaphoreType.DMA((3 * count,))],
        compiler_params=kernel_params(26),
        cost_estimate=cost(12 * rows * width * breadth, 2 * width * breadth),
    )(*ring.pieces, *small)


extra_rows = 16


def split_rows(out, start, value):
    size = value.shape[1]
    out[start:] = jnp.zeros((extra_rows, out.shape[1]), bf16)
    high = value.astype(bf16)
    out[start : start + 1, :size] = high
    out[start + 1 : start + 2, :size] = (value - high.astype(f32)).astype(bf16)


def joined_rows(rows, start, size):
    return rows[start : start + 1, :size].astype(f32) + rows[
        start + 1 : start + 2, :size
    ].astype(f32)


def attend_back_kernel(plan, block_rows, layer, axis, experts, *refs):
    count = len(plan)
    pieces, refs = refs[:count], refs[count:]
    d_pieces, refs = refs[:4], refs[4:]
    raw_in, probs_in, tiny, cosine, sine = refs[:5]
    d_attn, d_qkv, d_own, d_other, weights, sems = refs[5:]
    head = cosine.shape[1]
    rows = raw_in.shape[0]
    start = layer * (experts + 4) + experts
    query_gain = from_heads(tiny[start + 2 : start + 3], axis, head // axis)
    key_gain = from_heads(tiny[start + 3 : start + 4], axis, head // axis)
    half = d_pieces[0].shape[0]
    for number, piece in enumerate(d_pieces):
        d_attn[number * half : (number + 1) * half] = piece[...]
    group = probs_in.shape[0]
    split = raw_in.shape[1]
    rest = weights.shape[1] - split
    near = copy_pieces(pieces, plan, block_rows, pl.ds(split, rest), weights, sems)
    far = copy_pieces(pieces, plan, block_rows, pl.ds(0, split), weights, sems, count)
    start_all(near)
    cos, sin = cosine[...], sine[...]
    wait_all(near)
    start_all(far)
    d_mixed = dot(d_attn[...], weights[:, split:]).astype(bf16)
    k_raw = raw_in[:, group * head : (group + 1) * head]
    k_inverse = inverse_rms(k_raw)
    k_hat = k_raw * k_inverse
    keys = rope(k_hat * key_gain, cos, sin).astype(bf16)
    values = raw_in[:, (group + 1) * head :].astype(bf16)
    factor = head ** (-0.5)
    d_keys = jnp.zeros_like(k_raw)
    d_values = jnp.zeros_like(k_raw)
    gain_sum = jnp.zeros_like(query_gain)
    for number in range(group):
        span = slice(number * head, (number + 1) * head)
        q_raw = raw_in[:, span]
        q_inverse = inverse_rms(q_raw)
        q_hat = q_raw * q_inverse
        query = (rope(q_hat * query_gain, cos, sin) * factor).astype(bf16)
        probs = probs_in[number]
        d_one = d_mixed[:, span]
        d_probs = dot_cols(d_one, values)
        d_scores = probs * (d_probs - jnp.sum(probs * d_probs, axis=-1, keepdims=True))
        d_scores = d_scores.astype(bf16)
        d_values = d_values + dot_rows(probs.astype(bf16), d_one)
        d_keys = d_keys + dot_rows(d_scores, query)
        d_gained = rope_back(dot(d_scores, keys) * factor, cos, sin)
        gain_sum = gain_sum + jnp.sum(d_gained * q_hat, axis=0, keepdims=True)
        d_hat = d_gained * query_gain
        d_q = q_inverse * (d_hat - q_hat * jnp.mean(d_hat * q_hat, axis=-1, keepdims=True))
        d_qkv[:rows, span] = d_q.astype(bf16)
    d_gained = rope_back(d_keys, cos, sin)
    key_sum = jnp.sum(d_gained * k_hat, axis=0, keepdims=True)
    split_rows(d_qkv, rows, jnp.concatenate([gain_sum, key_sum], axis=1))
    d_hat = d_gained * key_gain
    d_k = k_inverse * (d_hat - k_hat * jnp.mean(d_hat * k_hat, axis=-1, keepdims=True))
    d_qkv[:rows, group * head : (group + 1) * head] = d_k.astype(bf16)
    d_qkv[:rows, (group + 1) * head :] = d_values.astype(bf16)
    wait_all(far)
    d_normed = dot_cols(d_qkv[:rows], weights[:, :split])
    half = d_own.shape[0]
    d_own[...] = d_normed[:half]
    d_other[...] = d_normed[half:].astype(bf16)


def attend_back(layer, ring, breadth, split, experts, pieces, raw, probs, tiny, tables):
    width = pieces[0].shape[1]
    rows = raw.shape[0]
    small = (*pieces, raw, probs, tiny, tables[0], tables[1])
    shapes = (
        array((rows, width), bf16),
        array((rows + extra_rows, raw.shape[1]), bf16),
        array((rows // 2, width), f32),
        array((rows // 2, width), bf16),
    )
    count = len(ring.pieces)
    return pl.pallas_call(
        functools.partial(attend_back_kernel, ring.plan, ring.rows, layer, split, experts),
        in_specs=[anywhere] * count + [full(one) for one in small],
        out_specs=tuple(full(one) for one in shapes),
        out_shape=shapes,
        scratch_shapes=[pltpu.VMEM((width, breadth), bf16), pltpu.SemaphoreType.DMA((2 * count,))],
        compiler_params=kernel_params(56),
        cost_estimate=cost(12 * rows * width * breadth, 2 * width * breadth),
    )(*ring.pieces, *small)


def choose_weights_kernel(layer, *refs):
    refs, (w_both, w_down, sems) = refs[:6], refs[6:]
    is_own = lax.axis_index("section") == layer
    experts = refs[0].shape[0]
    units = w_down.shape[0] // experts

    def copies(sources):
        made = []
        for number in range(experts):
            gate = pl.ds(2 * number * units, units)
            up = pl.ds((2 * number + 1) * units, units)
            targets = (
                w_both.at[:, gate],
                w_both.at[:, up],
                w_down.at[pl.ds(number * units, units)],
            )
            for i, target in enumerate(targets):
                sem = sems.at[3 * number + i]
                made.append(pltpu.make_async_copy(sources[i].at[number], target, sem))
        return made

    @pl.when(is_own)
    def _():
        start_all(copies(refs[:3]))

    @pl.when(jnp.logical_not(is_own))
    def _():
        start_all(copies(refs[3:]))

    wait_all(copies(refs[:3]))


def choose_weights(layer, weights):
    experts, width, units = weights[0].shape
    total = experts * units
    return pl.pallas_call(
        functools.partial(choose_weights_kernel, layer),
        in_specs=[anywhere] * 6,
        out_specs=(anywhere,) * 2,
        out_shape=(array((width, 2 * total), bf16), array((total, width), bf16)),
        scratch_shapes=[pltpu.SemaphoreType.DMA((3 * experts,))],
        compiler_params=kernel_params(8),
        cost_estimate=cost(1000, 1000),
    )(*weights)


def expert_copies(experts, sources, w_both, w_down, sems):
    units = w_down.shape[0] // experts
    groups = []
    for number in range(experts):
        wide = pl.ds(2 * number * units, 2 * units)
        narrow = pl.ds(number * units, units)
        groups.append(
            (
                pltpu.make_async_copy(
                    sources[0].at[:, wide], w_both.at[:, wide], sems.at[2 * number]
                ),
                pltpu.make_async_copy(
                    sources[1].at[narrow], w_down.at[narrow], sems.at[2 * number + 1]
                ),
            )
        )
    return groups


def load_pieces(pieces, tile, scratch, sems):
    if len(pieces) == 1:
        pieces = [pieces[0].at[pl.ds(tile * tile_rows, tile_rows)]]
    copies, start = [], 0
    for number, piece in enumerate(pieces):
        rows = piece.shape[0]
        target = scratch.at[pl.ds(start, rows)]
        copies.append(pltpu.make_async_copy(piece, target, sems.at[number]))
        start += rows
    start_all(copies)
    return copies


def store_pieces(value, outs, columns):
    start = 0
    for out in outs:
        rows = out.shape[0]
        out[:, columns] = value[start : start + rows]
        start += rows


def experts_kernel(count, layer, tile, before, *refs):
    pieces, refs = refs[:count], refs[count:]
    weight_refs, ones, refs = refs[:2], refs[2], refs[3 + before :]
    outs, refs = refs[:count], refs[count:]
    act_store, gates_out, rows_store, scaled_store = refs[:4]
    rows_in, scaled, w_both, w_down, sems, weight_sems, store_sems, act_out = refs[4:]
    width = w_both.shape[0]
    experts = ones.shape[0]
    units = w_down.shape[0] // experts
    loads = load_pieces(pieces, tile, rows_in, sems)
    weights = expert_copies(experts, weight_refs, w_both, w_down, weight_sems)
    weights[0][0].start()
    place = pl.ds(tile * tile_rows, tile_rows)
    stores = [
        pltpu.make_async_copy(
            rows_in.at[:, pl.ds(0, width)], rows_store.at[place], store_sems.at[0]
        ),
        pltpu.make_async_copy(scaled, scaled_store.at[place], store_sems.at[1]),
        pltpu.make_async_copy(act_out, act_store, store_sems.at[2]),
    ]
    wait_all(loads)
    stores[0].start()
    extra = rows_in[:, width:].astype(f32)
    gates = extra + pltpu.roll(extra, lanes // 2, 1)
    gates_out[...] = gates
    for number in range(experts):
        weights[number][0].wait()
        if number + 1 < experts:
            weights[number + 1][0].start()
        weights[number][1].start()
        span = slice(2 * number * units, 2 * (number + 1) * units)
        act = dot(rows_in[:, :width], w_both[:, span])
        act_out[:, span] = act.astype(act_out.dtype)
        gate_act, up_act = act[:, :units], act[:, units:]
        hidden = (gate_act / (1.0 + jnp.exp(-gate_act)) * up_act).astype(bf16)
        gate = jnp.sum(gates * ones[number : number + 1], axis=1, keepdims=True)
        scaled[:, number * units : (number + 1) * units] = (hidden.astype(f32) * gate).astype(bf16)
    stores[1].start()
    stores[2].start()
    for number in range(experts):
        weights[number][1].wait()
    step = width // 4
    for number in range(4):
        span = slice(number * step, (number + 1) * step)
        store_pieces(dot(scaled[...], w_down[:, span]).astype(bf16), outs, span)
    wait_all(stores)


def expert_scratch(wide, width, total_units, kind, count, experts):
    return [
        pltpu.VMEM((tile_rows, wide), bf16),
        kind,
        pltpu.VMEM((width, 2 * total_units), bf16),
        pltpu.VMEM((total_units, width), bf16),
        pltpu.SemaphoreType.DMA((count,)),
        pltpu.SemaphoreType.DMA((2 * experts,)),
        pltpu.SemaphoreType.DMA((3,)),
    ]


def run_experts(pieces, weights, ones, layer, tile, rows, stores):
    count = len(pieces)
    experts, total_units, width = ones.shape[0], *weights[1].shape
    stores = stores or ()
    sizes = [min(one.shape[0], tile_rows) for one in pieces]
    shapes = tuple([array((one, width), bf16) for one in sizes]) + (
        array((tile_rows, 2 * total_units), f32 if small_grid() else bf16),
        array((tile_rows, lanes), f32),
        array((rows, width), bf16),
        array((rows, total_units), bf16),
    )
    outs = pl.pallas_call(
        functools.partial(experts_kernel, count, layer, tile, len(stores)),
        in_specs=[anywhere] * (count + 2) + [full(ones)] + [anywhere] * len(stores),
        out_specs=tuple(full(one) for one in shapes[:count])
        + (anywhere, full(shapes[count + 1]), anywhere, anywhere),
        out_shape=shapes,
        scratch_shapes=expert_scratch(
            pieces[0].shape[1],
            width,
            total_units,
            pltpu.VMEM((tile_rows, total_units), bf16),
            count,
            experts,
        )
        + [pltpu.VMEM(shapes[count].shape, shapes[count].dtype)],
        input_output_aliases={count + 3: count + 2, count + 4: count + 3} if stores else {},
        compiler_params=kernel_params(26),
        cost_estimate=cost(12 * tile_rows * width * total_units, 6 * width * total_units),
    )(*pieces, *weights, ones, *stores)
    return list(outs[:count]), outs[count : count + 2], outs[count + 2 :]


def experts_back_kernel(count, layer, tile, before, *refs):
    pieces, refs = refs[:count], refs[count:]
    weight_refs, ones, act_in, gates_in = refs[:2], refs[2], refs[3], refs[4]
    refs = refs[5 + before :]
    outs, refs = refs[:count], refs[count:]
    d_store, grad_store = refs[:2]
    rows_in, d_act, w_both, w_down, sems, weight_sems, store_sems, act = refs[2:]
    width = w_both.shape[0]
    experts = ones.shape[0]
    units = w_down.shape[0] // experts
    loads = load_pieces(pieces, tile, rows_in, sems)
    weights = expert_copies(experts, weight_refs, w_both, w_down, weight_sems)
    weights[0][1].start()
    act_copy = pltpu.make_async_copy(act_in, act, store_sems.at[2])
    act_copy.start()
    place = pl.ds(tile * tile_rows, tile_rows)
    stores = [
        pltpu.make_async_copy(rows_in, grad_store.at[place], store_sems.at[0]),
        pltpu.make_async_copy(d_act, d_store.at[place], store_sems.at[1]),
    ]
    wait_all(loads)
    stores[0].start()
    gates = gates_in[...]
    placed = jnp.zeros_like(gates)
    for number in range(experts):
        weights[number][1].wait()
        if number + 1 < experts:
            weights[number + 1][1].start()
        weights[number][0].start()
        base = 2 * number * units
        plain = dot_cols(rows_in[...], w_down[number * units : (number + 1) * units])
        if number == 0:
            act_copy.wait()
        one = ones[number : number + 1]
        gate = jnp.sum(gates * one, axis=1, keepdims=True)
        gate_act = act[:, base : base + units].astype(f32)
        up_act = act[:, base + units : base + 2 * units].astype(f32)
        sigmoid = 1.0 / (1.0 + jnp.exp(-gate_act))
        silu = gate_act * sigmoid
        hidden = (silu * up_act).astype(bf16).astype(f32)
        placed = placed + jnp.sum(plain * hidden, axis=1, keepdims=True) * one
        d_hidden = plain * gate
        d_act[:, base + units : base + 2 * units] = (d_hidden * silu).astype(bf16)
        d_gate = d_hidden * up_act * (sigmoid + silu * (1.0 - sigmoid))
        d_act[:, base : base + units] = d_gate.astype(bf16)
    stores[1].start()
    for number in range(experts):
        weights[number][0].wait()
    step = width // 4
    for number in range(4):
        span = slice(number * step, (number + 1) * step)
        store_pieces(dot_cols(d_act[...], w_both[span]).astype(bf16), outs, span)
    store_pieces(placed.astype(bf16), outs, slice(width, width + lanes))
    wait_all(stores)


def run_experts_back(pieces, weights, ones, kept, layer, tile, rows, stores):
    count = len(pieces)
    experts, total_units, width = ones.shape[0], *weights[1].shape
    stores = stores or ()
    act, gates = kept
    sizes = [min(one.shape[0], tile_rows) for one in pieces]
    shapes = tuple([array((one, width + lanes), bf16) for one in sizes]) + (
        array((rows, 2 * total_units), bf16),
        array((rows, width), bf16),
    )
    outs = pl.pallas_call(
        functools.partial(experts_back_kernel, count, layer, tile, len(stores)),
        in_specs=[anywhere] * (count + 2)
        + [full(ones), anywhere, full(gates)]
        + [anywhere] * len(stores),
        out_specs=tuple(full(one) for one in shapes[:count]) + (anywhere,) * 2,
        out_shape=shapes,
        scratch_shapes=expert_scratch(
            width,
            width,
            total_units,
            pltpu.VMEM((tile_rows, 2 * total_units), bf16),
            count,
            experts,
        )
        + [pltpu.VMEM(act.shape, act.dtype)],
        input_output_aliases={count + 5: count, count + 6: count + 1} if stores else {},
        compiler_params=kernel_params(26),
        cost_estimate=cost(12 * tile_rows * width * total_units, 6 * width * total_units),
    )(*pieces, *weights, ones, act, gates, *stores)
    return list(outs[:count]), outs[count:]


def grads_kernel(column, before, count, *refs):
    sources, refs = refs[:8], refs[8 + before :]
    outs, (left, right, result, sems, out_sems) = refs[:count], refs[count:]
    core = lax.axis_index("section")
    rows = left.shape[0] // 2
    place, step = column
    spans = [pl.ds(0, left.shape[1]), pl.ds(0, right.shape[1])]
    spans[place] = pl.ds(step * grad_columns, grad_columns)

    def copies(layer):
        made = []
        for number, target in enumerate((left, right)):
            for got in range(2):
                source = sources[4 * number + 2 * got + layer]
                made.append(
                    pltpu.make_async_copy(
                        source.at[:, spans[number]],
                        target.at[pl.ds(got * rows, rows)],
                        sems.at[2 * number + got],
                    )
                )
        return made

    for layer in range(2):

        @pl.when(core == layer)
        def _():
            start_all(copies(layer))

    wait_all(copies(0))
    experts = outs[0].shape[0]
    units = result.shape[1 - place] // (experts * count)
    result[...] = dot_rows(left[...], right[...])
    stores = []
    for expert in range(experts):
        for number, out in enumerate(outs):
            start = (expert * len(outs) + number) * units
            if place == 0:
                source = result.at[:, pl.ds(start, units)]
                target = out.at[expert, spans[0]]
            else:
                source = result.at[pl.ds(start, units)]
                target = out.at[expert, :, spans[1]]
            stores.append(pltpu.make_async_copy(source, target, out_sems.at[len(stores)]))
    start_all(stores)
    wait_all(stores)


def run_grads(place, step, left, right, shapes, before):
    before = before or ()
    rows = left[0].shape[0]
    widths = [left[0].shape[1], right[0].shape[1]]
    widths[place] = grad_columns
    experts = shapes[0].shape[0]
    return pl.pallas_call(
        functools.partial(grads_kernel, (place, step), len(before), len(shapes)),
        in_specs=[anywhere] * (8 + len(before)),
        out_specs=(anywhere,) * len(shapes),
        out_shape=shapes,
        scratch_shapes=[
            pltpu.VMEM((2 * rows, widths[0]), bf16),
            pltpu.VMEM((2 * rows, widths[1]), bf16),
            pltpu.VMEM((widths[0], widths[1]), f32),
            pltpu.SemaphoreType.DMA((4,)),
            pltpu.SemaphoreType.DMA((experts * len(shapes),)),
        ],
        input_output_aliases={8 + i: i for i in range(len(before))},
        compiler_params=kernel_params(56),
        cost_estimate=cost(10**8, 10**5),
    )(*left, *right, *before)


def wide_grads(experts, rows_in, d_act):
    width, units = rows_in[0].shape[1], d_act[0].shape[1] // (2 * experts)
    shapes = (array((experts, width, units), f32),) * 2
    made = []
    for step in range(width // grad_columns):
        made.append(run_grads(0, step, rows_in, d_act, shapes, made[-1] if made else None))
    return made


def down_grads(experts, scaled, grads):
    width, units = grads[0].shape[1], scaled[0].shape[1] // experts
    shapes = (array((experts, units, width), f32),)
    made = []
    for step in range(width // grad_columns):
        made.append(run_grads(1, step, scaled, grads, shapes, made[-1] if made else None))
    return made


def out_grads_kernel(plan, rows, *refs):
    count = len(plan)
    pieces, (spread, g_out, mixed, d_cols, sems) = refs[:count], refs[count:]
    copies = copy_pieces(pieces, plan, rows, pl.ds(0, mixed.shape[1]), mixed, sems)
    copies.append(pltpu.make_async_copy(spread.at[:, pl.ds(0, rows)], d_cols, sems.at[count]))
    start_all(copies)
    wait_all(copies)
    g_out[...] = dot_rows(mixed[...], d_cols[...].reshape(mixed.shape[0], d_cols.shape[2]))


def out_grads(ring, spread):
    blocks, _, columns = spread.shape
    breadth = ring.shard.shape[1]
    count = len(ring.pieces)
    shape = array((breadth, columns), f32)
    total = blocks * ring.rows
    return pl.pallas_call(
        functools.partial(out_grads_kernel, ring.plan, ring.rows),
        in_specs=[anywhere] * (count + 1),
        out_specs=full(shape),
        out_shape=shape,
        scratch_shapes=[
            pltpu.VMEM((total, breadth), bf16),
            pltpu.VMEM((blocks, ring.rows, columns), bf16),
            pltpu.SemaphoreType.DMA((count + 1,)),
        ],
        compiler_params=kernel_params(56),
        cost_estimate=cost(10**8, 10**5),
    )(*ring.pieces, spread)


def stack_layer_kernel(sums, zero, one, got, out):
    core = lax.axis_index("section")
    columns = zero.shape[1]
    rows = zero.shape[0] - (extra_rows if sums else 0)
    half = rows // 2
    for number, own in ((0, zero), (1, one)):

        @pl.when(core == number)
        def _():
            here = slice(number * columns, (number + 1) * columns)
            there = slice((1 - number) * columns, (2 - number) * columns)
            out[:rows, here] = own[:rows]
            out[:half, there] = got[half:rows]
            out[half:rows, there] = got[:half]
            if sums:
                total = joined_rows(own, rows, sums) + joined_rows(got, rows, sums)
                split_rows(out, rows, total)


def stack_layer(zero, one, got, sums=0):
    rows, columns = zero.shape
    kernel = functools.partial(stack_layer_kernel, sums)
    return simple(kernel, [array((rows, 2 * columns), zero.dtype)], zero, one, got)[0]


def projection_grads_kernel(plan, rows, *refs):
    count = len(plan)
    pieces, (spread, late_spread, w_query, w_key, w_value), refs = (
        refs[:count],
        refs[count : count + 5],
        refs[count + 5 :],
    )
    g_query, g_key, g_value, late, d_qkv, normed, parts, sems = refs
    tokens = rows - extra_rows
    copies = copy_pieces(pieces, plan, rows, pl.ds(0, d_qkv.shape[1]), d_qkv, sems)
    target = normed.at[:, pl.ds(0, tokens)]
    copies.append(pltpu.make_async_copy(spread, target, sems.at[count]))
    source = late_spread.at[:, pl.ds(tokens, parts.shape[1])]
    copies.append(pltpu.make_async_copy(source, parts, sems.at[count + 1]))
    start_all(copies)
    blocks, _, part = normed.shape
    normed[:, tokens:] = jnp.zeros((blocks, extra_rows, part), bf16)
    wait_all(copies)
    wide = g_query.shape[1] // 2
    head = g_key.shape[1] // 2
    both = dot_rows(normed[...].reshape(blocks * rows, part), d_qkv[...])
    for side in range(2):
        start = side * (wide + 2 * head)
        g_query[:, side * wide : (side + 1) * wide] = both[:, start : start + wide]
        g_key[:, side * head : (side + 1) * head] = both[:, start + wide : start + wide + head]
        g_value[:, side * head : (side + 1) * head] = both[
            :, start + wide + head : start + wide + 2 * head
        ]
    products = (
        jnp.sum(w_query[...].astype(f32) * g_query[...], axis=1, keepdims=True)
        + jnp.sum(w_key[...].astype(f32) * g_key[...], axis=1, keepdims=True)
        + jnp.sum(w_value[...].astype(f32) * g_value[...], axis=1, keepdims=True)
    )
    heads = jnp.zeros((1, 2 * head), f32)
    for block in range(blocks):
        heads = heads + joined_rows(d_qkv, block * rows + tokens, 2 * head)
    late[...] = jnp.zeros_like(late)
    late[8:, :part] = jnp.sum(parts[...].astype(f32), axis=0)
    late[:1, :part] = jnp.transpose(jnp.broadcast_to(products, (part, lanes)))[:1]
    late[1:2, : 2 * head] = heads


def projection_grads(ring, spread, late_spread, weights, head):
    blocks, tokens, part = spread.shape
    size = late_spread.shape[1] - tokens
    breadth = ring.shard.shape[1]
    wide = breadth // 2 - 2 * head
    count = len(ring.pieces)
    total = blocks * ring.rows
    shapes = (
        array((part, 2 * wide), f32),
        array((part, 2 * head), f32),
        array((part, 2 * head), f32),
        array((8 + size, max(part, 2 * head)), f32),
    )
    return pl.pallas_call(
        functools.partial(projection_grads_kernel, ring.plan, ring.rows),
        in_specs=[anywhere] * (count + 2) + [full(one) for one in weights],
        out_specs=tuple(full(one) for one in shapes),
        out_shape=shapes,
        scratch_shapes=[
            pltpu.VMEM((total, breadth), bf16),
            pltpu.VMEM((blocks, ring.rows, part), bf16),
            pltpu.VMEM((blocks, size, part), bf16),
            pltpu.SemaphoreType.DMA((count + 2,)),
        ],
        compiler_params=kernel_params(56),
        cost_estimate=cost(20 * total * part * breadth, 4 * total * breadth),
    )(*ring.pieces, spread, late_spread, *weights)


def both_rows(shard):
    far = swap_x(shard)
    return (shard, far, swap_core(shard), swap_core(far))


def merge_kernel(own, got, kept, given):
    block = own[...] + got[...].astype(f32)
    half = kept.shape[0]
    kept[...] = block[:half]
    given[...] = block[half:].astype(bf16)


def own_rows(own, other):
    rows, width = own.shape
    shapes = [array((rows // 2, width), kind) for kind in (f32, bf16)]
    kept, given = simple(merge_kernel, shapes, own, swap_core(other))
    return kept, swap_x(given)


def route_kernel(layer, x, kept, got, tiny, mask, mid_out, payload, gates_out):
    experts = mask.shape[1]
    width = x.shape[1]
    start = layer * (experts + 4)
    mid = x[...] + kept[...] + got[...].astype(f32)
    mid_out[...] = mid
    gain = tiny[start + experts + 1 : start + experts + 2]
    normed = (mid * inverse_rms(mid) * gain).astype(bf16)
    payload[:, :width] = normed
    logits = dot_cols(normed, tiny[start : start + experts].astype(bf16))
    logits = jnp.where(mask[...] > 0.0, logits, masked_score)
    weights = jnp.exp(logits - jnp.max(logits, axis=-1, keepdims=True))
    gates = weights / jnp.sum(weights, axis=-1, keepdims=True)
    gates_out[...] = gates
    high = gates.astype(bf16)
    low = (gates - high.astype(f32)).astype(bf16)
    payload[:, width:] = jnp.zeros((x.shape[0], lanes), bf16)
    payload[:, width : width + experts] = high
    payload[:, width + lanes // 2 : width + lanes // 2 + experts] = low


def route(layer, x, kept, got, tiny, mask):
    rows, width = x.shape
    shapes = [
        array((rows, width), f32),
        array((rows, width + lanes), bf16),
        array(mask.shape, f32),
    ]
    kernel = functools.partial(route_kernel, layer)
    return simple(kernel, shapes, x, kept, got, tiny, mask)


def sum_parts(parts):
    total = parts[0][...]
    for one in parts[1:]:
        total = total + one[...].astype(f32)
    return total


def enter_kernel(count, experts, mid, *refs):
    parts, (tiny, x_out, normed) = refs[:count], refs[count:]
    x = (mid[...] + sum_parts(parts)).astype(bf16).astype(f32)
    x_out[...] = x
    row = 2 * experts + 4
    normed[...] = (x * inverse_rms(x) * tiny[row : row + 1]).astype(bf16)


def enter(mid, parts, tiny, experts):
    shapes = [array(mid.shape, f32), array(mid.shape, bf16)]
    kernel = functools.partial(enter_kernel, len(parts), experts)
    return simple(kernel, shapes, mid, *parts, tiny)


def finish_kernel(mid, *refs):
    refs[-1][...] = (mid[...] + sum_parts(refs[:-1])).astype(bf16)


def finish(mid, parts):
    return simple(finish_kernel, [array(mid.shape, bf16)], mid, *parts)[0]


def norm_back(value, gain, grad):
    inverse = inverse_rms(value)
    hat = value * inverse
    d_hat = grad * gain
    d_value = inverse * (d_hat - hat * jnp.mean(d_hat * hat, axis=-1, keepdims=True))
    return d_value, jnp.sum(grad * hat, axis=0, keepdims=True)


def unroute_kernel(count, layer, *refs):
    parts, refs = refs[:count], refs[count:]
    grad, mid, tiny, gates_in, payload, d_out, d_low, g_router, g_gain = refs
    width = mid.shape[1]
    experts = gates_in.shape[1]
    start = layer * (experts + 4)
    back = sum_parts(parts)
    gates = gates_in[...]
    gate_grad = back[:, width : width + experts]
    d_logits = gates * (gate_grad - jnp.sum(gates * gate_grad, axis=-1, keepdims=True))
    d_logits = d_logits.astype(bf16)
    d_normed = back[:, :width] + dot(d_logits, tiny[start : start + experts].astype(bf16))
    gain = tiny[start + experts + 1 : start + experts + 2]
    d_mid, gain_sum = norm_back(mid[...], gain, d_normed)
    d_mid = d_mid + grad[...].astype(f32)
    d_out[...] = d_mid
    d_low[...] = d_mid.astype(bf16)
    g_router[...] = dot_rows(d_logits, payload[:, :width])
    g_gain[...] = gain_sum


def unroute(layer, parts, grad, mid, tiny, gates, payload):
    width, experts = mid.shape[1], gates.shape[1]
    shapes = [
        array(mid.shape, f32),
        array(mid.shape, bf16),
        array((experts, width), f32),
        array((1, width), f32),
    ]
    kernel = functools.partial(unroute_kernel, len(parts), layer)
    return simple(kernel, shapes, *parts, grad, mid, tiny, gates, payload)


def leave_kernel(row, kept, got, x, d_mid, tiny, d_out):
    d_normed = kept[...] + got[...].astype(f32)
    d_x, _ = norm_back(x[...], tiny[row : row + 1], d_normed)
    d_out[...] = (d_mid[...] + d_x).astype(bf16)


def leave(layer, experts, kept, got, x, d_mid, tiny):
    kernel = functools.partial(leave_kernel, layer * (experts + 4) + experts)
    return simple(kernel, [array(x.shape, bf16)], kept, got, x, d_mid, tiny)[0]


def count_rows(tiles):
    return max(tile_rows, tiles[0][0].shape[0])


def apply_experts(tiles, weights, ones, layer):
    kept, outs, stores = [], [], None
    for number, pieces in enumerate(tiles):
        out, saved, stores = run_experts(
            pieces, weights, ones, layer, number, count_rows(tiles), stores
        )
        outs.append(out)
        kept.append(saved)
    return outs, kept, stores


def apply_experts_back(tiles, weights, ones, kept, layer):
    backs, stores = [], None
    for number, (pieces, saved) in enumerate(zip(tiles, kept)):
        back, stores = run_experts_back(
            pieces, weights, ones, saved, layer, number, count_rows(tiles), stores
        )
        backs.append(back)
    return backs, stores


def choose_kernel(zero, one, out):
    core = lax.axis_index("section")
    for number, own in enumerate((zero, one)):

        @pl.when(core == number)
        def _():
            out[: own.shape[0]] = own[...]


def small_kernel(router0, gain0, router1, gain1, own, other):
    core = lax.axis_index("section")
    layers = ((router0, gain0), (router1, gain1))
    experts = router0.shape[0]
    for number in range(2):

        @pl.when(core == number)
        def _():
            for out, layer in ((own, number), (other, 1 - number)):
                router, gain = layers[layer]
                out[...] = jnp.zeros_like(out)
                out[:experts] = router[...]
                out[experts : experts + 1] = gain[...]


def late_kernel(zero, one, own, got, out):
    rows = zero.shape[0]
    choose_kernel(zero, one, out)
    out[rows:] = (own[...] + got[...]).astype(bf16)


def other_layer_kernel(zero, one, out, sem):
    core = lax.axis_index("section")
    for number, source in enumerate((one, zero)):

        @pl.when(core == number)
        def _():
            pltpu.make_async_copy(source, out, sem).start()

    pltpu.make_async_copy(zero, out, sem).wait()


def exchange(zero, one):
    sent = pl.pallas_call(
        other_layer_kernel,
        in_specs=[anywhere] * 2,
        out_specs=anywhere,
        out_shape=array(zero.shape, zero.dtype),
        scratch_shapes=[pltpu.SemaphoreType.DMA],
        compiler_params=kernel_params(8),
        cost_estimate=cost(1000, 1000),
    )(zero, one)
    got = swap_core(sent)
    return zero, one, got, got


def by_columns(value, split):
    columns = value.shape[1] // split
    return jnp.stack([value[:, i * columns : (i + 1) * columns] for i in range(split)])


def to_owners(blocks):
    return lax.all_to_all(blocks, "expert", split_axis=0, concat_axis=0, tiled=True)


def body(
    ends_in,
    attn_gain,
    w_query,
    key_matrix,
    value_matrix,
    query_gain,
    key_gain,
    w_out,
    ffn_gain,
    router,
    w_gate,
    w_up,
    w_down,
    routes,
    lengths,
):
    core = lax.axis_index("section")
    first = core == 0
    side = lax.axis_index("tensor")
    index = lax.axis_index("expert")
    split = lax.axis_size("expert")
    rows, width = ends_in.shape[2:]
    half = rows // 2
    experts = router.shape[2]
    head = query_gain.shape[1] * split

    def pick(zero, one):
        return jnp.where(first, zero, one)

    def mine(pair):
        return pick(pair[0], pair[1])

    def theirs(pair):
        return pick(pair[1], pair[0])

    def by_layer(own):
        got = swap_core(own)
        return pick(own, got), pick(got, own)

    def pick_side(zero, one):
        return jnp.where(side == 0, zero, one)

    def half_rows(block):
        return pick_side(block[:half], block[half:])

    def side_first(block):
        return pick_side(block, cat(block[half:], block[:half]))

    part = w_query.shape[1]
    columns = w_query.shape[2] // 2
    transposed = w_out[0].T
    groups = [
        cat(
            w_query[0][:, g * columns : (g + 1) * columns],
            key_matrix[0][:, g * head : (g + 1) * head],
            value_matrix[0][:, g * head : (g + 1) * head],
            transposed[:, g * columns : (g + 1) * columns],
            axis=1,
        )
        for g in range(2)
    ]
    kept, got = mine(groups), swap_core(theirs(groups))
    breadth = kept.shape[1]

    share = head // split
    gains = cat(query_gain[0][:, None], key_gain[0][:, None], axis=1)
    tiny = cat(
        router[0],
        attn_gain[0][:, None],
        ffn_gain[0][:, None],
        jnp.pad(gains, ((0, part - share), (0, 0))),
        axis=1,
    )
    size = tiny.shape[1]
    tiny = cat(*by_layer(tiny), axis=1)
    tiny = jnp.pad(tiny, ((0, 0), (0, -2 * size % lanes)))
    ring0 = Ring(cat(pick(kept, got), tiny, axis=1))
    ring1 = Ring(pick(got, kept))
    started = ring0.advance()

    ends_in, w_gate, w_up, w_down = lax.optimization_barrier(
        (ends_in, w_gate, w_up, w_down, *started)
    )[:4]
    own_weights = (w_gate[0], w_up[0], w_down[0])
    expert_weights = own_weights + tuple(swap_core(one) for one in own_weights)
    crossed = swap_core(ends_in[0])
    x_all, grad_all = pick(ends_in[0], crossed), pick(crossed, ends_in[0])
    x_own = mine(x_all)
    x_in = half_rows(x_own).astype(f32)
    grad_last = half_rows(mine(grad_all))
    x_both = cat(side_first(x_own), side_first(theirs(x_all))).astype(f32)
    x_hat = x_both * inverse_rms(x_both)

    routes, lengths = lax.optimization_barrier((routes, lengths, *ring0.advance()))[:2]
    routes_crossed = swap_core(pick(routes[0, 1], routes[0, 0]))
    routes_own = [pick(routes[0, 0], routes_crossed), pick(routes_crossed, routes[0, 1])]
    expert_ids = jnp.arange(experts, dtype=jnp.int32)
    masks = [
        jnp.any(half_rows(r)[:, :, None] == expert_ids[None, None, :], axis=1).astype(f32)
        for r in routes_own
    ]
    per_device = w_gate.shape[1]
    lane_ids = jnp.arange(lanes, dtype=jnp.int32)
    local_ids = index * per_device + jnp.arange(per_device, dtype=jnp.int32)
    ones = (lane_ids[None, :] == local_ids[:, None]).astype(f32)
    row_index = (jnp.arange(rows, dtype=jnp.int32) + side * half) % rows
    length_pair = [pick(lengths[0, 0], lengths[1, 0]), pick(lengths[1, 0], lengths[0, 0])]
    tables = make_tables(length_pair, row_index, head)

    ring0.advance()
    ring0.advance()
    ring1.advance(*ring0.latest)

    tiny, normed0, mixed0, raw0, probs0, own, other = attend(
        0, ring0, breadth, split, experts, (x_hat,), tables
    )
    other = after(other, *ring1.latest)
    mid0, payload0, gates0 = route(0, x_in, *own_rows(own, other), tiny, masks[0])
    gather = Gather(payload0)
    gather.along_z()
    weights0 = choose_weights(0, (after(expert_weights[0], payload0), *expert_weights[1:]))
    gather.near(*weights0)
    gather.far()
    tiles = gather.tiles()
    ring1.advance(tiles[-1][-1])
    outs0, kept0, stores0 = apply_experts(tiles, weights0, ones, 0)
    scatter = Scatter(outs0)
    scatter.far()
    scatter.near(beside=ring1.latest)
    parts = scatter.along_z()
    ring1.advance(*parts)
    ring1.advance()
    x_mid, shard = enter(mid0, parts, tiny, experts)

    normed_pieces = both_rows(shard)
    grad_gather = Gather(grad_last)
    along = grad_gather.along_z(normed_pieces[-1])
    normed1, mixed1, raw1, probs1, own, other = attend(
        1, ring1, breadth, split, experts, (*normed_pieces, tiny), tables
    )
    other = after(other, *along)
    mid1, payload1, gates1 = route(1, x_mid, *own_rows(own, other), tiny, masks[1])
    beside = grad_gather.near(payload1)
    gather = Gather(payload1)
    gather.along_z()
    weights1 = choose_weights(1, (after(expert_weights[0], payload1), *expert_weights[1:]))
    gather.near(*weights1, *beside)
    gather.far()
    tiles = gather.tiles()
    beside = grad_gather.far(tiles[-1][-1])
    mixed_got = swap_core(pick(mixed1, mixed0))
    ring_mixed = Ring(stack_layer(mixed0, mixed1, mixed_got))
    ring_mixed.advance(tiles[-1][-1])
    outs1, kept1, stores1 = apply_experts(tiles, weights1, ones, 1)

    outs1[-1][-1] = after(outs1[-1][-1], *ring_mixed.latest, *beside)
    tiles = grad_gather.tiles(outs1[-1][-1])
    ring_mixed.advance(tiles[-1][-1])
    backs, back_stores1 = apply_experts_back(tiles, weights1, ones, kept1, 1)
    scatter = Scatter(backs)
    scatter.far(*ring_mixed.latest)
    reached = scatter.near()
    out_scatter = Scatter(outs1)
    beside = out_scatter.far(*reached)
    parts = scatter.along_z()
    parts[-1] = after(parts[-1], *beside)
    d_mid, d_low, g_router1, g_ffn_gain1 = unroute(
        1, parts, grad_last, mid1, tiny, gates1, payload1
    )
    d_pieces = both_rows(d_low)
    ring_mixed.advance(d_pieces[-1])

    if small_grid():
        rows_in = exchange(after(stores0[0], d_pieces[-1]), stores1[0])
        early = (rows_in[2],)
    else:
        early = ()
    d_attn1, d_qkv1, d_own, d_other = attend_back(
        1, ring1, breadth, split, experts, d_pieces, raw1, probs1, tiny, tables
    )
    d_other = after(d_other, *ring_mixed.latest, *early)
    ring_mixed.advance(d_qkv1)
    d_one = leave(1, experts, *own_rows(d_own, d_other), x_mid, d_mid, tiny)

    d_one = after(d_one, *ring_mixed.latest)
    gather = Gather(d_one)
    gather.along_z()
    beside = out_scatter.near(d_one)
    weights0 = choose_weights(0, (after(expert_weights[0], d_one), *expert_weights[1:]))
    gather.near(*beside, *weights0)
    gather.far()
    tiles = gather.tiles()
    backs, back_stores0 = apply_experts_back(tiles, weights0, ones, kept0, 0)

    if not small_grid():
        rows_in = exchange(after(stores0[0], back_stores0[0]), stores1[0])
    d_act = exchange(after(back_stores0[0], rows_in[2]), back_stores1[0])
    wide = wide_grads(per_device, rows_in, d_act)
    scatter = Scatter(backs)
    normed_own = simple(
        choose_kernel, [array(normed0.shape, bf16)], normed0, after(normed1, *scatter.far())
    )[0]
    normed_blocks = by_columns(normed_own, split)
    scatter.near(beside=(*wide[0], normed_blocks))
    parts = scatter.along_z()
    parts[-1] = after(parts[-1], *wide[1])
    d_mid, d_low, g_router0, g_ffn_gain0 = unroute(
        0, parts, d_one, mid0, tiny, gates0, payload0
    )
    d_pieces = both_rows(d_low)
    normed_spread = to_owners(after(normed_blocks, d_pieces[-1]))
    out_parts = out_scatter.along_z(d_pieces[-1])
    d_attn0, d_qkv0, d_own, d_other = attend_back(
        0, ring0, breadth, split, experts, d_pieces, raw0, probs0, tiny, tables
    )

    qkv_got = swap_core(pick(d_qkv1, after(d_qkv0, normed_spread, *out_parts)))
    ring_d = Ring(stack_layer(d_qkv0, d_qkv1, qkv_got, 2 * head))
    one_round = ring_d.advance()
    d_other = after(d_other, ring_d.shard)
    d_zero = leave(0, experts, *own_rows(d_own, d_other), x_in, d_mid, tiny)
    scaled = exchange(after(stores0[1], ring_d.shard), stores1[1])
    gate = ring_d.shard if small_grid() else scaled[2]
    late = (scaled, exchange(after(back_stores0[1], gate), back_stores1[1]))
    down = down_grads(per_device, *late)
    ring_d.advance()
    rows_small = -(-(experts + 1) // 16) * 16
    small_own, small_other = simple(
        small_kernel,
        [array((rows_small, width), f32)] * 2,
        after(g_router0, *one_round),
        g_ffn_gain0,
        g_router1,
        g_ffn_gain1,
    )
    late_rows = simple(
        late_kernel,
        [array((2 * rows + rows_small, width), bf16)],
        d_attn0,
        d_attn1,
        small_own,
        swap_core(small_other),
    )[0]
    late_spread = to_owners(by_columns(late_rows, split))
    three_rounds = ring_d.advance(*down[0])
    ring_d.advance(*down[1])
    g_out = out_grads(ring_mixed, late_spread)
    out1 = finish(mid1, out_parts)
    end_own = pick(d_zero, out1)
    end_got = swap_core(pick(out1, d_zero))
    projections = (w_query[0], key_matrix[0], value_matrix[0])
    g_query, g_key, g_value, late = projection_grads(
        ring_d, normed_spread, after(late_spread, *ring_mixed.latest), projections, head
    )
    (g_gate, g_up), (g_down,) = wide[-1], down[-1]

    small = late + swap_x(late)
    g_attn_gain = small[0, :part] / attn_gain[0].astype(f32)
    g_query_gain = lax.dynamic_slice(small[1], (index * share,), (share,))
    g_key_gain = lax.dynamic_slice(small[1], (head + index * share,), (share,))
    g_router = small[8 : 8 + experts, :part].T
    g_ffn_gain = small[8 + experts, :part]

    ends = jnp.stack([pick(end_own, end_got), pick(end_got, end_own)])
    ends_far = swap_x(ends)
    ends_out = cat(pick_side(ends, ends_far), pick_side(ends_far, ends), axis=1)

    outs = (
        ends_out,
        g_attn_gain,
        g_query,
        g_key,
        g_value,
        g_query_gain,
        g_key_gain,
        g_out,
        g_ffn_gain,
        g_router,
        g_gate,
        g_up,
        g_down,
    )
    return tuple(one[None] for one in outs)


def solution(mesh):
    return jax.shard_map(
        body,
        mesh=mesh,
        in_specs=(
            P("section", None, "expert", None),
            P("section", "expert"),
            P("section", "expert", "tensor"),
            P("section", "expert", "tensor"),
            P("section", "expert", "tensor"),
            P("section", "expert"),
            P("section", "expert"),
            P("section", "tensor", "expert"),
            P("section", "expert"),
            P("section", "expert", None),
            P("section", "expert", None, "tensor"),
            P("section", "expert", None, "tensor"),
            P("section", "expert", "tensor", None),
            P("section", None, "expert", None),
            P(None, "expert", None),
        ),
        out_specs=(
            P("section", None, "expert", None),
            P("section", "expert"),
            P("section", "expert", "tensor"),
            P("section", "expert", "tensor"),
            P("section", "expert", "tensor"),
            P("section", "expert"),
            P("section", "expert"),
            P("section", "tensor", "expert"),
            P("section", "expert"),
            P("section", "expert", None),
            P("section", "expert", None, "tensor"),
            P("section", "expert", None, "tensor"),
            P("section", "expert", "tensor", None),
        ),
        check_vma=False,
    )
```

```python
import functools

import jax
import jax.numpy as jnp
import numpy as np
from jax import lax
from jax.experimental import pallas as pl
from jax.experimental.pallas import tpu as pltpu
from jax.sharding import PartitionSpec as P

epsilon = 1e-06
rope_base = 1000000.0
masked_score = -1e30
bf16 = jnp.bfloat16
f32 = jnp.float32
lanes = 128
tile_rows = 512
grad_columns = 1024


def dot(left, right):
    return jnp.dot(left, right, preferred_element_type=f32)


def dot_rows(left, right):
    return lax.dot_general(left, right, (((0,), (0,)), ((), ())), preferred_element_type=f32)


def dot_cols(left, right):
    return lax.dot_general(left, right, (((1,), (1,)), ((), ())), preferred_element_type=f32)


def cat(*pieces, axis=0):
    return jnp.concatenate(pieces, axis=axis)


def swap_core(value):
    return lax.ppermute(value, "section", [(0, 1), (1, 0)])


def swap_x(value):
    return lax.ppermute(value, "tensor", [(0, 1), (1, 0)])


def swap_e(value, bits):
    count = lax.axis_size("expert")
    return lax.ppermute(value, "expert", [(i, i ^ bits) for i in range(count)])


def small_grid():
    return lax.axis_size("expert") == 8


def after(value, *others):
    return lax.optimization_barrier((value, *others))[0] if others else value


anywhere = pl.BlockSpec(memory_space=pl.ANY)


def full(one):
    return pl.BlockSpec(one.shape, lambda *_: (0,) * len(one.shape))


def array(shape, kind):
    return jax.ShapeDtypeStruct(shape, kind)


def kernel_params(megabytes):
    return pltpu.CompilerParams(vmem_limit_bytes=megabytes * 2**20)


def cost(flops, moved):
    return pl.CostEstimate(flops=flops, bytes_accessed=moved, transcendentals=0)


def simple(kernel, shapes, *operands):
    return pl.pallas_call(
        kernel,
        in_specs=[full(one) for one in operands],
        out_specs=tuple(full(one) for one in shapes),
        out_shape=tuple(shapes),
        compiler_params=kernel_params(16),
        cost_estimate=cost(1000, 1000),
    )(*operands)


def stack_kernel(*refs):
    start = 0
    for ref in refs[:-1]:
        refs[-1][start : start + ref.shape[0]] = ref[...]
        start += ref.shape[0]


def stack(*pieces):
    rows = sum(one.shape[0] for one in pieces)
    return simple(stack_kernel, [array((rows, pieces[0].shape[1]), pieces[0].dtype)], *pieces)[0]


def near_kernel(to_x, top, to_y, bottom, out_x, out_y):
    half = top.shape[0]
    out_x[:half] = (to_x[:half].astype(f32) + top[...].astype(f32)).astype(bf16)
    out_x[half:] = to_x[half:]
    out_y[:half] = to_y[:half]
    out_y[half:] = (to_y[half:].astype(f32) + bottom[...].astype(f32)).astype(bf16)


def total_kernel(own, from_x, from_y, kept, *blocks):
    total = own[...].astype(f32) + from_x[...].astype(f32) + from_y[...].astype(f32)
    step = kept.shape[0]
    kept[...] = total[:step]
    for number, block in enumerate(blocks):
        block[...] = total[(number + 1) * step : (number + 2) * step].astype(bf16)


class Gather:
    def __init__(self, shard):
        self.shard = shard
        self.small = small_grid()

    def along_z(self, *gate):
        if self.small:
            shard = after(self.shard, *gate)
            self.line = (shard, swap_e(shard, 2), swap_e(shard, 4), swap_e(shard, 6))
            return self.line[1:]
        return ()

    def near(self, *gate):
        if self.small:
            own = after(stack(*self.line), *gate)
            self.near_pieces = (own, swap_x(own), swap_e(own, 1))
            return self.near_pieces[1:]
        return ()

    def far(self, *gate):
        if self.small:
            own, from_x, from_y = self.near_pieces
            half = own.shape[0] // 2
            self.far_pieces = (
                swap_e(after(from_x[:half], *gate), 1),
                swap_x(after(from_y[half:], *gate)),
            )
            return self.far_pieces
        shard = after(self.shard, *gate)
        self.whole = lax.all_gather(shard, ("expert", "tensor"), axis=0, tiled=True)
        return (self.whole,)

    def tiles(self, *gate):
        if self.small:
            top, bottom = self.far_pieces
            return [[*self.near_pieces, top, after(bottom, *gate)]]
        whole = after(self.whole, *gate)
        return [[whole]] * (whole.shape[0] // tile_rows)


class Scatter:
    def __init__(self, tiles):
        self.tiles = tiles
        self.small = small_grid()

    def far(self, *gate):
        if self.small:
            far_top, far_bottom = self.tiles[0][3:]
            self.top = swap_e(after(far_top, *gate), 1)
            self.bottom = swap_x(after(far_bottom, *gate))
            return (self.top, self.bottom)
        return ()

    def near(self, *gate, beside=()):
        if self.small:
            own, to_x, to_y = self.tiles[0][:3]
            shape = array(to_x.shape, bf16)
            to_x, to_y = simple(near_kernel, [shape] * 2, to_x, self.top, to_y, self.bottom)
            from_x, from_y = swap_x(after(to_x, *gate)), swap_e(after(to_y, *gate), 1)
            from_x = after(from_x, *beside)
            rows, columns = own.shape
            shapes = [array((rows // 4, columns), kind) for kind in (f32, bf16, bf16, bf16)]
            self.blocks = simple(total_kernel, shapes, own, from_x, from_y)
            return self.blocks[:1]
        return ()

    def along_z(self, *gate):
        if self.small:
            kept, *blocks = self.blocks
            moved = [swap_e(after(one, *gate), bits) for one, bits in zip(blocks, (2, 4, 6))]
            return [kept, *moved]
        whole = cat(*[one for pieces in self.tiles for one in pieces])
        whole = after(whole, *gate).astype(f32)
        return [lax.psum_scatter(whole, ("expert", "tensor"), scatter_dimension=0, tiled=True)]


cycle = (0, 2, 4, 6, 7, 5, 3, 1)


def owner_at(distance):
    index = lax.axis_index("expert")
    place = jnp.where(index % 2 == 0, index // 2, 7 - index // 2)
    spot = (place + distance) & 7
    return jnp.where(spot < 4, 2 * spot, 15 - 2 * spot)


class Ring:
    def __init__(self, shard):
        self.shard = shard
        self.rows = shard.shape[0]
        self.plus = self.minus = shard
        self.pieces = [shard]
        self.plan = [(0, 0)]
        self.latest = (shard,)
        self.small = small_grid()

    def advance(self, *gate):
        if not self.small:
            if len(self.latest) == 1 and self.latest[0] is self.shard:
                whole = lax.all_gather(after(self.shard, *gate), "expert", axis=0, tiled=True)
                self.pieces, self.plan, self.latest = [whole], [(None, 0)], (whole,)
            return self.latest
        number = len(self.pieces) // 2 + 1
        up = [(a, b) for a, b in zip(cycle, cycle[1:] + cycle[:1])]
        down = [(b, a) for a, b in up]
        plus, minus, middle = self.plus, self.minus, 0
        if number == 4:
            middle = self.rows // 32 * 16
            plus, minus = plus[:middle], minus[middle:]
        self.plus = lax.ppermute(after(plus, *gate), "expert", up)
        self.minus = lax.ppermute(after(minus, *gate), "expert", down)
        self.pieces += [self.plus, self.minus]
        self.plan += [(-number, 0), (number, middle)]
        self.latest = (self.plus, self.minus)
        return self.latest

    def collect(self, part):
        if not self.small:
            return part(self.pieces[0])
        columns = part(self.shard).shape[1]
        whole = jnp.zeros((8 * self.rows, columns), self.shard.dtype)
        for (distance, start), piece in zip(self.plan, self.pieces):
            place = (owner_at(distance) * self.rows + start, 0)
            whole = lax.dynamic_update_slice(whole, part(piece), place)
        return whole


def copy_pieces(pieces, plan, rows, columns, target, sems, first=0):
    copies = []
    for number, ((distance, start), piece) in enumerate(zip(plan, pieces)):
        place = start
        if distance is not None:
            place = pl.multiple_of(owner_at(distance) * rows + start, 16)
        copies.append(
            pltpu.make_async_copy(
                piece.at[:, columns],
                target.at[pl.ds(place, piece.shape[0]), columns],
                sems.at[first + number],
            )
        )
    return copies


def start_all(copies):
    for one in copies:
        one.start()


def wait_all(copies):
    for one in copies:
        one.wait()


def inverse_rms(value):
    return lax.rsqrt(jnp.mean(value * value, axis=-1, keepdims=True) + epsilon)


def rms_norm(value, gain):
    return value * inverse_rms(value) * gain


def layout(lengths_row, row_index):
    ends = jnp.cumsum(lengths_row, dtype=jnp.int32)
    starts = ends - lengths_row
    segment = jnp.sum((row_index[:, None] >= ends[None, :]).astype(jnp.int32), axis=1)
    member = segment[:, None] == jnp.arange(ends.shape[0], dtype=jnp.int32)[None, :]
    return segment, row_index - jnp.sum(jnp.where(member, starts[None, :], 0), axis=1)


def make_tables(length_pair, row_index, head):
    half = head // 2
    inverse = np.power(rope_base, -(np.arange(half) * 2.0) / head).astype(np.float32)
    segments, angles = [], []
    for number, one in enumerate(length_pair):
        segment, position = layout(one, row_index)
        segments.append(segment + number * (one.shape[0] + 1))
        angles.append(position.astype(f32)[:, None] * inverse[None, :])
    segment, angle = cat(*segments), cat(*angles)
    order = cat(row_index, row_index)
    allowed = (segment[:, None] == segment[None, :]) & (order[None, :] <= order[:, None])
    cosine, sine = jnp.cos(angle), jnp.sin(angle)
    return cat(cosine, cosine, axis=1), cat(-sine, sine, axis=1), allowed.astype(f32)


def rope(value, cosine, sine):
    return value * cosine + pltpu.roll(value, value.shape[1] // 2, 1) * sine


def rope_back(value, cosine, sine):
    return value * cosine + pltpu.roll(value * sine, value.shape[1] // 2, 1)


def from_heads(row, split, share):
    wide, head = row.shape[1], split * share
    part = wide // split
    lane = lax.broadcasted_iota(jnp.int32, (wide, head), 0)
    place = lax.broadcasted_iota(jnp.int32, (wide, head), 1)
    found = (lane // part == place // share) & (lane % part == place % share)
    chosen = jnp.where(found, 1.0, 0.0).astype(bf16)
    return dot(jnp.broadcast_to(row, (8, wide)).astype(bf16), chosen)[:1]


def attend_kernel(plan, rows, layer, split, experts, *refs):
    count = len(plan)
    pieces, refs = refs[:count], refs[count:]
    if layer == 0:
        (x_hat, cosine, sine, allowed), refs = refs[:4], refs[4:]
        tiny, normed, *refs = refs
    else:
        normed_pieces, (tiny, cosine, sine, allowed), refs = refs[:4], refs[4:8], refs[8:]
        normed, *refs = refs
    mixed, raw_out, probs_out, out_own, out_other, weights, sems = refs
    head = cosine.shape[1]
    group = probs_out.shape[0]
    near_columns = raw_out.shape[1]
    far_columns = mixed.shape[1]
    breadth = near_columns + far_columns
    near = copy_pieces(pieces, plan, rows, pl.ds(0, near_columns), weights, sems)
    far = copy_pieces(pieces, plan, rows, pl.ds(near_columns, far_columns), weights, sems, count)
    if layer == 0:
        last = pl.ds(breadth, weights.shape[1] - breadth)
        small = copy_pieces(pieces, plan, rows, last, weights, sems, 2 * count)
        start_all(small)
    start_all(near)
    start_all(far)
    share = head // split
    size = experts + 4
    if layer == 0:
        wait_all(small)
        tiny[...] = jnp.transpose(weights[:, breadth:].astype(f32))
        normed[...] = (x_hat[...] * tiny[experts : experts + 1]).astype(bf16)
    else:
        half = normed_pieces[0].shape[0]
        for number, piece in enumerate(normed_pieces):
            normed[number * half : (number + 1) * half] = piece[...]
    start = layer * size + experts
    query_gain = from_heads(tiny[start + 2 : start + 3], split, share)
    key_gain = from_heads(tiny[start + 3 : start + 4], split, share)
    wait_all(near)
    raw = dot(normed[...], weights[:, :near_columns])
    raw_out[...] = raw
    cos, sin, allow = cosine[...], sine[...], allowed[...] > 0.0
    k_raw = raw[:, group * head : (group + 1) * head]
    keys = rope(k_raw * inverse_rms(k_raw) * key_gain, cos, sin).astype(bf16)
    values = raw[:, (group + 1) * head :].astype(bf16)
    for number in range(group):
        q_raw = raw[:, number * head : (number + 1) * head]
        query = rope(q_raw * inverse_rms(q_raw) * query_gain, cos, sin) * head ** (-0.5)
        scores = jnp.where(allow, dot_cols(query.astype(bf16), keys), masked_score)
        unscaled = jnp.exp(scores - jnp.max(scores, axis=-1, keepdims=True))
        probs = unscaled / jnp.sum(unscaled, axis=-1, keepdims=True)
        probs_out[number] = probs
        mixed[:, number * head : (number + 1) * head] = dot(probs.astype(bf16), values).astype(
            bf16
        )
    wait_all(far)
    out = dot_cols(mixed[...], weights[:, near_columns:breadth])
    half = out_own.shape[0]
    out_own[...] = out[:half]
    out_other[...] = out[half:].astype(bf16)


def attend(layer, ring, breadth, split, experts, inputs, tables):
    head = tables[0].shape[1]
    rows = tables[0].shape[0]
    width = inputs[0].shape[1]
    group = (breadth // head - 2) // 2
    near = (group + 2) * head
    columns = breadth if layer else ring.shard.shape[1]
    small = (*inputs, *tables)
    shapes = (
        array((rows, width), bf16),
        array((rows, group * head), bf16),
        array((rows, near), f32),
        array((group, rows, rows), f32),
        array((rows // 2, width), f32),
        array((rows // 2, width), bf16),
    )
    if layer == 0:
        shapes = (array((columns - breadth, width), f32), *shapes)
    count = len(ring.pieces)
    return pl.pallas_call(
        functools.partial(attend_kernel, ring.plan, ring.rows, layer, split, experts),
        in_specs=[anywhere] * count + [full(one) for one in small],
        out_specs=tuple(full(one) for one in shapes),
        out_shape=shapes,
        scratch_shapes=[pltpu.VMEM((width, columns), bf16), pltpu.SemaphoreType.DMA((3 * count,))],
        compiler_params=kernel_params(26),
        cost_estimate=cost(12 * rows * width * breadth, 2 * width * breadth),
    )(*ring.pieces, *small)


extra_rows = 16


def split_rows(out, start, value):
    size = value.shape[1]
    out[start:] = jnp.zeros((extra_rows, out.shape[1]), bf16)
    high = value.astype(bf16)
    out[start : start + 1, :size] = high
    out[start + 1 : start + 2, :size] = (value - high.astype(f32)).astype(bf16)


def joined_rows(rows, start, size):
    return rows[start : start + 1, :size].astype(f32) + rows[
        start + 1 : start + 2, :size
    ].astype(f32)


def attend_back_kernel(plan, block_rows, layer, axis, experts, *refs):
    count = len(plan)
    pieces, refs = refs[:count], refs[count:]
    d_pieces, refs = refs[:4], refs[4:]
    raw_in, probs_in, tiny, cosine, sine = refs[:5]
    d_attn, d_qkv, d_own, d_other, weights, sems = refs[5:]
    head = cosine.shape[1]
    rows = raw_in.shape[0]
    start = layer * (experts + 4) + experts
    query_gain = from_heads(tiny[start + 2 : start + 3], axis, head // axis)
    key_gain = from_heads(tiny[start + 3 : start + 4], axis, head // axis)
    half = d_pieces[0].shape[0]
    for number, piece in enumerate(d_pieces):
        d_attn[number * half : (number + 1) * half] = piece[...]
    group = probs_in.shape[0]
    split = raw_in.shape[1]
    rest = weights.shape[1] - split
    near = copy_pieces(pieces, plan, block_rows, pl.ds(split, rest), weights, sems)
    far = copy_pieces(pieces, plan, block_rows, pl.ds(0, split), weights, sems, count)
    start_all(near)
    cos, sin = cosine[...], sine[...]
    wait_all(near)
    start_all(far)
    d_mixed = dot(d_attn[...], weights[:, split:]).astype(bf16)
    k_raw = raw_in[:, group * head : (group + 1) * head]
    k_inverse = inverse_rms(k_raw)
    k_hat = k_raw * k_inverse
    keys = rope(k_hat * key_gain, cos, sin).astype(bf16)
    values = raw_in[:, (group + 1) * head :].astype(bf16)
    factor = head ** (-0.5)
    d_keys = jnp.zeros_like(k_raw)
    d_values = jnp.zeros_like(k_raw)
    gain_sum = jnp.zeros_like(query_gain)
    for number in range(group):
        span = slice(number * head, (number + 1) * head)
        q_raw = raw_in[:, span]
        q_inverse = inverse_rms(q_raw)
        q_hat = q_raw * q_inverse
        query = (rope(q_hat * query_gain, cos, sin) * factor).astype(bf16)
        probs = probs_in[number]
        d_one = d_mixed[:, span]
        d_probs = dot_cols(d_one, values)
        d_scores = probs * (d_probs - jnp.sum(probs * d_probs, axis=-1, keepdims=True))
        d_scores = d_scores.astype(bf16)
        d_values = d_values + dot_rows(probs.astype(bf16), d_one)
        d_keys = d_keys + dot_rows(d_scores, query)
        d_gained = rope_back(dot(d_scores, keys) * factor, cos, sin)
        gain_sum = gain_sum + jnp.sum(d_gained * q_hat, axis=0, keepdims=True)
        d_hat = d_gained * query_gain
        d_q = q_inverse * (d_hat - q_hat * jnp.mean(d_hat * q_hat, axis=-1, keepdims=True))
        d_qkv[:rows, span] = d_q.astype(bf16)
    d_gained = rope_back(d_keys, cos, sin)
    key_sum = jnp.sum(d_gained * k_hat, axis=0, keepdims=True)
    split_rows(d_qkv, rows, jnp.concatenate([gain_sum, key_sum], axis=1))
    d_hat = d_gained * key_gain
    d_k = k_inverse * (d_hat - k_hat * jnp.mean(d_hat * k_hat, axis=-1, keepdims=True))
    d_qkv[:rows, group * head : (group + 1) * head] = d_k.astype(bf16)
    d_qkv[:rows, (group + 1) * head :] = d_values.astype(bf16)
    wait_all(far)
    d_normed = dot_cols(d_qkv[:rows], weights[:, :split])
    half = d_own.shape[0]
    d_own[...] = d_normed[:half]
    d_other[...] = d_normed[half:].astype(bf16)


def attend_back(layer, ring, breadth, split, experts, pieces, raw, probs, tiny, tables):
    width = pieces[0].shape[1]
    rows = raw.shape[0]
    small = (*pieces, raw, probs, tiny, tables[0], tables[1])
    shapes = (
        array((rows, width), bf16),
        array((rows + extra_rows, raw.shape[1]), bf16),
        array((rows // 2, width), f32),
        array((rows // 2, width), bf16),
    )
    count = len(ring.pieces)
    return pl.pallas_call(
        functools.partial(attend_back_kernel, ring.plan, ring.rows, layer, split, experts),
        in_specs=[anywhere] * count + [full(one) for one in small],
        out_specs=tuple(full(one) for one in shapes),
        out_shape=shapes,
        scratch_shapes=[pltpu.VMEM((width, breadth), bf16), pltpu.SemaphoreType.DMA((2 * count,))],
        compiler_params=kernel_params(56),
        cost_estimate=cost(12 * rows * width * breadth, 2 * width * breadth),
    )(*ring.pieces, *small)


def choose_weights_kernel(layer, *refs):
    refs, (w_both, w_down, sems) = refs[:6], refs[6:]
    is_own = lax.axis_index("section") == layer
    experts = refs[0].shape[0]
    units = w_down.shape[0] // experts

    def copies(sources):
        made = []
        for number in range(experts):
            gate = pl.ds(2 * number * units, units)
            up = pl.ds((2 * number + 1) * units, units)
            targets = (
                w_both.at[:, gate],
                w_both.at[:, up],
                w_down.at[pl.ds(number * units, units)],
            )
            for i, target in enumerate(targets):
                sem = sems.at[3 * number + i]
                made.append(pltpu.make_async_copy(sources[i].at[number], target, sem))
        return made

    @pl.when(is_own)
    def _():
        start_all(copies(refs[:3]))

    @pl.when(jnp.logical_not(is_own))
    def _():
        start_all(copies(refs[3:]))

    wait_all(copies(refs[:3]))


def choose_weights(layer, weights):
    experts, width, units = weights[0].shape
    total = experts * units
    return pl.pallas_call(
        functools.partial(choose_weights_kernel, layer),
        in_specs=[anywhere] * 6,
        out_specs=(anywhere,) * 2,
        out_shape=(array((width, 2 * total), bf16), array((total, width), bf16)),
        scratch_shapes=[pltpu.SemaphoreType.DMA((3 * experts,))],
        compiler_params=kernel_params(8),
        cost_estimate=cost(1000, 1000),
    )(*weights)


def expert_copies(experts, sources, w_both, w_down, sems):
    units = w_down.shape[0] // experts
    groups = []
    for number in range(experts):
        wide = pl.ds(2 * number * units, 2 * units)
        narrow = pl.ds(number * units, units)
        groups.append(
            (
                pltpu.make_async_copy(
                    sources[0].at[:, wide], w_both.at[:, wide], sems.at[2 * number]
                ),
                pltpu.make_async_copy(
                    sources[1].at[narrow], w_down.at[narrow], sems.at[2 * number + 1]
                ),
            )
        )
    return groups


def load_pieces(pieces, tile, scratch, sems):
    if len(pieces) == 1:
        pieces = [pieces[0].at[pl.ds(tile * tile_rows, tile_rows)]]
    copies, start = [], 0
    for number, piece in enumerate(pieces):
        rows = piece.shape[0]
        target = scratch.at[pl.ds(start, rows)]
        copies.append(pltpu.make_async_copy(piece, target, sems.at[number]))
        start += rows
    start_all(copies)
    return copies


def store_pieces(value, outs, columns):
    start = 0
    for out in outs:
        rows = out.shape[0]
        out[:, columns] = value[start : start + rows]
        start += rows


def experts_kernel(count, layer, tile, before, *refs):
    pieces, refs = refs[:count], refs[count:]
    weight_refs, ones, refs = refs[:2], refs[2], refs[3 + before :]
    outs, refs = refs[:count], refs[count:]
    act_store, gates_out, rows_store, scaled_store = refs[:4]
    rows_in, scaled, w_both, w_down, sems, weight_sems, store_sems, act_out = refs[4:]
    width = w_both.shape[0]
    experts = ones.shape[0]
    units = w_down.shape[0] // experts
    loads = load_pieces(pieces, tile, rows_in, sems)
    weights = expert_copies(experts, weight_refs, w_both, w_down, weight_sems)
    weights[0][0].start()
    place = pl.ds(tile * tile_rows, tile_rows)
    stores = [
        pltpu.make_async_copy(
            rows_in.at[:, pl.ds(0, width)], rows_store.at[place], store_sems.at[0]
        ),
        pltpu.make_async_copy(scaled, scaled_store.at[place], store_sems.at[1]),
        pltpu.make_async_copy(act_out, act_store, store_sems.at[2]),
    ]
    wait_all(loads)
    stores[0].start()
    extra = rows_in[:, width:].astype(f32)
    gates = extra + pltpu.roll(extra, lanes // 2, 1)
    gates_out[...] = gates
    for number in range(experts):
        weights[number][0].wait()
        if number + 1 < experts:
            weights[number + 1][0].start()
        weights[number][1].start()
        span = slice(2 * number * units, 2 * (number + 1) * units)
        act = dot(rows_in[:, :width], w_both[:, span])
        act_out[:, span] = act.astype(act_out.dtype)
        gate_act, up_act = act[:, :units], act[:, units:]
        hidden = (gate_act / (1.0 + jnp.exp(-gate_act)) * up_act).astype(bf16)
        gate = jnp.sum(gates * ones[number : number + 1], axis=1, keepdims=True)
        scaled[:, number * units : (number + 1) * units] = (hidden.astype(f32) * gate).astype(bf16)
    stores[1].start()
    stores[2].start()
    for number in range(experts):
        weights[number][1].wait()
    step = width // 4
    for number in range(4):
        span = slice(number * step, (number + 1) * step)
        store_pieces(dot(scaled[...], w_down[:, span]).astype(bf16), outs, span)
    wait_all(stores)


def expert_scratch(wide, width, total_units, kind, count, experts):
    return [
        pltpu.VMEM((tile_rows, wide), bf16),
        kind,
        pltpu.VMEM((width, 2 * total_units), bf16),
        pltpu.VMEM((total_units, width), bf16),
        pltpu.SemaphoreType.DMA((count,)),
        pltpu.SemaphoreType.DMA((2 * experts,)),
        pltpu.SemaphoreType.DMA((3,)),
    ]


def run_experts(pieces, weights, ones, layer, tile, rows, stores):
    count = len(pieces)
    experts, total_units, width = ones.shape[0], *weights[1].shape
    stores = stores or ()
    sizes = [min(one.shape[0], tile_rows) for one in pieces]
    shapes = tuple([array((one, width), bf16) for one in sizes]) + (
        array((tile_rows, 2 * total_units), f32 if small_grid() else bf16),
        array((tile_rows, lanes), f32),
        array((rows, width), bf16),
        array((rows, total_units), bf16),
    )
    outs = pl.pallas_call(
        functools.partial(experts_kernel, count, layer, tile, len(stores)),
        in_specs=[anywhere] * (count + 2) + [full(ones)] + [anywhere] * len(stores),
        out_specs=tuple(full(one) for one in shapes[:count])
        + (anywhere, full(shapes[count + 1]), anywhere, anywhere),
        out_shape=shapes,
        scratch_shapes=expert_scratch(
            pieces[0].shape[1],
            width,
            total_units,
            pltpu.VMEM((tile_rows, total_units), bf16),
            count,
            experts,
        )
        + [pltpu.VMEM(shapes[count].shape, shapes[count].dtype)],
        input_output_aliases={count + 3: count + 2, count + 4: count + 3} if stores else {},
        compiler_params=kernel_params(26),
        cost_estimate=cost(12 * tile_rows * width * total_units, 6 * width * total_units),
    )(*pieces, *weights, ones, *stores)
    return list(outs[:count]), outs[count : count + 2], outs[count + 2 :]


def experts_back_kernel(count, layer, tile, before, *refs):
    pieces, refs = refs[:count], refs[count:]
    weight_refs, ones, act_in, gates_in = refs[:2], refs[2], refs[3], refs[4]
    refs = refs[5 + before :]
    outs, refs = refs[:count], refs[count:]
    d_store, grad_store = refs[:2]
    rows_in, d_act, w_both, w_down, sems, weight_sems, store_sems, act = refs[2:]
    width = w_both.shape[0]
    experts = ones.shape[0]
    units = w_down.shape[0] // experts
    loads = load_pieces(pieces, tile, rows_in, sems)
    weights = expert_copies(experts, weight_refs, w_both, w_down, weight_sems)
    weights[0][1].start()
    act_copy = pltpu.make_async_copy(act_in, act, store_sems.at[2])
    act_copy.start()
    place = pl.ds(tile * tile_rows, tile_rows)
    stores = [
        pltpu.make_async_copy(rows_in, grad_store.at[place], store_sems.at[0]),
        pltpu.make_async_copy(d_act, d_store.at[place], store_sems.at[1]),
    ]
    wait_all(loads)
    stores[0].start()
    gates = gates_in[...]
    placed = jnp.zeros_like(gates)
    for number in range(experts):
        weights[number][1].wait()
        if number + 1 < experts:
            weights[number + 1][1].start()
        weights[number][0].start()
        base = 2 * number * units
        plain = dot_cols(rows_in[...], w_down[number * units : (number + 1) * units])
        if number == 0:
            act_copy.wait()
        one = ones[number : number + 1]
        gate = jnp.sum(gates * one, axis=1, keepdims=True)
        gate_act = act[:, base : base + units].astype(f32)
        up_act = act[:, base + units : base + 2 * units].astype(f32)
        sigmoid = 1.0 / (1.0 + jnp.exp(-gate_act))
        silu = gate_act * sigmoid
        hidden = (silu * up_act).astype(bf16).astype(f32)
        placed = placed + jnp.sum(plain * hidden, axis=1, keepdims=True) * one
        d_hidden = plain * gate
        d_act[:, base + units : base + 2 * units] = (d_hidden * silu).astype(bf16)
        d_gate = d_hidden * up_act * (sigmoid + silu * (1.0 - sigmoid))
        d_act[:, base : base + units] = d_gate.astype(bf16)
    stores[1].start()
    for number in range(experts):
        weights[number][0].wait()
    step = width // 4
    for number in range(4):
        span = slice(number * step, (number + 1) * step)
        store_pieces(dot_cols(d_act[...], w_both[span]).astype(bf16), outs, span)
    store_pieces(placed.astype(bf16), outs, slice(width, width + lanes))
    wait_all(stores)


def run_experts_back(pieces, weights, ones, kept, layer, tile, rows, stores):
    count = len(pieces)
    experts, total_units, width = ones.shape[0], *weights[1].shape
    stores = stores or ()
    act, gates = kept
    sizes = [min(one.shape[0], tile_rows) for one in pieces]
    shapes = tuple([array((one, width + lanes), bf16) for one in sizes]) + (
        array((rows, 2 * total_units), bf16),
        array((rows, width), bf16),
    )
    outs = pl.pallas_call(
        functools.partial(experts_back_kernel, count, layer, tile, len(stores)),
        in_specs=[anywhere] * (count + 2)
        + [full(ones), anywhere, full(gates)]
        + [anywhere] * len(stores),
        out_specs=tuple(full(one) for one in shapes[:count]) + (anywhere,) * 2,
        out_shape=shapes,
        scratch_shapes=expert_scratch(
            width,
            width,
            total_units,
            pltpu.VMEM((tile_rows, 2 * total_units), bf16),
            count,
            experts,
        )
        + [pltpu.VMEM(act.shape, act.dtype)],
        input_output_aliases={count + 5: count, count + 6: count + 1} if stores else {},
        compiler_params=kernel_params(26),
        cost_estimate=cost(12 * tile_rows * width * total_units, 6 * width * total_units),
    )(*pieces, *weights, ones, act, gates, *stores)
    return list(outs[:count]), outs[count:]


def grads_kernel(column, before, count, *refs):
    sources, refs = refs[:8], refs[8 + before :]
    outs, (left, right, result, sems, out_sems) = refs[:count], refs[count:]
    core = lax.axis_index("section")
    rows = left.shape[0] // 2
    place, step = column
    spans = [pl.ds(0, left.shape[1]), pl.ds(0, right.shape[1])]
    spans[place] = pl.ds(step * grad_columns, grad_columns)

    def copies(layer):
        made = []
        for number, target in enumerate((left, right)):
            for got in range(2):
                source = sources[4 * number + 2 * got + layer]
                made.append(
                    pltpu.make_async_copy(
                        source.at[:, spans[number]],
                        target.at[pl.ds(got * rows, rows)],
                        sems.at[2 * number + got],
                    )
                )
        return made

    for layer in range(2):

        @pl.when(core == layer)
        def _():
            start_all(copies(layer))

    wait_all(copies(0))
    experts = outs[0].shape[0]
    units = result.shape[1 - place] // (experts * count)
    result[...] = dot_rows(left[...], right[...])
    stores = []
    for expert in range(experts):
        for number, out in enumerate(outs):
            start = (expert * len(outs) + number) * units
            if place == 0:
                source = result.at[:, pl.ds(start, units)]
                target = out.at[expert, spans[0]]
            else:
                source = result.at[pl.ds(start, units)]
                target = out.at[expert, :, spans[1]]
            stores.append(pltpu.make_async_copy(source, target, out_sems.at[len(stores)]))
    start_all(stores)
    wait_all(stores)


def run_grads(place, step, left, right, shapes, before):
    before = before or ()
    rows = left[0].shape[0]
    widths = [left[0].shape[1], right[0].shape[1]]
    widths[place] = grad_columns
    experts = shapes[0].shape[0]
    return pl.pallas_call(
        functools.partial(grads_kernel, (place, step), len(before), len(shapes)),
        in_specs=[anywhere] * (8 + len(before)),
        out_specs=(anywhere,) * len(shapes),
        out_shape=shapes,
        scratch_shapes=[
            pltpu.VMEM((2 * rows, widths[0]), bf16),
            pltpu.VMEM((2 * rows, widths[1]), bf16),
            pltpu.VMEM((widths[0], widths[1]), f32),
            pltpu.SemaphoreType.DMA((4,)),
            pltpu.SemaphoreType.DMA((experts * len(shapes),)),
        ],
        input_output_aliases={8 + i: i for i in range(len(before))},
        compiler_params=kernel_params(56),
        cost_estimate=cost(10**8, 10**5),
    )(*left, *right, *before)


def wide_grads(experts, rows_in, d_act):
    width, units = rows_in[0].shape[1], d_act[0].shape[1] // (2 * experts)
    shapes = (array((experts, width, units), f32),) * 2
    made = []
    for step in range(width // grad_columns):
        made.append(run_grads(0, step, rows_in, d_act, shapes, made[-1] if made else None))
    return made


def down_grads(experts, scaled, grads):
    width, units = grads[0].shape[1], scaled[0].shape[1] // experts
    shapes = (array((experts, units, width), f32),)
    made = []
    for step in range(width // grad_columns):
        made.append(run_grads(1, step, scaled, grads, shapes, made[-1] if made else None))
    return made


def out_grads_kernel(plan, rows, *refs):
    count = len(plan)
    pieces, (spread, g_out, mixed, d_cols, sems) = refs[:count], refs[count:]
    copies = copy_pieces(pieces, plan, rows, pl.ds(0, mixed.shape[1]), mixed, sems)
    copies.append(pltpu.make_async_copy(spread.at[:, pl.ds(0, rows)], d_cols, sems.at[count]))
    start_all(copies)
    wait_all(copies)
    g_out[...] = dot_rows(mixed[...], d_cols[...].reshape(mixed.shape[0], d_cols.shape[2]))


def out_grads(ring, spread):
    blocks, _, columns = spread.shape
    breadth = ring.shard.shape[1]
    count = len(ring.pieces)
    shape = array((breadth, columns), f32)
    total = blocks * ring.rows
    return pl.pallas_call(
        functools.partial(out_grads_kernel, ring.plan, ring.rows),
        in_specs=[anywhere] * (count + 1),
        out_specs=full(shape),
        out_shape=shape,
        scratch_shapes=[
            pltpu.VMEM((total, breadth), bf16),
            pltpu.VMEM((blocks, ring.rows, columns), bf16),
            pltpu.SemaphoreType.DMA((count + 1,)),
        ],
        compiler_params=kernel_params(56),
        cost_estimate=cost(10**8, 10**5),
    )(*ring.pieces, spread)


def stack_layer_kernel(sums, zero, one, got, out):
    core = lax.axis_index("section")
    columns = zero.shape[1]
    rows = zero.shape[0] - (extra_rows if sums else 0)
    half = rows // 2
    for number, own in ((0, zero), (1, one)):

        @pl.when(core == number)
        def _():
            here = slice(number * columns, (number + 1) * columns)
            there = slice((1 - number) * columns, (2 - number) * columns)
            out[:rows, here] = own[:rows]
            out[:half, there] = got[half:rows]
            out[half:rows, there] = got[:half]
            if sums:
                total = joined_rows(own, rows, sums) + joined_rows(got, rows, sums)
                split_rows(out, rows, total)


def stack_layer(zero, one, got, sums=0):
    rows, columns = zero.shape
    kernel = functools.partial(stack_layer_kernel, sums)
    return simple(kernel, [array((rows, 2 * columns), zero.dtype)], zero, one, got)[0]


def projection_grads_kernel(plan, rows, *refs):
    count = len(plan)
    pieces, (spread, late_spread, w_query, w_key, w_value), refs = (
        refs[:count],
        refs[count : count + 5],
        refs[count + 5 :],
    )
    g_query, g_key, g_value, late, d_qkv, normed, parts, sems = refs
    tokens = rows - extra_rows
    copies = copy_pieces(pieces, plan, rows, pl.ds(0, d_qkv.shape[1]), d_qkv, sems)
    target = normed.at[:, pl.ds(0, tokens)]
    copies.append(pltpu.make_async_copy(spread, target, sems.at[count]))
    source = late_spread.at[:, pl.ds(tokens, parts.shape[1])]
    copies.append(pltpu.make_async_copy(source, parts, sems.at[count + 1]))
    start_all(copies)
    blocks, _, part = normed.shape
    normed[:, tokens:] = jnp.zeros((blocks, extra_rows, part), bf16)
    wait_all(copies)
    wide = g_query.shape[1] // 2
    head = g_key.shape[1] // 2
    both = dot_rows(normed[...].reshape(blocks * rows, part), d_qkv[...])
    for side in range(2):
        start = side * (wide + 2 * head)
        g_query[:, side * wide : (side + 1) * wide] = both[:, start : start + wide]
        g_key[:, side * head : (side + 1) * head] = both[:, start + wide : start + wide + head]
        g_value[:, side * head : (side + 1) * head] = both[
            :, start + wide + head : start + wide + 2 * head
        ]
    products = (
        jnp.sum(w_query[...].astype(f32) * g_query[...], axis=1, keepdims=True)
        + jnp.sum(w_key[...].astype(f32) * g_key[...], axis=1, keepdims=True)
        + jnp.sum(w_value[...].astype(f32) * g_value[...], axis=1, keepdims=True)
    )
    heads = jnp.zeros((1, 2 * head), f32)
    for block in range(blocks):
        heads = heads + joined_rows(d_qkv, block * rows + tokens, 2 * head)
    late[...] = jnp.zeros_like(late)
    late[8:, :part] = jnp.sum(parts[...].astype(f32), axis=0)
    late[:1, :part] = jnp.transpose(jnp.broadcast_to(products, (part, lanes)))[:1]
    late[1:2, : 2 * head] = heads


def projection_grads(ring, spread, late_spread, weights, head):
    blocks, tokens, part = spread.shape
    size = late_spread.shape[1] - tokens
    breadth = ring.shard.shape[1]
    wide = breadth // 2 - 2 * head
    count = len(ring.pieces)
    total = blocks * ring.rows
    shapes = (
        array((part, 2 * wide), f32),
        array((part, 2 * head), f32),
        array((part, 2 * head), f32),
        array((8 + size, max(part, 2 * head)), f32),
    )
    return pl.pallas_call(
        functools.partial(projection_grads_kernel, ring.plan, ring.rows),
        in_specs=[anywhere] * (count + 2) + [full(one) for one in weights],
        out_specs=tuple(full(one) for one in shapes),
        out_shape=shapes,
        scratch_shapes=[
            pltpu.VMEM((total, breadth), bf16),
            pltpu.VMEM((blocks, ring.rows, part), bf16),
            pltpu.VMEM((blocks, size, part), bf16),
            pltpu.SemaphoreType.DMA((count + 2,)),
        ],
        compiler_params=kernel_params(56),
        cost_estimate=cost(20 * total * part * breadth, 4 * total * breadth),
    )(*ring.pieces, spread, late_spread, *weights)


def both_rows(shard):
    far = swap_x(shard)
    return (shard, far, swap_core(shard), swap_core(far))


def merge_kernel(own, got, kept, given):
    block = own[...] + got[...].astype(f32)
    half = kept.shape[0]
    kept[...] = block[:half]
    given[...] = block[half:].astype(bf16)


def own_rows(own, other):
    rows, width = own.shape
    shapes = [array((rows // 2, width), kind) for kind in (f32, bf16)]
    kept, given = simple(merge_kernel, shapes, own, swap_core(other))
    return kept, swap_x(given)


def route_kernel(layer, x, kept, got, tiny, mask, mid_out, payload, gates_out):
    experts = mask.shape[1]
    width = x.shape[1]
    start = layer * (experts + 4)
    mid = x[...] + kept[...] + got[...].astype(f32)
    mid_out[...] = mid
    gain = tiny[start + experts + 1 : start + experts + 2]
    normed = (mid * inverse_rms(mid) * gain).astype(bf16)
    payload[:, :width] = normed
    logits = dot_cols(normed, tiny[start : start + experts].astype(bf16))
    logits = jnp.where(mask[...] > 0.0, logits, masked_score)
    weights = jnp.exp(logits - jnp.max(logits, axis=-1, keepdims=True))
    gates = weights / jnp.sum(weights, axis=-1, keepdims=True)
    gates_out[...] = gates
    high = gates.astype(bf16)
    low = (gates - high.astype(f32)).astype(bf16)
    payload[:, width:] = jnp.zeros((x.shape[0], lanes), bf16)
    payload[:, width : width + experts] = high
    payload[:, width + lanes // 2 : width + lanes // 2 + experts] = low


def route(layer, x, kept, got, tiny, mask):
    rows, width = x.shape
    shapes = [
        array((rows, width), f32),
        array((rows, width + lanes), bf16),
        array(mask.shape, f32),
    ]
    kernel = functools.partial(route_kernel, layer)
    return simple(kernel, shapes, x, kept, got, tiny, mask)


def sum_parts(parts):
    total = parts[0][...]
    for one in parts[1:]:
        total = total + one[...].astype(f32)
    return total


def enter_kernel(count, experts, mid, *refs):
    parts, (tiny, x_out, normed) = refs[:count], refs[count:]
    x = (mid[...] + sum_parts(parts)).astype(bf16).astype(f32)
    x_out[...] = x
    row = 2 * experts + 4
    normed[...] = (x * inverse_rms(x) * tiny[row : row + 1]).astype(bf16)


def enter(mid, parts, tiny, experts):
    shapes = [array(mid.shape, f32), array(mid.shape, bf16)]
    kernel = functools.partial(enter_kernel, len(parts), experts)
    return simple(kernel, shapes, mid, *parts, tiny)


def finish_kernel(mid, *refs):
    refs[-1][...] = (mid[...] + sum_parts(refs[:-1])).astype(bf16)


def finish(mid, parts):
    return simple(finish_kernel, [array(mid.shape, bf16)], mid, *parts)[0]


def norm_back(value, gain, grad):
    inverse = inverse_rms(value)
    hat = value * inverse
    d_hat = grad * gain
    d_value = inverse * (d_hat - hat * jnp.mean(d_hat * hat, axis=-1, keepdims=True))
    return d_value, jnp.sum(grad * hat, axis=0, keepdims=True)


def unroute_kernel(count, layer, *refs):
    parts, refs = refs[:count], refs[count:]
    grad, mid, tiny, gates_in, payload, d_out, d_low, g_router, g_gain = refs
    width = mid.shape[1]
    experts = gates_in.shape[1]
    start = layer * (experts + 4)
    back = sum_parts(parts)
    gates = gates_in[...]
    gate_grad = back[:, width : width + experts]
    d_logits = gates * (gate_grad - jnp.sum(gates * gate_grad, axis=-1, keepdims=True))
    d_logits = d_logits.astype(bf16)
    d_normed = back[:, :width] + dot(d_logits, tiny[start : start + experts].astype(bf16))
    gain = tiny[start + experts + 1 : start + experts + 2]
    d_mid, gain_sum = norm_back(mid[...], gain, d_normed)
    d_mid = d_mid + grad[...].astype(f32)
    d_out[...] = d_mid
    d_low[...] = d_mid.astype(bf16)
    g_router[...] = dot_rows(d_logits, payload[:, :width])
    g_gain[...] = gain_sum


def unroute(layer, parts, grad, mid, tiny, gates, payload):
    width, experts = mid.shape[1], gates.shape[1]
    shapes = [
        array(mid.shape, f32),
        array(mid.shape, bf16),
        array((experts, width), f32),
        array((1, width), f32),
    ]
    kernel = functools.partial(unroute_kernel, len(parts), layer)
    return simple(kernel, shapes, *parts, grad, mid, tiny, gates, payload)


def leave_kernel(row, kept, got, x, d_mid, tiny, d_out):
    d_normed = kept[...] + got[...].astype(f32)
    d_x, _ = norm_back(x[...], tiny[row : row + 1], d_normed)
    d_out[...] = (d_mid[...] + d_x).astype(bf16)


def leave(layer, experts, kept, got, x, d_mid, tiny):
    kernel = functools.partial(leave_kernel, layer * (experts + 4) + experts)
    return simple(kernel, [array(x.shape, bf16)], kept, got, x, d_mid, tiny)[0]


def count_rows(tiles):
    return max(tile_rows, tiles[0][0].shape[0])


def apply_experts(tiles, weights, ones, layer):
    kept, outs, stores = [], [], None
    for number, pieces in enumerate(tiles):
        out, saved, stores = run_experts(
            pieces, weights, ones, layer, number, count_rows(tiles), stores
        )
        outs.append(out)
        kept.append(saved)
    return outs, kept, stores


def apply_experts_back(tiles, weights, ones, kept, layer):
    backs, stores = [], None
    for number, (pieces, saved) in enumerate(zip(tiles, kept)):
        back, stores = run_experts_back(
            pieces, weights, ones, saved, layer, number, count_rows(tiles), stores
        )
        backs.append(back)
    return backs, stores


def choose_kernel(zero, one, out):
    core = lax.axis_index("section")
    for number, own in enumerate((zero, one)):

        @pl.when(core == number)
        def _():
            out[: own.shape[0]] = own[...]


def small_kernel(router0, gain0, router1, gain1, own, other):
    core = lax.axis_index("section")
    layers = ((router0, gain0), (router1, gain1))
    experts = router0.shape[0]
    for number in range(2):

        @pl.when(core == number)
        def _():
            for out, layer in ((own, number), (other, 1 - number)):
                router, gain = layers[layer]
                out[...] = jnp.zeros_like(out)
                out[:experts] = router[...]
                out[experts : experts + 1] = gain[...]


def late_kernel(zero, one, own, got, out):
    rows = zero.shape[0]
    choose_kernel(zero, one, out)
    out[rows:] = (own[...] + got[...]).astype(bf16)


def other_layer_kernel(zero, one, out, sem):
    core = lax.axis_index("section")
    for number, source in enumerate((one, zero)):

        @pl.when(core == number)
        def _():
            pltpu.make_async_copy(source, out, sem).start()

    pltpu.make_async_copy(zero, out, sem).wait()


def exchange(zero, one):
    sent = pl.pallas_call(
        other_layer_kernel,
        in_specs=[anywhere] * 2,
        out_specs=anywhere,
        out_shape=array(zero.shape, zero.dtype),
        scratch_shapes=[pltpu.SemaphoreType.DMA],
        compiler_params=kernel_params(8),
        cost_estimate=cost(1000, 1000),
    )(zero, one)
    got = swap_core(sent)
    return zero, one, got, got


def by_columns(value, split):
    columns = value.shape[1] // split
    return jnp.stack([value[:, i * columns : (i + 1) * columns] for i in range(split)])


def to_owners(blocks):
    return lax.all_to_all(blocks, "expert", split_axis=0, concat_axis=0, tiled=True)


def body(
    ends_in,
    attn_gain,
    w_query,
    key_matrix,
    value_matrix,
    query_gain,
    key_gain,
    w_out,
    ffn_gain,
    router,
    w_gate,
    w_up,
    w_down,
    routes,
    lengths,
):
    core = lax.axis_index("section")
    first = core == 0
    side = lax.axis_index("tensor")
    index = lax.axis_index("expert")
    split = lax.axis_size("expert")
    rows, width = ends_in.shape[2:]
    half = rows // 2
    experts = router.shape[2]
    head = query_gain.shape[1] * split

    def pick(zero, one):
        return jnp.where(first, zero, one)

    def mine(pair):
        return pick(pair[0], pair[1])

    def theirs(pair):
        return pick(pair[1], pair[0])

    def by_layer(own):
        got = swap_core(own)
        return pick(own, got), pick(got, own)

    def pick_side(zero, one):
        return jnp.where(side == 0, zero, one)

    def half_rows(block):
        return pick_side(block[:half], block[half:])

    def side_first(block):
        return pick_side(block, cat(block[half:], block[:half]))

    part = w_query.shape[1]
    columns = w_query.shape[2] // 2
    transposed = w_out[0].T
    groups = [
        cat(
            w_query[0][:, g * columns : (g + 1) * columns],
            key_matrix[0][:, g * head : (g + 1) * head],
            value_matrix[0][:, g * head : (g + 1) * head],
            transposed[:, g * columns : (g + 1) * columns],
            axis=1,
        )
        for g in range(2)
    ]
    kept, got = mine(groups), swap_core(theirs(groups))
    breadth = kept.shape[1]

    share = head // split
    gains = cat(query_gain[0][:, None], key_gain[0][:, None], axis=1)
    tiny = cat(
        router[0],
        attn_gain[0][:, None],
        ffn_gain[0][:, None],
        jnp.pad(gains, ((0, part - share), (0, 0))),
        axis=1,
    )
    size = tiny.shape[1]
    tiny = cat(*by_layer(tiny), axis=1)
    tiny = jnp.pad(tiny, ((0, 0), (0, -2 * size % lanes)))
    ring0 = Ring(cat(pick(kept, got), tiny, axis=1))
    ring1 = Ring(pick(got, kept))
    started = ring0.advance()

    ends_in, w_gate, w_up, w_down = lax.optimization_barrier(
        (ends_in, w_gate, w_up, w_down, *started)
    )[:4]
    own_weights = (w_gate[0], w_up[0], w_down[0])
    expert_weights = own_weights + tuple(swap_core(one) for one in own_weights)
    crossed = swap_core(ends_in[0])
    x_all, grad_all = pick(ends_in[0], crossed), pick(crossed, ends_in[0])
    x_own = mine(x_all)
    x_in = half_rows(x_own).astype(f32)
    grad_last = half_rows(mine(grad_all))
    x_both = cat(side_first(x_own), side_first(theirs(x_all))).astype(f32)
    x_hat = x_both * inverse_rms(x_both)

    routes, lengths = lax.optimization_barrier((routes, lengths, *ring0.advance()))[:2]
    routes_crossed = swap_core(pick(routes[0, 1], routes[0, 0]))
    routes_own = [pick(routes[0, 0], routes_crossed), pick(routes_crossed, routes[0, 1])]
    expert_ids = jnp.arange(experts, dtype=jnp.int32)
    masks = [
        jnp.any(half_rows(r)[:, :, None] == expert_ids[None, None, :], axis=1).astype(f32)
        for r in routes_own
    ]
    per_device = w_gate.shape[1]
    lane_ids = jnp.arange(lanes, dtype=jnp.int32)
    local_ids = index * per_device + jnp.arange(per_device, dtype=jnp.int32)
    ones = (lane_ids[None, :] == local_ids[:, None]).astype(f32)
    row_index = (jnp.arange(rows, dtype=jnp.int32) + side * half) % rows
    length_pair = [pick(lengths[0, 0], lengths[1, 0]), pick(lengths[1, 0], lengths[0, 0])]
    tables = make_tables(length_pair, row_index, head)

    ring0.advance()
    ring0.advance()
    ring1.advance(*ring0.latest)

    tiny, normed0, mixed0, raw0, probs0, own, other = attend(
        0, ring0, breadth, split, experts, (x_hat,), tables
    )
    other = after(other, *ring1.latest)
    mid0, payload0, gates0 = route(0, x_in, *own_rows(own, other), tiny, masks[0])
    gather = Gather(payload0)
    gather.along_z()
    weights0 = choose_weights(0, (after(expert_weights[0], payload0), *expert_weights[1:]))
    gather.near()
    gather.far(*weights0)
    tiles = gather.tiles()
    ring1.advance(tiles[-1][-1])
    outs0, kept0, stores0 = apply_experts(tiles, weights0, ones, 0)
    scatter = Scatter(outs0)
    scatter.far()
    scatter.near(beside=ring1.latest)
    parts = scatter.along_z()
    ring1.advance(*parts)
    ring1.advance()
    x_mid, shard = enter(mid0, parts, tiny, experts)

    normed_pieces = both_rows(shard)
    grad_gather = Gather(grad_last)
    along = grad_gather.along_z(normed_pieces[-1])
    normed1, mixed1, raw1, probs1, own, other = attend(
        1, ring1, breadth, split, experts, (*normed_pieces, tiny), tables
    )
    other = after(other, *along)
    mid1, payload1, gates1 = route(1, x_mid, *own_rows(own, other), tiny, masks[1])
    beside = grad_gather.near(payload1)
    gather = Gather(payload1)
    gather.along_z()
    weights1 = choose_weights(1, (after(expert_weights[0], payload1), *expert_weights[1:]))
    gather.near(*weights1, *beside)
    gather.far()
    tiles = gather.tiles()
    beside = grad_gather.far(tiles[-1][-1])
    mixed_got = swap_core(pick(mixed1, mixed0))
    ring_mixed = Ring(stack_layer(mixed0, mixed1, mixed_got))
    ring_mixed.advance(tiles[-1][-1])
    outs1, kept1, stores1 = apply_experts(tiles, weights1, ones, 1)

    outs1[-1][-1] = after(outs1[-1][-1], *ring_mixed.latest, *beside)
    tiles = grad_gather.tiles(outs1[-1][-1])
    ring_mixed.advance(tiles[-1][-1])
    backs, back_stores1 = apply_experts_back(tiles, weights1, ones, kept1, 1)
    scatter = Scatter(backs)
    scatter.far(*ring_mixed.latest)
    reached = scatter.near()
    out_scatter = Scatter(outs1)
    beside = out_scatter.far(*reached)
    parts = scatter.along_z()
    parts[-1] = after(parts[-1], *beside)
    d_mid, d_low, g_router1, g_ffn_gain1 = unroute(
        1, parts, grad_last, mid1, tiny, gates1, payload1
    )
    d_pieces = both_rows(d_low)
    ring_mixed.advance(d_pieces[-1])

    if small_grid():
        rows_in = exchange(after(stores0[0], d_pieces[-1]), stores1[0])
        early = (rows_in[2],)
    else:
        early = ()
    d_attn1, d_qkv1, d_own, d_other = attend_back(
        1, ring1, breadth, split, experts, d_pieces, raw1, probs1, tiny, tables
    )
    d_other = after(d_other, *ring_mixed.latest, *early)
    ring_mixed.advance(d_qkv1)
    d_one = leave(1, experts, *own_rows(d_own, d_other), x_mid, d_mid, tiny)

    d_one = after(d_one, *ring_mixed.latest)
    gather = Gather(d_one)
    gather.along_z()
    beside = out_scatter.near(d_one)
    weights0 = choose_weights(0, (after(expert_weights[0], d_one), *expert_weights[1:]))
    gather.near(*beside)
    gather.far(*weights0)
    tiles = gather.tiles()
    backs, back_stores0 = apply_experts_back(tiles, weights0, ones, kept0, 0)

    if not small_grid():
        rows_in = exchange(after(stores0[0], back_stores0[0]), stores1[0])
    d_act = exchange(after(back_stores0[0], rows_in[2]), back_stores1[0])
    wide = wide_grads(per_device, rows_in, d_act)
    scatter = Scatter(backs)
    normed_own = simple(
        choose_kernel, [array(normed0.shape, bf16)], normed0, after(normed1, *scatter.far())
    )[0]
    normed_blocks = by_columns(normed_own, split)
    scatter.near(beside=(*wide[0], normed_blocks))
    parts = scatter.along_z()
    parts[-1] = after(parts[-1], *wide[1])
    d_mid, d_low, g_router0, g_ffn_gain0 = unroute(
        0, parts, d_one, mid0, tiny, gates0, payload0
    )
    d_pieces = both_rows(d_low)
    normed_spread = to_owners(after(normed_blocks, d_pieces[-1]))
    out_parts = out_scatter.along_z(d_pieces[-1])
    d_attn0, d_qkv0, d_own, d_other = attend_back(
        0, ring0, breadth, split, experts, d_pieces, raw0, probs0, tiny, tables
    )

    qkv_got = swap_core(pick(d_qkv1, after(d_qkv0, normed_spread, *out_parts)))
    ring_d = Ring(stack_layer(d_qkv0, d_qkv1, qkv_got, 2 * head))
    one_round = ring_d.advance()
    d_other = after(d_other, ring_d.shard)
    d_zero = leave(0, experts, *own_rows(d_own, d_other), x_in, d_mid, tiny)
    scaled = exchange(after(stores0[1], ring_d.shard), stores1[1])
    gate = ring_d.shard if small_grid() else scaled[2]
    late = (scaled, exchange(after(back_stores0[1], gate), back_stores1[1]))
    down = down_grads(per_device, *late)
    ring_d.advance()
    rows_small = -(-(experts + 1) // 16) * 16
    small_own, small_other = simple(
        small_kernel,
        [array((rows_small, width), f32)] * 2,
        after(g_router0, *one_round),
        g_ffn_gain0,
        g_router1,
        g_ffn_gain1,
    )
    late_rows = simple(
        late_kernel,
        [array((2 * rows + rows_small, width), bf16)],
        d_attn0,
        d_attn1,
        small_own,
        swap_core(small_other),
    )[0]
    late_spread = to_owners(by_columns(late_rows, split))
    three_rounds = ring_d.advance(*down[0])
    ring_d.advance(*down[1])
    g_out = out_grads(ring_mixed, late_spread)
    out1 = finish(mid1, out_parts)
    end_own = pick(d_zero, out1)
    end_got = swap_core(pick(out1, d_zero))
    projections = (w_query[0], key_matrix[0], value_matrix[0])
    g_query, g_key, g_value, late = projection_grads(
        ring_d, normed_spread, after(late_spread, *ring_mixed.latest), projections, head
    )
    (g_gate, g_up), (g_down,) = wide[-1], down[-1]

    small = late + swap_x(late)
    g_attn_gain = small[0, :part] / attn_gain[0].astype(f32)
    g_query_gain = lax.dynamic_slice(small[1], (index * share,), (share,))
    g_key_gain = lax.dynamic_slice(small[1], (head + index * share,), (share,))
    g_router = small[8 : 8 + experts, :part].T
    g_ffn_gain = small[8 + experts, :part]

    ends = jnp.stack([pick(end_own, end_got), pick(end_got, end_own)])
    ends_far = swap_x(ends)
    ends_out = cat(pick_side(ends, ends_far), pick_side(ends_far, ends), axis=1)

    outs = (
        ends_out,
        g_attn_gain,
        g_query,
        g_key,
        g_value,
        g_query_gain,
        g_key_gain,
        g_out,
        g_ffn_gain,
        g_router,
        g_gate,
        g_up,
        g_down,
    )
    return tuple(one[None] for one in outs)


def solution(mesh):
    return jax.shard_map(
        body,
        mesh=mesh,
        in_specs=(
            P("section", None, "expert", None),
            P("section", "expert"),
            P("section", "expert", "tensor"),
            P("section", "expert", "tensor"),
            P("section", "expert", "tensor"),
            P("section", "expert"),
            P("section", "expert"),
            P("section", "tensor", "expert"),
            P("section", "expert"),
            P("section", "expert", None),
            P("section", "expert", None, "tensor"),
            P("section", "expert", None, "tensor"),
            P("section", "expert", "tensor", None),
            P("section", None, "expert", None),
            P(None, "expert", None),
        ),
        out_specs=(
            P("section", None, "expert", None),
            P("section", "expert"),
            P("section", "expert", "tensor"),
            P("section", "expert", "tensor"),
            P("section", "expert", "tensor"),
            P("section", "expert"),
            P("section", "expert"),
            P("section", "tensor", "expert"),
            P("section", "expert"),
            P("section", "expert", None),
            P("section", "expert", None, "tensor"),
            P("section", "expert", None, "tensor"),
            P("section", "expert", "tensor", None),
        ),
        check_vma=False,
    )
```
